32 devices in a mesh: rep: 16 (over z, y, x), mp: 2 (over core).
Axes of the slice: x: 2, y: 2, z: 4, core: 2. Of those that a mesh axis runs over, the one named last changes fastest.
Arguments:
- tokens_in: bfloat16 [4096, 8192], P('rep', 'mp'), may hold values from -2100 to 2100
- norm_gain: bfloat16 [8192], P('mp'), may hold values from 0.5 to 1.5
- key_grad: bfloat16 [4096, 512], P('rep'), may hold values from -1 to 1
- error_in: float32 [16, 8192, 512], P('rep', 'mp'), may hold values from -6 to 6
- basis_init: float32 [512, 128], P('mp'), may hold values from -6 to 6
- weights_in: float32 [2, 4096, 512], P('mp', 'rep'), may hold values from -0.75 to 0.75
- momentum_in: float32 [2, 4096, 512], P('mp', 'rep'), may hold values from -1.5 to 1.5
Outputs:
- error_out: float32 [16, 8192, 512], P('rep', 'mp')
- weights_out: float32 [2, 4096, 512], P('mp', 'rep')
- momentum_out: float32 [2, 4096, 512], P('mp', 'rep')
The draws below stay inside these ranges and needn't reach their ends.
All inputs are finite; a program needn't handle non-finite values.
Results may differ from the reference program's by a relative error of at most 0.0025.
Values sent between devices are 32-bit elements; how exact they have to be, the bound alone decides.
No kernel may reach another device: no remote copies, remote signals or barrier semaphores. Data moves between devices by JAX's collectives and lax.ppermute only.
A program may use at most 64 MiB of HBM per device.

```python
import math
import jax
import jax.numpy as jnp
from jax import lax

D = 8192
RANK = 128
ITERS = 2
TOK = 256
KW = 512
DL = 4096
ALLTOK = 4096
N_REP = 16
N_MP = 2


def draw_tokens_in(key, part):
    first, second, third = jax.random.split(key, 3)
    row_scales = jnp.exp(jax.random.uniform(first, (ALLTOK, 1), jnp.float32) * math.log(10.0))
    column_scales = jnp.exp(jax.random.uniform(second, (1, D), jnp.float32) * math.log(10.0))
    rising = jnp.exp(jnp.arange(D, dtype=jnp.float32)[None, :] / D * math.log(3.0))
    values = jnp.clip(jax.random.normal(third, (ALLTOK, D), jnp.float32), -6.0, 6.0)
    return (values * row_scales * column_scales * rising).astype(jnp.bfloat16)


def shard_levels(key, dims, cuts, low, top_value):
    factor_of, own = 1.0, jax.random.fold_in(key, 6)
    for dim, blocks in cuts:
        draws = jnp.exp(jax.random.uniform(jax.random.fold_in(own, dim), (blocks,), jnp.float32, low / len(cuts), top_value / len(cuts)))
        factor_of = factor_of * jnp.repeat(draws, dims[dim] // blocks).reshape([-1 if axis == dim else 1 for axis in range(len(dims))])
    return factor_of


def centred(own_key, extent, deviation, bound, shards=(), held_as=jnp.bfloat16):
    result = deviation * jax.random.normal(own_key, extent, jnp.float32)
    if shards:
        result = result * shard_levels(own_key, extent, shards, -0.22, 0.18)
    return jnp.clip(result, -bound, bound).astype(held_as)


def setup_inputs(seed: int = 0) -> dict:
    keys = jax.random.split(jax.random.key(seed), 8)
    tokens_in = draw_tokens_in(jax.random.fold_in(keys[7], 71), 0)
    norm_gain = jnp.clip(1.0 + 0.1 * jax.random.normal(keys[1], (D,), jnp.float32), 0.5, 1.5).astype(jnp.bfloat16)
    key_grad = centred(keys[2], (ALLTOK, KW), (TOK ** -0.5), 1.0, ((0, 16),))
    error_in = centred(keys[3], (N_REP, D, KW), 1.0, 6.0, ((0, 16), (1, 2)), jnp.float32)
    basis_init = centred(keys[4], (KW, RANK), 1.0, 6.0, ((0, 2),), jnp.float32)
    weights_in = centred(keys[5], (N_MP, DL, KW), 0.05, 0.75, ((0, 2), (1, 16)), jnp.float32)
    momentum_in = centred(keys[6], (N_MP, DL, KW), 0.1, 1.5, ((0, 2), (1, 16)), jnp.float32)
    return {"tokens_in": tokens_in, "norm_gain": norm_gain, "key_grad": key_grad, "error_in": error_in, "basis_init": basis_init, "weights_in": weights_in, "momentum_in": momentum_in}


precise = lax.Precision.HIGHEST
epsilon = 1e-05
momentum_rate = 0.9
outer_rate = 0.7

def right_solve(lower_factor, row_block):
    return jax.scipy.linalg.solve_triangular(lower_factor, row_block.T, lower=True).T

def reference(tokens_in, norm_gain, key_grad, error_in, basis_init, weights_in, momentum_in):
    widened = tokens_in.astype(jnp.float32)
    mean_square = lax.optimization_barrier(jnp.mean(widened * widened, axis=1, keepdims=True))
    normed = (widened * lax.rsqrt(mean_square + epsilon) * norm_gain.astype(jnp.float32)[None, :]).astype(jnp.bfloat16)
    normed_wide = normed.astype(jnp.float32).reshape(N_REP, TOK, D)
    cotangents = key_grad.astype(jnp.float32).reshape(N_REP, TOK, KW)
    weight_change = jnp.einsum('rtd,rtk->rdk', normed_wide, cotangents, precision=precise)
    merged = weight_change + error_in
    right_factor = basis_init
    orthonormal = jnp.zeros((D, RANK), jnp.float32)
    for iteration in range(ITERS):
        left_factor = jnp.einsum('rdk,kq->dq', merged, right_factor, precision=precise) / N_REP
        gram_matrix = jnp.dot(left_factor.T, left_factor, precision=precise)
        lower_factor = jnp.linalg.cholesky(gram_matrix)
        orthonormal = right_solve(lower_factor, left_factor)
        right_factor = jnp.einsum('rdk,dq->kq', merged, orthonormal, precision=precise) / N_REP
    approximant = jnp.dot(orthonormal, right_factor.T, precision=precise)
    error_out = merged - approximant[None]
    approx_rows = approximant.reshape(N_MP, D // N_MP, KW)
    momentum_out = momentum_rate * momentum_in + approx_rows
    weights_out = weights_in - outer_rate * (approx_rows + momentum_rate * momentum_out)
    return (error_out, weights_out, momentum_out)
```

```python
import functools

import jax
import jax.numpy as jnp
from jax import lax
from jax.experimental import pallas as pl
from jax.experimental.pallas import tpu as pltpu
from jax.sharding import PartitionSpec as P

BLOCK = 128

precise = lax.Precision.HIGHEST
epsilon = 1e-05
momentum_rate = 0.9
outer_rate = 0.7


def contract(first, second, dims, precision=precise):
    return lax.dot_general(
        first,
        second,
        ((dims[:1], dims[1:]), ((), ())),
        precision=precision,
        preferred_element_type=jnp.float32,
    )


def flip(value, axis, mask):
    size = lax.axis_size(axis)
    return lax.ppermute(value, axis, [(i, i ^ mask) for i in range(size)])


def bit_of(axis, bit):
    return (lax.axis_index(axis) >> bit) & 1


def rows_of(value, start, count):
    return lax.dynamic_slice_in_dim(value, start, count, 0)


def halve(value, axis, bit):
    half = value.shape[0] // 2
    side = bit_of(axis, bit)
    sent = rows_of(value, (1 - side) * half, half)
    return rows_of(value, side * half, half) + flip(sent, axis, 1 << bit)


def double(value, axis, bit):
    other = flip(value, axis, 1 << bit)
    side = bit_of(axis, bit)
    both = jnp.concatenate([value, value], 0)
    return lax.dynamic_update_slice_in_dim(both, other, (1 - side) * value.shape[0], 0)


def bit_count(size):
    return size.bit_length() - 1


def sum_over(value, axis):
    for bit in range(bit_count(lax.axis_size(axis))):
        value = value + flip(value, axis, 1 << bit)
    return value


def sum_everywhere(value):
    rep_bits = bit_count(lax.axis_size("rep"))
    mp_bits = bit_count(lax.axis_size("mp"))
    for bit in range(mp_bits):
        value = halve(value, "mp", bit)
    place = lax.axis_index("rep") & 3
    part = value.shape[0] // 4
    pieces = [rows_of(value, (place ^ m) * part, part) for m in range(4)]
    got = [flip(pieces[m], "rep", m) for m in (1, 2, 3)]
    value = (pieces[0] + got[0]) + (got[1] + got[2])
    bit = 2
    while bit < rep_bits:
        if bit + 1 < rep_bits:
            got = [flip(value, "rep", m << bit) for m in (1, 2, 3)]
            value = (value + got[0]) + (got[1] + got[2])
            bit += 2
        else:
            value = value + flip(value, "rep", 1 << bit)
            bit += 1
    got = [value] + [flip(value, "rep", m) for m in (1, 2, 3)]
    whole = jnp.zeros((4 * part,) + value.shape[1:], value.dtype)
    for m in range(4):
        whole = lax.dynamic_update_slice_in_dim(whole, got[m], (place ^ m) * part, 0)
    for bit in reversed(range(mp_bits)):
        whole = double(whole, "mp", bit)
    return whole


LIGHT = pl.CostEstimate(flops=1, bytes_accessed=1, transcendentals=0)


def kernel_call(*args, **options):
    return pl.pallas_call(
        *args, compiler_params=pltpu.CompilerParams(vmem_limit_bytes=16 * 2**20), **options
    )


def near(*arrays):
    return [pltpu.with_memory_space_constraint(array, pltpu.VMEM) for array in arrays]


def distant(array):
    return pltpu.with_memory_space_constraint(array, pltpu.HBM)


def near_shape(shape, dtype=jnp.float32):
    return pltpu.VMEM(shape, dtype)


def specs(*places):
    return [pl.BlockSpec(memory_space=place) for place in places]


def pieces_of(count, most):
    cuts, place = [], 0
    while place < count:
        size = min(most, count - place)
        cuts.append((place, size))
        place += size
    return cuts


def split(value):
    high = value.astype(jnp.bfloat16)
    return high, (value - high.astype(jnp.float32)).astype(jnp.bfloat16)


def squares_kernel(cuts, tokens_ref, out_ref, held_ref, sems):
    copies = []
    for index, (start, size) in enumerate(cuts):
        at = pl.ds(start, size)
        copies.append(
            pltpu.make_async_copy(tokens_ref.at[:, at], held_ref.at[:, at], sems.at[index])
        )
        copies[-1].start()
    total = None
    for copy, (start, size) in zip(copies, cuts):
        copy.wait()
        for place in range(start, start + size, BLOCK):
            wide = held_ref[:, place : place + BLOCK].astype(jnp.float32)
            total = wide * wide if total is None else total + wide * wide
    out_ref[...] = jnp.broadcast_to(jnp.sum(total, axis=1, keepdims=True), out_ref.shape)


def squares(tokens):
    cuts = pieces_of(tokens.shape[1], max(BLOCK, tokens.shape[1] // 4))
    return kernel_call(
        functools.partial(squares_kernel, cuts),
        out_shape=near_shape((tokens.shape[0], BLOCK)),
        in_specs=specs(pltpu.HBM),
        out_specs=specs(pltpu.VMEM)[0],
        scratch_shapes=[
            pltpu.VMEM(tokens.shape, tokens.dtype),
            pltpu.SemaphoreType.DMA((len(cuts),)),
        ],
    )(distant(tokens))


def merge_kernel(
    cuts, depth, start_ref, tokens_ref, squares_ref, gain_ref, grad_ref, error_ref, out_ref, held_ref, sems
):
    copies = []
    for index, (place, size) in enumerate(cuts):
        there = pl.ds(pl.multiple_of(start_ref[0] + place, BLOCK), size)
        here = pl.ds(place, size)
        pair = [
            pltpu.make_async_copy(tokens_ref.at[:, there], held_ref.at[:, here], sems.at[index, 0]),
            pltpu.make_async_copy(error_ref.at[there, :], out_ref.at[here, :], sems.at[index, 1]),
        ]
        for copy in pair:
            copy.start()
        copies.append(pair)
    scale = lax.rsqrt(squares_ref[...] / depth + epsilon)[:, :1]
    for pair, (place, size) in zip(copies, cuts):
        here = pl.ds(place, size)
        there = pl.ds(pl.multiple_of(start_ref[0] + place, BLOCK), size)
        gain = gain_ref[:, there].astype(jnp.float32)
        pair[0].wait()
        normed = (held_ref[:, here].astype(jnp.float32) * scale * gain).astype(jnp.bfloat16)
        change = lax.dot_general(
            normed, grad_ref[...], (((0,), (0,)), ((), ())), preferred_element_type=jnp.float32
        )
        pair[1].wait()
        out_ref[here, :] = change + out_ref[here, :]


def merge(start, count, depth, tokens, square_sums, gain, grad, error):
    cuts = pieces_of(count, 3 * BLOCK)
    return kernel_call(
        functools.partial(merge_kernel, cuts, depth),
        out_shape=near_shape((count, grad.shape[1])),
        in_specs=specs(pltpu.SMEM, pltpu.HBM, pltpu.VMEM, pltpu.VMEM, pltpu.VMEM, pltpu.HBM),
        out_specs=specs(pltpu.VMEM)[0],
        scratch_shapes=[
            pltpu.VMEM((tokens.shape[0], count), tokens.dtype),
            pltpu.SemaphoreType.DMA((len(cuts), 2)),
        ],
        cost_estimate=pl.CostEstimate(
            flops=2 * count * grad.shape[1] * tokens.shape[0],
            bytes_accessed=8 * count * grad.shape[1] + 2 * tokens.shape[0] * count,
            transcendentals=0,
        ),
    )(
        jnp.reshape(start, (1,)).astype(jnp.int32),
        distant(tokens),
        *near(square_sums, gain, grad),
        distant(error),
    )


def sides_of(side, half):
    return pl.ds(pl.multiple_of(side * half, 8), half), pl.ds(pl.multiple_of((1 - side) * half, 8), half)


def join_kernel(count, side_ref, own_ref, got_ref, *refs):
    keep_ref, send_ref = refs[-2:]
    stays, goes = sides_of(side_ref[0], count // 2)
    send_ref[...] = own_ref[goes, :] + got_ref[goes, :]
    keep_ref[...] = own_ref[stays, :] + got_ref[stays, :]


def last_kernel(own_ref, got_ref, *refs):
    refs[-1][...] = own_ref[...] + got_ref[...]


def join(own, got, side, after):
    count, width = own.shape
    arrays, places = near(own, got), [pltpu.VMEM] * 2
    if side is None:
        kernel, shapes = last_kernel, (near_shape((count, width)),)
    else:
        kernel = functools.partial(join_kernel, count)
        shapes = (near_shape((count // 2, width)),) * 2
        arrays.insert(0, jnp.reshape(side, (1,)).astype(jnp.int32))
        places.insert(0, pltpu.SMEM)
    return kernel_call(
        kernel,
        out_shape=shapes,
        in_specs=specs(*places, *[pl.ANY] * len(after)),
        out_specs=tuple(specs(*[pltpu.VMEM] * len(shapes))),
        cost_estimate=LIGHT,
    )(*arrays, *after)


def stack_kernel(count, side_ref, own_ref, got_ref, out_ref):
    stays, goes = sides_of(side_ref[0], count)
    out_ref[stays, :] = own_ref[...]
    out_ref[goes, :] = got_ref[...]


def stack(own, got, side):
    count, width = own.shape
    return kernel_call(
        functools.partial(stack_kernel, count),
        out_shape=near_shape((2 * count, width)),
        in_specs=specs(pltpu.SMEM, pltpu.VMEM, pltpu.VMEM),
        out_specs=specs(pltpu.VMEM)[0],
        cost_estimate=LIGHT,
    )(jnp.reshape(side, (1,)).astype(jnp.int32), *near(own, got))


def gram_kernel(replicas, *refs):
    out_ref = refs[-1]
    rows = jnp.concatenate([ref[...] for ref in refs[:-1]], 0) / replicas
    blocks = rows.shape[1] // BLOCK
    place = 0
    for a in range(blocks):
        left = rows[:, a * BLOCK : (a + 1) * BLOCK]
        band = contract(left, rows[:, a * BLOCK :], (0, 0))
        for b in range(blocks - a):
            out_ref[place * BLOCK : (place + 1) * BLOCK, :] = band[:, b * BLOCK : (b + 1) * BLOCK]
            place += 1


def gram(parts, replicas):
    blocks = parts[0].shape[1] // BLOCK
    return kernel_call(
        functools.partial(gram_kernel, replicas),
        out_shape=near_shape((blocks * (blocks + 1) // 2 * BLOCK, BLOCK)),
        in_specs=specs(*[pltpu.VMEM] * len(parts)),
        out_specs=specs(pltpu.VMEM)[0],
    )(*near(*parts))


def factor(matrix):
    size = matrix.shape[0]
    group = 8
    lane = lax.broadcasted_iota(jnp.int32, (size, size), 1)
    row = lax.broadcasted_iota(jnp.int32, (size, size), 0)
    done = []
    live = matrix
    for start in range(0, size, group):
        if start:
            done.append(live[:group])
            live = live[group:]
        count = size - start
        lanes, rows = lane[start:], row[start:]
        columns = [
            jnp.broadcast_to(live[:, start + t : start + t + 1], (count, size)) for t in range(group)
        ]
        for t in range(group):
            pivot = start + t
            inverse = 1.0 / columns[t][t : t + 1, :]
            below = rows > pivot
            scale = jnp.where(below, columns[t] * inverse, 0.0)
            own = jnp.where(lanes[t : t + 1] == pivot, 1.0, live[t : t + 1, :])
            live = jnp.where(below & (lanes == pivot), 0.0, live) - scale * own
            for s in range(t + 1, group):
                columns[s] = columns[s] - scale * columns[s][t : t + 1, :]
    done.append(live)
    result = jnp.concatenate(done, 0)
    diagonal = jnp.sum(jnp.where(lane == row, result, 0.0), axis=1, keepdims=True)
    unit = jnp.where(lane < row, result, jnp.where(lane == row, 1.0, 0.0))
    return unit, diagonal


def first_kernel(replicas, packed_ref, basis_ref, *refs):
    whole_ref, right_ref, left_ref = refs[-3:]
    blocks = basis_ref.shape[0] // BLOCK
    place = 0
    for a in range(blocks):
        for b in range(a, blocks):
            tile = packed_ref[place * BLOCK : (place + 1) * BLOCK, :]
            whole_ref[a * BLOCK : (a + 1) * BLOCK, b * BLOCK : (b + 1) * BLOCK] = tile
            if b > a:
                whole_ref[b * BLOCK : (b + 1) * BLOCK, a * BLOCK : (a + 1) * BLOCK] = tile.T
            place += 1
    basis = basis_ref[...]
    plain = contract(whole_ref[...], basis, (1, 0))
    unit, diagonal = factor(contract(basis, plain, (0, 0)))
    right = contract(plain, unit * lax.rsqrt(diagonal), (1, 1))
    right_ref[...] = right
    rows = jnp.concatenate([ref[...] for ref in refs[:-3]], 0) / replicas
    left_ref[...] = contract(rows, right, (1, 0))


def first_pass(packed, basis, parts, replicas):
    width, rank = basis.shape
    return kernel_call(
        functools.partial(first_kernel, replicas),
        out_shape=(
            near_shape((width, width)),
            near_shape((width, rank)),
            near_shape((sum(part.shape[0] for part in parts), rank)),
        ),
        in_specs=specs(*[pltpu.VMEM] * (2 + len(parts))),
        out_specs=tuple(specs(*[pltpu.VMEM] * 3)),
    )(*near(packed, basis, *parts))


def product_kernel(whole_ref, right_ref, plain_ref, gram_ref):
    right = right_ref[...]
    plain = contract(whole_ref[...], right, (1, 0))
    plain_ref[...] = plain
    gram_ref[...] = contract(right, plain, (0, 0))


def weight_kernel(plain_ref, gram_ref, high_ref, low_ref):
    unit, diagonal = factor(gram_ref[...])
    inverse = unit * lax.rsqrt(diagonal)
    turned = contract(inverse, plain_ref[...], (1, 1))
    high_ref[...], low_ref[...] = split(contract(inverse, turned, (0, 0)))


def second_pass(whole, right):
    width, rank = right.shape
    pair = functools.partial(
        kernel_call,
        in_specs=specs(pltpu.VMEM, pltpu.VMEM),
        out_specs=tuple(specs(pltpu.VMEM, pltpu.VMEM)),
    )
    plain, gram_matrix = pair(
        product_kernel, out_shape=(near_shape((width, rank)), near_shape((rank, rank)))
    )(*near(whole, right))
    half = near_shape((rank, width), jnp.bfloat16)
    return pair(weight_kernel, out_shape=(half, half))(*near(plain, gram_matrix))


def low_rank(left, high, low):
    left_high, left_low = split(left)
    dot = functools.partial(jnp.dot, preferred_element_type=jnp.float32)
    return dot(left_high, high) + (dot(left_high, low) + dot(left_low, high))


def error_pieces(counts):
    pieces, base = [], 0
    for index, count in enumerate(counts):
        pieces += [(index, place, base + place, size) for place, size in pieces_of(count, 3 * BLOCK)]
        base += count
    return pieces


def fetch_merged(counts, refs, held_ref, sems):
    copies = []
    for number, (index, place, spot, size) in enumerate(error_pieces(counts)):
        copies.append(
            pltpu.make_async_copy(
                refs[index].at[pl.ds(place, size), :], held_ref.at[pl.ds(spot, size), :], sems.at[0, number]
            )
        )
        copies[-1].start()
    return copies


def write_errors(counts, fetched, starts_ref, high, low, lefts, out_ref, held_ref, sems):
    copies = []
    for number, (index, place, spot, size) in enumerate(error_pieces(counts)):
        there = pl.ds(pl.multiple_of(starts_ref[index] + place, BLOCK), size)
        here = pl.ds(spot, size)
        change = low_rank(lefts[index][pl.ds(place, size), :], high, low)
        fetched[number].wait()
        held_ref[here, :] = held_ref[here, :] - change
        copies.append(
            pltpu.make_async_copy(held_ref.at[here, :], out_ref.at[there, :], sems.at[1, number])
        )
        copies[-1].start()
    for copy in copies:
        copy.wait()


def error_kernel(counts, starts_ref, high_ref, low_ref, *refs):
    n = len(counts)
    out_ref, held_ref, sems = refs[-3:]
    fetched = fetch_merged(counts, refs[:n], held_ref, sems)
    high, low = high_ref[...], low_ref[...]
    write_errors(counts, fetched, starts_ref, high, low, refs[n : 2 * n], out_ref, held_ref, sems)


def last_error_kernel(counts, all_counts, starts_ref, high_ref, low_ref, *refs):
    n, total = len(counts), len(all_counts)
    lefts = refs[n : n + total]
    weights_ref, momentum_ref = refs[n + total : n + total + 2]
    out_ref, weights_out, momentum_out, held_ref, left_ref, sems = refs[-6:]
    fetched = fetch_merged(counts, refs[:n], held_ref, sems)
    high, low = high_ref[...], low_ref[...]
    rows = left_ref.shape[0]
    size = min(BLOCK, rows)
    for place in range(0, rows, size):
        want = starts_ref[len(all_counts)] + place
        for index, count in enumerate(all_counts):
            skip = want - starts_ref[index]

            @pl.when((skip >= 0) & (skip < count))
            def _(index=index, skip=skip, place=place):
                left_ref[place : place + size, :] = lefts[index][pl.ds(pl.multiple_of(skip, 8), size), :]

    own_rows = low_rank(left_ref[...], high, low)
    momentum = momentum_rate * momentum_ref[...] + own_rows
    momentum_out[...] = momentum
    weights_out[...] = weights_ref[...] - outer_rate * (own_rows + momentum_rate * momentum)
    write_errors(counts, fetched, starts_ref, high, low, lefts, out_ref, held_ref, sems)


def error_scratch(counts, width):
    cuts = len(error_pieces(counts))
    return pltpu.VMEM((sum(counts), width), jnp.float32), pltpu.SemaphoreType.DMA((2, cuts))


def error_cost(counts, width, rank):
    return pl.CostEstimate(
        flops=6 * sum(counts) * width * rank, bytes_accessed=8 * sum(counts) * width, transcendentals=0
    )


def error_rows(starts, merged, lefts, high, low, shape):
    counts = [left.shape[0] for left in lefts]
    n = len(counts)
    return kernel_call(
        functools.partial(error_kernel, counts),
        out_shape=jax.ShapeDtypeStruct(shape, jnp.float32),
        in_specs=specs(pltpu.SMEM, pltpu.VMEM, pltpu.VMEM, *[pltpu.HBM] * n, *[pltpu.VMEM] * n),
        out_specs=specs(pltpu.HBM)[0],
        scratch_shapes=error_scratch(counts, shape[1]),
        cost_estimate=error_cost(counts, shape[1], high.shape[0]),
    )(jnp.stack(starts).astype(jnp.int32), *near(high, low), *map(distant, merged), *near(*lefts))


def last_rows(kept, starts, merged, lefts, other_starts, other_lefts, high, low, weights, momentum):
    rows, width = weights.shape
    counts = [left.shape[0] for left in lefts]
    all_counts = counts + [left.shape[0] for left in other_lefts]
    own = lax.axis_index("rep") * rows
    arrays = [
        jnp.stack([*starts, *other_starts, own]).astype(jnp.int32),
        *near(high, low),
        *map(distant, merged),
        *near(*lefts, *other_lefts),
        weights,
        momentum,
        kept,
    ]
    result = jax.ShapeDtypeStruct(weights.shape, jnp.float32)
    held, sems = error_scratch(counts, width)
    return kernel_call(
        functools.partial(last_error_kernel, counts, all_counts),
        out_shape=(jax.ShapeDtypeStruct(kept.shape, jnp.float32), result, result),
        in_specs=specs(
            pltpu.SMEM,
            pltpu.VMEM,
            pltpu.VMEM,
            *[pltpu.HBM] * len(counts),
            *[pltpu.VMEM] * (len(all_counts) + 2),
            pltpu.HBM,
        ),
        out_specs=tuple(specs(pltpu.HBM, pltpu.VMEM, pltpu.VMEM)),
        scratch_shapes=[held, pltpu.VMEM((rows, high.shape[0]), jnp.float32), sems],
        input_output_aliases={len(arrays) - 1: 0},
        cost_estimate=error_cost(counts, width, high.shape[0]),
    )(*arrays)


def stream_plan(replicas, rows_each):
    bits = bit_count(replicas)
    grain = max(8, 2 * BLOCK // replicas)
    units = rows_each // grain
    streams = max(1, min(3, units, bits - 1))
    widths = [units // streams + (1 if streams - 1 - s < units % streams else 0) for s in range(streams)]
    lead = list(range(min(3, bits)))
    rest = list(range(len(lead), bits))
    return [
        (w * grain, lead[s % len(lead) :] + lead[: s % len(lead)] + rest) for s, w in enumerate(widths)
    ]


def on_device(tokens_in, norm_gain, key_grad, error_in, basis_init, weights_in, momentum_in):
    replicas = lax.axis_size("rep")
    steps = bit_count(replicas)
    depth = tokens_in.shape[1]
    error = error_in[0]
    square_sums = sum_over(squares(tokens_in), "mp")
    basis = lax.all_gather(basis_init, "mp", axis=0, tiled=True)
    sources = (
        depth * lax.axis_size("mp"), tokens_in, square_sums, norm_gain[None, :], key_grad, error
    )

    plan = stream_plan(replicas, depth // replicas)
    halves, places, place = [], [], 0
    for width, order in plan:
        half = width * replicas // 2
        side = bit_of("rep", order[0])
        halves.append(half)
        places.append((place + side * half, place + (1 - side) * half))
        place += 2 * half
    streams = range(len(plan))
    order = [order for _, order in plan]
    far, got = [None] * len(plan), [None] * len(plan)
    turns = [len(plan) - 1, *range(len(plan) - 1)]
    for s in turns:
        far[s] = merge(places[s][1], halves[s], *sources)
        got[s] = flip(far[s], "rep", 1 << order[s][0])
    own = [merge(places[s][0], halves[s], *sources) for s in streams]
    parts, after = list(own), [*own, basis]
    for step in range(steps):
        for s in streams:
            if step + 1 < steps:
                side = bit_of("rep", order[s][step + 1])
                parts[s], send = join(parts[s], got[s], side, after)
                got[s] = flip(send, "rep", 1 << order[s][step + 1])
            else:
                (parts[s],) = join(parts[s], got[s], None, after)
            after = [parts[s]]

    packed = sum_everywhere(gram(parts, replicas))
    whole, right, left = first_pass(packed, basis, parts, replicas)
    high, low = second_pass(whole, right)

    lefts, place = [], 0
    for width, _ in plan:
        lefts.append(left[place : place + width])
        place += width
    for step in reversed(range(steps)):
        others = [None] * len(plan)
        for bit in range(steps):
            alike = [s for s in streams if order[s][step] == bit]
            if alike:
                came = flip(jnp.concatenate([lefts[s] for s in alike], 0), "rep", 1 << bit)
                place = 0
                for s in alike:
                    others[s] = came[place : place + lefts[s].shape[0]]
                    place += lefts[s].shape[0]
        if step:
            lefts = [stack(lefts[s], others[s], bit_of("rep", order[s][step])) for s in streams]

    here, there = [p[0] for p in places], [p[1] for p in places]
    error_out = error_rows(here, own, lefts, high, low, error.shape)
    error_out, weights_out, momentum_out = last_rows(
        error_out, there, far, others, here, lefts, high, low, weights_in[0], momentum_in[0]
    )
    return (error_out[None], weights_out[None], momentum_out[None])


def solution(mesh):
    in_specs = (
        P("rep", "mp"),
        P("mp"),
        P("rep", None),
        P("rep", "mp", None),
        P("mp", None),
        P("mp", "rep", None),
        P("mp", "rep", None),
    )
    out_specs = (P("rep", "mp", None), P("mp", "rep", None), P("mp", "rep", None))
    return jax.shard_map(
        on_device, mesh=mesh, in_specs=in_specs, out_specs=out_specs, check_vma=False
    )
```

```python
import dataclasses
import functools

import jax
import jax.numpy as jnp
from jax import lax
from jax.experimental import pallas as pl
from jax.experimental.pallas import tpu as pltpu
from jax.sharding import PartitionSpec as P

BLOCK = 128

SHARES = (
    (5, (0, 1, 2, 3)),
    (5, (1, 2, 0, 3)),
    (6, (2, 0, 1, 3)),
)
BACK = {0: (3, 2, 1, 0), 1: (3, 0, 2, 1), 2: (3, 1, 0, 2)}
TURNS = (2, 0, 1)

precise = lax.Precision.HIGHEST
epsilon = 1e-05
momentum_rate = 0.9
outer_rate = 0.7


def contract(first, second, dims, precision=precise):
    return lax.dot_general(
        first,
        second,
        ((dims[:1], dims[1:]), ((), ())),
        precision=precision,
        preferred_element_type=jnp.float32,
    )


def flip(value, axis, mask):
    size = lax.axis_size(axis)
    return lax.ppermute(value, axis, [(i, i ^ mask) for i in range(size)])


def bit_of(axis, bit):
    return (lax.axis_index(axis) >> bit) & 1


def rows_of(value, start, count):
    return lax.dynamic_slice_in_dim(value, start, count, 0)


def halve(value, axis, bit):
    half = value.shape[0] // 2
    side = bit_of(axis, bit)
    sent = rows_of(value, (1 - side) * half, half)
    return rows_of(value, side * half, half) + flip(sent, axis, 1 << bit)


def double(value, axis, bit):
    other = flip(value, axis, 1 << bit)
    side = bit_of(axis, bit)
    both = jnp.concatenate([value, value], 0)
    return lax.dynamic_update_slice_in_dim(both, other, (1 - side) * value.shape[0], 0)


def bit_count(size):
    return size.bit_length() - 1


def sum_over(value, axis):
    for bit in range(bit_count(lax.axis_size(axis))):
        value = value + flip(value, axis, 1 << bit)
    return value


def sum_everywhere(value):
    rep_bits = bit_count(lax.axis_size("rep"))
    mp_bits = bit_count(lax.axis_size("mp"))
    for bit in range(mp_bits):
        value = halve(value, "mp", bit)
    place = lax.axis_index("rep") & 3
    part = value.shape[0] // 4
    pieces = [rows_of(value, (place ^ m) * part, part) for m in range(4)]
    got = [flip(pieces[m], "rep", m) for m in (1, 2, 3)]
    value = (pieces[0] + got[0]) + (got[1] + got[2])
    bit = 2
    while bit < rep_bits:
        if bit + 1 < rep_bits:
            got = [flip(value, "rep", m << bit) for m in (1, 2, 3)]
            value = (value + got[0]) + (got[1] + got[2])
            bit += 2
        else:
            value = value + flip(value, "rep", 1 << bit)
            bit += 1
    got = [value] + [flip(value, "rep", m) for m in (1, 2, 3)]
    whole = jnp.zeros((4 * part,) + value.shape[1:], value.dtype)
    for m in range(4):
        whole = lax.dynamic_update_slice_in_dim(whole, got[m], (place ^ m) * part, 0)
    for bit in reversed(range(mp_bits)):
        whole = double(whole, "mp", bit)
    return whole


LIGHT = pl.CostEstimate(flops=1, bytes_accessed=1, transcendentals=0)


def kernel_call(*args, **options):
    return pl.pallas_call(
        *args, compiler_params=pltpu.CompilerParams(vmem_limit_bytes=10 * 2**20), **options
    )


def near(*arrays):
    return [pltpu.with_memory_space_constraint(array, pltpu.VMEM) for array in arrays]


def distant(array):
    return pltpu.with_memory_space_constraint(array, pltpu.HBM)


def near_shape(shape, dtype=jnp.float32):
    return pltpu.VMEM(shape, dtype)


def specs(*places):
    return [pl.BlockSpec(memory_space=place) for place in places]


def pieces_of(count, most):
    cuts, place = [], 0
    while place < count:
        size = min(most, count - place)
        cuts.append((place, size))
        place += size
    return cuts


def split(value):
    high = value.astype(jnp.bfloat16)
    return high, (value - high.astype(jnp.float32)).astype(jnp.bfloat16)


def squares_kernel(cuts, tokens_ref, out_ref, held_ref, sems):
    copies = []
    for index, (start, size) in enumerate(cuts):
        at = pl.ds(start, size)
        copies.append(
            pltpu.make_async_copy(tokens_ref.at[:, at], held_ref.at[:, at], sems.at[index])
        )
        copies[-1].start()
    total = None
    for copy, (start, size) in zip(copies, cuts):
        copy.wait()
        for place in range(start, start + size, BLOCK):
            wide = held_ref[:, place : place + BLOCK].astype(jnp.float32)
            total = wide * wide if total is None else total + wide * wide
    out_ref[...] = jnp.broadcast_to(jnp.sum(total, axis=1, keepdims=True), out_ref.shape)


def squares(tokens):
    cuts = pieces_of(tokens.shape[1], max(BLOCK, tokens.shape[1] // 4))
    return kernel_call(
        functools.partial(squares_kernel, cuts),
        out_shape=near_shape((tokens.shape[0], BLOCK)),
        in_specs=specs(pltpu.HBM),
        out_specs=specs(pltpu.VMEM)[0],
        scratch_shapes=[
            pltpu.VMEM(tokens.shape, tokens.dtype),
            pltpu.SemaphoreType.DMA((len(cuts),)),
        ],
    )(distant(tokens))


def merge_kernel(
    counts, depth, starts_ref, tokens_ref, squares_ref, gain_ref, grad_ref, error_ref, *refs
):
    outs, held_ref, sems = refs[: len(counts)], refs[-2], refs[-1]
    pieces, base = [], 0
    for s, count in counts:
        for place, size in pieces_of(count, 2 * BLOCK):
            there = pl.ds(pl.multiple_of(starts_ref[s] + place, BLOCK), size)
            here, spot = pl.ds(place, size), pl.ds(base + place, size)
            number = len(pieces)
            copies = [
                pltpu.make_async_copy(tokens_ref.at[:, there], held_ref.at[:, spot], sems.at[number, 0]),
                pltpu.make_async_copy(error_ref.at[there, :], outs[s].at[here, :], sems.at[number, 1]),
            ]
            for copy in copies:
                copy.start()
            pieces.append((s, there, here, spot, copies))
        base += count
    scale = lax.rsqrt(squares_ref[...] / depth + epsilon)[:, :1]
    for s, there, here, spot, copies in pieces:
        gain = gain_ref[:, there].astype(jnp.float32)
        copies[0].wait()
        normed = (held_ref[:, spot].astype(jnp.float32) * scale * gain).astype(jnp.bfloat16)
        change = lax.dot_general(
            normed, grad_ref[...], (((0,), (0,)), ((), ())), preferred_element_type=jnp.float32
        )
        copies[1].wait()
        outs[s][here, :] = change + outs[s][here, :]


def merge(starts, counts, turns, depth, tokens, square_sums, gain, grad, error):
    rows = sum(counts)
    in_turn = [(s, counts[s]) for s in turns]
    pieces = sum(len(pieces_of(count, 2 * BLOCK)) for count in counts)
    return kernel_call(
        functools.partial(merge_kernel, in_turn, depth),
        out_shape=tuple(near_shape((count, grad.shape[1])) for count in counts),
        in_specs=specs(pltpu.SMEM, pltpu.HBM, pltpu.VMEM, pltpu.VMEM, pltpu.VMEM, pltpu.HBM),
        out_specs=tuple(specs(*[pltpu.VMEM] * len(counts))),
        scratch_shapes=[
            pltpu.VMEM((tokens.shape[0], rows), tokens.dtype),
            pltpu.SemaphoreType.DMA((pieces, 2)),
        ],
        cost_estimate=pl.CostEstimate(
            flops=2 * rows * grad.shape[1] * tokens.shape[0],
            bytes_accessed=8 * rows * grad.shape[1] + 2 * tokens.shape[0] * rows,
            transcendentals=0,
        ),
    )(
        jnp.stack(starts).astype(jnp.int32),
        distant(tokens),
        *near(square_sums, gain, grad),
        distant(error),
    )


def sides_of(side, half):
    return pl.ds(pl.multiple_of(side * half, 8), half), pl.ds(pl.multiple_of((1 - side) * half, 8), half)


def join_kernel(count, side_ref, own_ref, got_ref, *refs):
    keep_ref, send_ref = refs[-2:]
    stays, goes = sides_of(side_ref[0], count // 2)
    send_ref[...] = own_ref[goes, :] + got_ref[goes, :]
    keep_ref[...] = own_ref[stays, :] + got_ref[stays, :]


def last_kernel(own_ref, got_ref, *refs):
    refs[-1][...] = own_ref[...] + got_ref[...]


def join(own, got, side, after):
    count, width = own.shape
    arrays, places = near(own, got), [pltpu.VMEM] * 2
    if side is None:
        kernel, shapes = last_kernel, (near_shape((count, width)),)
    else:
        kernel = functools.partial(join_kernel, count)
        shapes = (near_shape((count // 2, width)),) * 2
        arrays.insert(0, jnp.reshape(side, (1,)).astype(jnp.int32))
        places.insert(0, pltpu.SMEM)
    return kernel_call(
        kernel,
        out_shape=shapes,
        in_specs=specs(*places, *[pl.ANY] * len(after)),
        out_specs=tuple(specs(*[pltpu.VMEM] * len(shapes))),
        cost_estimate=LIGHT,
    )(*arrays, *after)


def bundles(plan, step):
    bits = sorted({stream.back[step] for stream in plan})
    groups = [[s for s, stream in enumerate(plan) if stream.back[step] == bit] for bit in bits]
    where = {}
    for index, group in enumerate(groups):
        place = 0
        for s in group:
            where[s] = (index, place)
            place += plan[s].width << step
    return bits, groups, where


def bundle_shapes(plan, step, width):
    _, groups, _ = bundles(plan, step)
    return tuple(near_shape((sum(plan[s].width << step for s in group), width)) for group in groups)


def gather_kernel(plan, step, sides_ref, *refs):
    bits, groups, before = bundles(plan, step)
    _, later_groups, after = bundles(plan, step + 1)
    n = len(groups)
    own, got, out = refs[:n], refs[n : 2 * n], refs[-len(later_groups) :]
    for s, stream in enumerate(plan):
        source, from_row = before[s]
        target, to_row = after[s]
        bit = stream.back[step]
        place = stream.order.index(bit)
        outer = 1 << sum(stream.order.index(b) < place for b in stream.back[:step])
        inner = (stream.width << step) // outer
        for i in range(outer):
            for refs_of, side in ((own, sides_ref[bit]), (got, 1 - sides_ref[bit])):
                row = pl.multiple_of(to_row + 2 * i * inner + side * inner, 8)
                out[target][pl.ds(row, inner), :] = refs_of[source][pl.ds(from_row + i * inner, inner), :]


def gather_step(plan, step, sides, own, got, after):
    shapes = bundle_shapes(plan, step + 1, own[0].shape[1])
    return kernel_call(
        functools.partial(gather_kernel, plan, step),
        out_shape=shapes,
        in_specs=specs(pltpu.SMEM, *[pltpu.VMEM] * (2 * len(own)), *[pl.ANY] * len(after)),
        out_specs=tuple(specs(*[pltpu.VMEM] * len(shapes))),
        cost_estimate=LIGHT,
    )(sides, *near(*own, *got), *after)


def gram_kernel(replicas, *refs):
    out_ref = refs[-1]
    rows = jnp.concatenate([ref[...] for ref in refs[:-1]], 0) / replicas
    blocks = rows.shape[1] // BLOCK
    place = 0
    for a in range(blocks):
        left = rows[:, a * BLOCK : (a + 1) * BLOCK]
        band = contract(left, rows[:, a * BLOCK :], (0, 0))
        for b in range(blocks - a):
            out_ref[place * BLOCK : (place + 1) * BLOCK, :] = band[:, b * BLOCK : (b + 1) * BLOCK]
            place += 1


def gram(parts, replicas):
    blocks = parts[0].shape[1] // BLOCK
    return kernel_call(
        functools.partial(gram_kernel, replicas),
        out_shape=near_shape((blocks * (blocks + 1) // 2 * BLOCK, BLOCK)),
        in_specs=specs(*[pltpu.VMEM] * len(parts)),
        out_specs=specs(pltpu.VMEM)[0],
    )(*near(*parts))


def factor(matrix):
    size = matrix.shape[0]
    group = 8
    lane = lax.broadcasted_iota(jnp.int32, (size, size), 1)
    row = lax.broadcasted_iota(jnp.int32, (size, size), 0)
    done = []
    live = matrix
    for start in range(0, size, group):
        if start:
            done.append(live[:group])
            live = live[group:]
        count = size - start
        lanes, rows = lane[start:], row[start:]
        columns = [
            jnp.broadcast_to(live[:, start + t : start + t + 1], (count, size)) for t in range(group)
        ]
        for t in range(group):
            pivot = start + t
            inverse = 1.0 / columns[t][t : t + 1, :]
            below = rows > pivot
            scale = jnp.where(below, columns[t] * inverse, 0.0)
            own = jnp.where(lanes[t : t + 1] == pivot, 1.0, live[t : t + 1, :])
            live = jnp.where(below & (lanes == pivot), 0.0, live) - scale * own
            for s in range(t + 1, group):
                columns[s] = columns[s] - scale * columns[s][t : t + 1, :]
    done.append(live)
    result = jnp.concatenate(done, 0)
    diagonal = jnp.sum(jnp.where(lane == row, result, 0.0), axis=1, keepdims=True)
    unit = jnp.where(lane < row, result, jnp.where(lane == row, 1.0, 0.0))
    return unit, diagonal


def first_kernel(plan, replicas, packed_ref, basis_ref, *refs):
    whole_ref, right_ref = refs[len(plan) : len(plan) + 2]
    blocks = basis_ref.shape[0] // BLOCK
    place = 0
    for a in range(blocks):
        for b in range(a, blocks):
            tile = packed_ref[place * BLOCK : (place + 1) * BLOCK, :]
            whole_ref[a * BLOCK : (a + 1) * BLOCK, b * BLOCK : (b + 1) * BLOCK] = tile
            if b > a:
                whole_ref[b * BLOCK : (b + 1) * BLOCK, a * BLOCK : (a + 1) * BLOCK] = tile.T
            place += 1
    basis = basis_ref[...]
    plain = contract(whole_ref[...], basis, (1, 0))
    unit, diagonal = factor(contract(basis, plain, (0, 0)))
    right = contract(plain, unit * lax.rsqrt(diagonal), (1, 1))
    right_ref[...] = right
    _, groups, _ = bundles(plan, 0)
    for group, left_ref in zip(groups, refs[len(plan) + 2 :]):
        rows = jnp.concatenate([refs[s][...] for s in group], 0) / replicas
        left_ref[...] = contract(rows, right, (1, 0))


def first_pass(plan, packed, basis, parts, replicas):
    width, rank = basis.shape
    shapes = (near_shape((width, width)), near_shape((width, rank)), *bundle_shapes(plan, 0, rank))
    whole, right, *lefts = kernel_call(
        functools.partial(first_kernel, plan, replicas),
        out_shape=shapes,
        in_specs=specs(*[pltpu.VMEM] * (2 + len(parts))),
        out_specs=tuple(specs(*[pltpu.VMEM] * len(shapes))),
    )(*near(packed, basis, *parts))
    return whole, right, lefts


def product_kernel(whole_ref, right_ref, plain_ref, gram_ref):
    right = right_ref[...]
    plain = contract(whole_ref[...], right, (1, 0))
    plain_ref[...] = plain
    gram_ref[...] = contract(right, plain, (0, 0))


def weight_kernel(plain_ref, gram_ref, high_ref, low_ref):
    unit, diagonal = factor(gram_ref[...])
    inverse = unit * lax.rsqrt(diagonal)
    turned = contract(inverse, plain_ref[...], (1, 1))
    high_ref[...], low_ref[...] = split(contract(inverse, turned, (0, 0)))


def second_pass(whole, right):
    width, rank = right.shape
    pair = functools.partial(
        kernel_call,
        in_specs=specs(pltpu.VMEM, pltpu.VMEM),
        out_specs=tuple(specs(pltpu.VMEM, pltpu.VMEM)),
    )
    plain, gram_matrix = pair(
        product_kernel, out_shape=(near_shape((width, rank)), near_shape((rank, rank)))
    )(*near(whole, right))
    half = near_shape((rank, width), jnp.bfloat16)
    return pair(weight_kernel, out_shape=(half, half))(*near(plain, gram_matrix))


def low_rank(left, high, low):
    left_high, left_low = split(left)
    dot = functools.partial(jnp.dot, preferred_element_type=jnp.float32)
    both = jnp.concatenate([left_high, left_low], 1)
    return dot(both, jnp.concatenate([high, high], 0)) + dot(left_high, low)


def error_pieces(plan, replicas):
    pieces, base = [], 0
    for s, stream in enumerate(plan):
        count = stream.width * replicas // 2
        pieces += [(s, place, base + place, size) for place, size in pieces_of(count, 4 * BLOCK)]
        base += count
    return pieces


def write_errors(plan, replicas, starts_ref, high, low, merged, lefts, out_ref, held_ref, sems, meanwhile=None):
    pieces = error_pieces(plan, replicas)
    _, _, where = bundles(plan, bit_count(replicas) - 1)
    fetched = []
    for number, (s, place, spot, size) in enumerate(pieces):
        fetched.append(
            pltpu.make_async_copy(
                merged[s].at[pl.ds(place, size), :], held_ref.at[pl.ds(spot, size), :], sems.at[0, number]
            )
        )
        fetched[-1].start()
    if meanwhile:
        meanwhile()
    written = []
    for number, (s, place, spot, size) in enumerate(pieces):
        index, first = where[s]
        there = pl.ds(pl.multiple_of(starts_ref[s] + place, BLOCK), size)
        here = pl.ds(spot, size)
        change = low_rank(lefts[index][pl.ds(first + place, size), :], high, low)
        fetched[number].wait()
        held_ref[here, :] = held_ref[here, :] - change
        written.append(
            pltpu.make_async_copy(held_ref.at[here, :], out_ref.at[there, :], sems.at[1, number])
        )
        written[-1].start()
    for copy in written:
        copy.wait()


def error_kernel(plan, replicas, starts_ref, high_ref, low_ref, *refs):
    n = len(plan)
    write_errors(
        plan, replicas, starts_ref, high_ref[...], low_ref[...], refs[:n], refs[n:-3], *refs[-3:]
    )


def last_error_kernel(plan, replicas, starts_ref, high_ref, low_ref, *refs):
    n = len(plan)
    _, groups, where = bundles(plan, bit_count(replicas) - 1)
    m = len(groups)
    merged, others, lefts = refs[:n], refs[n : n + m], refs[n + m : n + 2 * m]
    weights_ref, momentum_ref = refs[n + 2 * m : n + 2 * m + 2]
    out_ref, weights_out, momentum_out, held_ref, left_ref, sems = refs[-6:]
    high, low = high_ref[...], low_ref[...]
    rows = left_ref.shape[0]
    size = min(BLOCK, rows)

    def outer():
        for place in range(0, rows, size):
            want = starts_ref[2 * n] + place
            for k, bundle in ((0, others), (n, lefts)):
                for s, stream in enumerate(plan):
                    index, first = where[s]
                    skip = want - starts_ref[k + s]

                    @pl.when((skip >= 0) & (skip < stream.width * replicas // 2))
                    def _(bundle=bundle, index=index, first=first, skip=skip, place=place):
                        row = pl.multiple_of(first + skip, 8)
                        left_ref[place : place + size, :] = bundle[index][pl.ds(row, size), :]

        own_rows = low_rank(left_ref[...], high, low)
        momentum = momentum_rate * momentum_ref[...] + own_rows
        momentum_out[...] = momentum
        weights_out[...] = weights_ref[...] - outer_rate * (own_rows + momentum_rate * momentum)

    write_errors(plan, replicas, starts_ref, high, low, merged, others, out_ref, held_ref, sems, outer)


def error_options(plan, replicas, width, rank):
    pieces = error_pieces(plan, replicas)
    rows = sum(piece[3] for piece in pieces)
    scratch = pltpu.VMEM((rows, width), jnp.float32), pltpu.SemaphoreType.DMA((2, len(pieces)))
    cost = pl.CostEstimate(
        flops=6 * rows * width * rank, bytes_accessed=8 * rows * width, transcendentals=0
    )
    return scratch, cost


def error_rows(plan, replicas, starts, merged, lefts, high, low, shape):
    scratch, cost = error_options(plan, replicas, shape[1], high.shape[0])
    return kernel_call(
        functools.partial(error_kernel, plan, replicas),
        out_shape=jax.ShapeDtypeStruct(shape, jnp.float32),
        in_specs=specs(
            pltpu.SMEM, *[pltpu.VMEM] * 2, *[pltpu.HBM] * len(merged), *[pltpu.VMEM] * len(lefts)
        ),
        out_specs=specs(pltpu.HBM)[0],
        scratch_shapes=scratch,
        cost_estimate=cost,
    )(jnp.stack(starts).astype(jnp.int32), *near(high, low), *map(distant, merged), *near(*lefts))


def last_rows(plan, replicas, kept, starts, merged, others, lefts, high, low, weights, momentum):
    rows, width = weights.shape
    (held, sems), cost = error_options(plan, replicas, width, high.shape[0])
    arrays = [
        jnp.stack([*starts, lax.axis_index("rep") * rows]).astype(jnp.int32),
        *near(high, low),
        *map(distant, merged),
        *near(*others, *lefts),
        weights,
        momentum,
        kept,
    ]
    result = jax.ShapeDtypeStruct(weights.shape, jnp.float32)
    return kernel_call(
        functools.partial(last_error_kernel, plan, replicas),
        out_shape=(jax.ShapeDtypeStruct(kept.shape, jnp.float32), result, result),
        in_specs=specs(
            pltpu.SMEM,
            *[pltpu.VMEM] * 2,
            *[pltpu.HBM] * len(merged),
            *[pltpu.VMEM] * (2 * len(lefts) + 2),
            pltpu.HBM,
        ),
        out_specs=tuple(specs(pltpu.HBM, pltpu.VMEM, pltpu.VMEM)),
        scratch_shapes=[held, pltpu.VMEM((rows, high.shape[0]), jnp.float32), sems],
        input_output_aliases={len(arrays) - 1: 0},
        cost_estimate=cost,
    )(*arrays)


@dataclasses.dataclass(frozen=True)
class Stream:
    width: int
    order: tuple
    back: tuple


def stream_plan(replicas, rows_each):
    bits = bit_count(replicas)
    grain = max(8, 2 * BLOCK // replicas)
    units = rows_each // grain
    if bits == 4 and units % 16 == 0:
        shares = SHARES
        plan = [
            Stream(share * units // 16 * grain, order, BACK[order[0]])
            for share, order in shares
        ]
        return plan, TURNS
    streams = max(1, min(3, units, bits - 1))
    widths = [units // streams + (1 if s < units % streams else 0) for s in range(streams)]
    lead = list(range(min(3, bits)))
    rest = list(range(len(lead), bits))
    orders = [tuple(lead[s % len(lead) :] + lead[: s % len(lead)] + rest) for s in range(streams)]
    plan = [Stream(w * grain, order, order[::-1]) for w, order in zip(widths, orders)]
    return plan, range(streams)


def on_device(tokens_in, norm_gain, key_grad, error_in, basis_init, weights_in, momentum_in):
    replicas = lax.axis_size("rep")
    steps = bit_count(replicas)
    depth = tokens_in.shape[1]
    error = error_in[0]
    square_sums = sum_over(squares(tokens_in), "mp")
    basis = lax.all_gather(basis_init, "mp", axis=0, tiled=True)
    sources = (
        depth * lax.axis_size("mp"), tokens_in, square_sums, norm_gain[None, :], key_grad, error
    )

    plan, turns = stream_plan(replicas, depth // replicas)
    halves, here, there, place = [], [], [], 0
    for stream in plan:
        half = stream.width * replicas // 2
        side = bit_of("rep", stream.order[0])
        halves.append(half)
        here.append(place + side * half)
        there.append(place + (1 - side) * half)
        place += 2 * half
    far = merge(there, halves, turns, *sources)
    got = [flip(part, "rep", 1 << stream.order[0]) for part, stream in zip(far, plan)]
    own = merge(here, halves, turns, *sources)
    parts, after = list(own), [basis]
    for step in range(steps):
        for s in turns:
            if step + 1 < steps:
                bit = plan[s].order[step + 1]
                parts[s], send = join(parts[s], got[s], bit_of("rep", bit), after)
                got[s] = flip(send, "rep", 1 << bit)
            else:
                (parts[s],) = join(parts[s], got[s], None, after)
        after = []

    packed = sum_everywhere(gram(parts, replicas))
    whole, right, lefts = first_pass(plan, packed, basis, parts, replicas)
    high, low = second_pass(whole, right)

    bit_sides = jnp.stack([bit_of("rep", bit) for bit in range(steps)]).astype(jnp.int32)
    for step in range(steps):
        bits, _, _ = bundles(plan, step)
        others = [flip(left, "rep", 1 << bit) for left, bit in zip(lefts, bits)]
        if step + 1 < steps:
            lefts = gather_step(plan, step, bit_sides, lefts, others, [high])

    error_out = error_rows(plan, replicas, here, own, lefts, high, low, error.shape)
    error_out, weights_out, momentum_out = last_rows(
        plan, replicas, error_out, there + here, far, others, lefts, high, low, weights_in[0], momentum_in[0]
    )
    return (error_out[None], weights_out[None], momentum_out[None])


def solution(mesh):
    in_specs = (
        P("rep", "mp"),
        P("mp"),
        P("rep", None),
        P("rep", "mp", None),
        P("mp", None),
        P("mp", "rep", None),
        P("mp", "rep", None),
    )
    out_specs = (P("rep", "mp", None), P("mp", "rep", None), P("mp", "rep", None))
    return jax.shard_map(
        on_device, mesh=mesh, in_specs=in_specs, out_specs=out_specs, check_vma=False
    )
```

```python
import dataclasses
import functools

import jax
import jax.numpy as jnp
from jax import lax
from jax.experimental import pallas as pl
from jax.experimental.pallas import tpu as pltpu
from jax.sharding import PartitionSpec as P

BLOCK = 128

SHARES = (
    (5, (2, 0, 1, 3)),
    (3, (0, 1, 3, 2)),
    (3, (0, 1, 3, 2)),
    (5, (1, 2, 0, 3)),
)
BACK = {0: (3, 2, 1, 0), 1: (3, 0, 2, 1), 2: (3, 1, 0, 2)}
ARRIVALS = (1, 3, 0, 2, 1, 3, 2, 1, 0, 3, 1, 2, 0, 2, 3, 0)
TURNS = (3, 1, 0, 2)

precise = lax.Precision.HIGHEST
epsilon = 1e-05
momentum_rate = 0.9
outer_rate = 0.7


def contract(first, second, dims, precision=precise):
    return lax.dot_general(
        first,
        second,
        ((dims[:1], dims[1:]), ((), ())),
        precision=precision,
        preferred_element_type=jnp.float32,
    )


def flip(value, axis, mask):
    size = lax.axis_size(axis)
    return lax.ppermute(value, axis, [(i, i ^ mask) for i in range(size)])


def bit_of(axis, bit):
    return (lax.axis_index(axis) >> bit) & 1


def rows_of(value, start, count):
    return lax.dynamic_slice_in_dim(value, start, count, 0)


def halve(value, axis, bit):
    half = value.shape[0] // 2
    side = bit_of(axis, bit)
    sent = rows_of(value, (1 - side) * half, half)
    return rows_of(value, side * half, half) + flip(sent, axis, 1 << bit)


def double(value, axis, bit):
    other = flip(value, axis, 1 << bit)
    side = bit_of(axis, bit)
    both = jnp.concatenate([value, value], 0)
    return lax.dynamic_update_slice_in_dim(both, other, (1 - side) * value.shape[0], 0)


def bit_count(size):
    return size.bit_length() - 1


def sum_over(value, axis):
    for bit in range(bit_count(lax.axis_size(axis))):
        value = value + flip(value, axis, 1 << bit)
    return value


def sum_everywhere(value):
    rep_bits = bit_count(lax.axis_size("rep"))
    mp_bits = bit_count(lax.axis_size("mp"))
    for bit in range(mp_bits):
        value = halve(value, "mp", bit)
    place = lax.axis_index("rep") & 3
    part = value.shape[0] // 4
    pieces = [rows_of(value, (place ^ m) * part, part) for m in range(4)]
    got = [flip(pieces[m], "rep", m) for m in (1, 2, 3)]
    value = (pieces[0] + got[0]) + (got[1] + got[2])
    bit = 2
    while bit < rep_bits:
        if bit + 1 < rep_bits:
            got = [flip(value, "rep", m << bit) for m in (1, 2, 3)]
            value = (value + got[0]) + (got[1] + got[2])
            bit += 2
        else:
            value = value + flip(value, "rep", 1 << bit)
            bit += 1
    got = [value] + [flip(value, "rep", m) for m in (1, 2, 3)]
    whole = jnp.zeros((4 * part,) + value.shape[1:], value.dtype)
    for m in range(4):
        whole = lax.dynamic_update_slice_in_dim(whole, got[m], (place ^ m) * part, 0)
    for bit in reversed(range(mp_bits)):
        whole = double(whole, "mp", bit)
    return whole


LIGHT = pl.CostEstimate(flops=1, bytes_accessed=1, transcendentals=0)


def kernel_call(*args, **options):
    return pl.pallas_call(
        *args, compiler_params=pltpu.CompilerParams(vmem_limit_bytes=10 * 2**20), **options
    )


def near(*arrays):
    return [pltpu.with_memory_space_constraint(array, pltpu.VMEM) for array in arrays]


def distant(array):
    return pltpu.with_memory_space_constraint(array, pltpu.HBM)


def near_shape(shape, dtype=jnp.float32):
    return pltpu.VMEM(shape, dtype)


def specs(*places):
    return [pl.BlockSpec(memory_space=place) for place in places]


def pieces_of(count, most):
    cuts, place = [], 0
    while place < count:
        size = min(most, count - place)
        cuts.append((place, size))
        place += size
    return cuts


def split(value):
    high = value.astype(jnp.bfloat16)
    return high, (value - high.astype(jnp.float32)).astype(jnp.bfloat16)


def squares_kernel(cuts, tokens_ref, out_ref, held_ref, sems):
    copies = []
    for index, (start, size) in enumerate(cuts):
        at = pl.ds(start, size)
        copies.append(
            pltpu.make_async_copy(tokens_ref.at[:, at], held_ref.at[:, at], sems.at[index])
        )
        copies[-1].start()
    total = None
    for copy, (start, size) in zip(copies, cuts):
        copy.wait()
        for place in range(start, start + size, BLOCK):
            wide = held_ref[:, place : place + BLOCK].astype(jnp.float32)
            total = wide * wide if total is None else total + wide * wide
    out_ref[...] = jnp.broadcast_to(jnp.sum(total, axis=1, keepdims=True), out_ref.shape)


def squares(tokens):
    cuts = pieces_of(tokens.shape[1], max(BLOCK, tokens.shape[1] // 4))
    return kernel_call(
        functools.partial(squares_kernel, cuts),
        out_shape=near_shape((tokens.shape[0], BLOCK)),
        in_specs=specs(pltpu.HBM),
        out_specs=specs(pltpu.VMEM)[0],
        scratch_shapes=[
            pltpu.VMEM(tokens.shape, tokens.dtype),
            pltpu.SemaphoreType.DMA((len(cuts),)),
        ],
    )(distant(tokens))


def merge_kernel(
    counts, leaves, depth, starts_ref, tokens_ref, squares_ref, gain_ref, grad_ref, error_ref, *refs
):
    n = len(counts)
    *refs, held_ref, sems, out_sems = refs
    if leaves:
        *outs, sum_ref = refs
    else:
        outs, whole_ref = refs[-n - 1 : -1], refs[-1]
    pieces, base = [], 0
    for s, count in enumerate(counts):
        for place, size in pieces_of(count, 4 * BLOCK):
            there = pl.ds(pl.multiple_of(starts_ref[s] + place, BLOCK), size)
            here, spot = pl.ds(place, size), pl.ds(base + place, size)
            number = len(pieces)
            target = sum_ref.at[spot, :] if leaves else outs[s].at[here, :]
            copies = [
                pltpu.make_async_copy(tokens_ref.at[:, there], held_ref.at[:, spot], sems.at[number, 0]),
                pltpu.make_async_copy(error_ref.at[there, :], target, sems.at[number, 1]),
            ]
            for copy in copies:
                copy.start()
            pieces.append((s, there, here, spot, target, copies))
        base += count
    scale = lax.rsqrt(squares_ref[...] / depth + epsilon)[:, :1]
    written = []
    for s, there, here, spot, target, copies in pieces:
        gain = gain_ref[:, there].astype(jnp.float32)
        copies[0].wait()
        normed = (held_ref[:, spot].astype(jnp.float32) * scale * gain).astype(jnp.bfloat16)
        change = lax.dot_general(
            normed, grad_ref[...], (((0,), (0,)), ((), ())), preferred_element_type=jnp.float32
        )
        copies[1].wait()
        target[...] = change + target[...]
        away = outs[s].at[here, :] if leaves else whole_ref.at[spot, :]
        written.append(pltpu.make_async_copy(target, away, out_sems.at[len(written)]))
        written[-1].start()
    for copy in written:
        copy.wait()


def merge(leaves, starts, counts, depth, tokens, square_sums, gain, grad, error, after=()):
    rows, width = sum(counts), grad.shape[1]
    pieces = sum(len(pieces_of(count, 4 * BLOCK)) for count in counts)
    if leaves:
        shapes = [pltpu.HBM((count, width), jnp.float32) for count in counts]
        places = [pltpu.HBM] * len(counts)
        scratch = [pltpu.VMEM((rows, width), jnp.float32)]
    else:
        shapes = [near_shape((count, width)) for count in counts]
        shapes.append(pltpu.HBM((rows, width), jnp.float32))
        places = [*[pltpu.VMEM] * len(counts), pltpu.HBM]
        scratch = []
    return kernel_call(
        functools.partial(merge_kernel, counts, leaves, depth),
        out_shape=tuple(shapes),
        in_specs=specs(
            pltpu.SMEM, pltpu.HBM, *[pltpu.VMEM] * 3, pltpu.HBM, *[pl.ANY] * len(after)
        ),
        out_specs=tuple(specs(*places)),
        scratch_shapes=[
            *scratch,
            pltpu.VMEM((tokens.shape[0], rows), tokens.dtype),
            pltpu.SemaphoreType.DMA((pieces, 2)),
            pltpu.SemaphoreType.DMA((pieces,)),
        ],
        cost_estimate=pl.CostEstimate(
            flops=2 * rows * width * tokens.shape[0],
            bytes_accessed=8 * rows * width + 2 * tokens.shape[0] * rows,
            transcendentals=0,
        ),
    )(
        jnp.stack(starts).astype(jnp.int32),
        distant(tokens),
        *near(square_sums, gain, grad),
        distant(error),
        *after,
    )


def sides_of(side, half):
    return pl.ds(pl.multiple_of(side * half, 8), half), pl.ds(pl.multiple_of((1 - side) * half, 8), half)


def join_kernel(count, side_ref, own_ref, got_ref, *refs):
    keep_ref, send_ref = refs[-2:]
    stays, goes = sides_of(side_ref[0], count // 2)
    send_ref[...] = own_ref[goes, :] + got_ref[goes, :]
    keep_ref[...] = own_ref[stays, :] + got_ref[stays, :]


def last_kernel(own_ref, got_ref, *refs):
    refs[-1][...] = own_ref[...] + got_ref[...]


def join(own, got, side, after, held):
    count, width = own.shape
    arrays, places = near(own, got), [pltpu.VMEM] * 2
    if side is None:
        kernel, shapes = last_kernel, (near_shape((count, width)),)
    else:
        kernel = functools.partial(join_kernel, count)
        shapes = (near_shape((count // 2, width)),) * 2
        arrays.insert(0, jnp.reshape(side, (1,)).astype(jnp.int32))
        places.insert(0, pltpu.SMEM)
    return kernel_call(
        kernel,
        out_shape=shapes,
        in_specs=specs(*places, *[pl.ANY] * len(after), *[pltpu.VMEM] * len(held)),
        out_specs=tuple(specs(*[pltpu.VMEM] * len(shapes))),
        cost_estimate=LIGHT,
    )(*arrays, *after, *near(*held))


def bundles(plan, step):
    bits = sorted({stream.back[step] for stream in plan})
    groups = [[s for s, stream in enumerate(plan) if stream.back[step] == bit] for bit in bits]
    where = {}
    for index, group in enumerate(groups):
        place = 0
        for s in group:
            where[s] = (index, place)
            place += plan[s].width << step
    return bits, groups, where


def bundle_shapes(plan, step, width):
    _, groups, _ = bundles(plan, step)
    return tuple(near_shape((sum(plan[s].width << step for s in group), width)) for group in groups)


def gather_kernel(plan, step, sides_ref, *refs):
    bits, groups, before = bundles(plan, step)
    _, later_groups, after = bundles(plan, step + 1)
    n = len(groups)
    own, got, out = refs[:n], refs[n : 2 * n], refs[-len(later_groups) :]
    for s, stream in enumerate(plan):
        source, from_row = before[s]
        target, to_row = after[s]
        bit = stream.back[step]
        place = stream.order.index(bit)
        outer = 1 << sum(stream.order.index(b) < place for b in stream.back[:step])
        inner = (stream.width << step) // outer
        for i in range(outer):
            for refs_of, side in ((own, sides_ref[bit]), (got, 1 - sides_ref[bit])):
                row = pl.multiple_of(to_row + 2 * i * inner + side * inner, 8)
                out[target][pl.ds(row, inner), :] = refs_of[source][pl.ds(from_row + i * inner, inner), :]


def gather_step(plan, step, sides, own, got, after):
    shapes = bundle_shapes(plan, step + 1, own[0].shape[1])
    return kernel_call(
        functools.partial(gather_kernel, plan, step),
        out_shape=shapes,
        in_specs=specs(pltpu.SMEM, *[pltpu.VMEM] * (2 * len(own)), *[pl.ANY] * len(after)),
        out_specs=tuple(specs(*[pltpu.VMEM] * len(shapes))),
        cost_estimate=LIGHT,
    )(sides, *near(*own, *got), *after)


def packed_rows(width, share):
    blocks = width // BLOCK
    rows = (blocks * (blocks - 1) // 2 + (blocks + 1) // 2) * BLOCK + 8 * (blocks // 2)
    return -(-rows // share) * share


def block_grid():
    row = lax.broadcasted_iota(jnp.int32, (BLOCK, BLOCK), 0)
    column = lax.broadcasted_iota(jnp.int32, (BLOCK, BLOCK), 1)
    return row, column


def gram_kernel(replicas, *refs):
    out_ref = refs[-1]
    rows = jnp.concatenate([ref[...] for ref in refs[:-1]], 0) / replicas
    blocks = rows.shape[1] // BLOCK
    row, column = block_grid()
    place, diagonals = 0, []
    for a in range(blocks):
        left = rows[:, a * BLOCK : (a + 1) * BLOCK]
        band = contract(left, rows[:, a * BLOCK :], (0, 0))
        diagonals.append(band[:, :BLOCK])
        for b in range(1, blocks - a):
            out_ref[place : place + BLOCK, :] = band[:, b * BLOCK : (b + 1) * BLOCK]
            place += BLOCK
    for a in range(0, blocks, 2):
        both = diagonals[a]
        if a + 1 < blocks:
            both = jnp.where(row <= column, both, diagonals[a + 1])
        out_ref[place : place + BLOCK, :] = both
        place += BLOCK
    for a in range(1, blocks, 2):
        line = jnp.sum(jnp.where(row == column, diagonals[a], 0.0), axis=0, keepdims=True)
        out_ref[place : place + 8, :] = jnp.broadcast_to(line, (8, BLOCK))
        place += 8
    if place < out_ref.shape[0]:
        out_ref[place:, :] = jnp.zeros((out_ref.shape[0] - place, BLOCK), jnp.float32)


def gram(parts, replicas, share):
    rows = packed_rows(parts[0].shape[1], share)
    return kernel_call(
        functools.partial(gram_kernel, replicas),
        out_shape=near_shape((rows, BLOCK)),
        in_specs=specs(*[pltpu.VMEM] * len(parts)),
        out_specs=specs(pltpu.VMEM)[0],
    )(*near(*parts))


def unpack(packed_ref, whole_ref):
    blocks = whole_ref.shape[0] // BLOCK
    row, column = block_grid()
    place = 0

    def put(a, b, tile):
        whole_ref[a * BLOCK : (a + 1) * BLOCK, b * BLOCK : (b + 1) * BLOCK] = tile

    for a in range(blocks):
        for b in range(a + 1, blocks):
            tile = packed_ref[place : place + BLOCK, :]
            put(a, b, tile)
            put(b, a, tile.T)
            place += BLOCK
    line_place = place + (blocks + 1) // 2 * BLOCK
    for a in range(0, blocks, 2):
        tile = packed_ref[place : place + BLOCK, :]
        turned = tile.T
        place += BLOCK
        put(a, a, jnp.where(row <= column, tile, turned))
        if a + 1 < blocks:
            line = packed_ref[line_place : line_place + 1, :]
            line_place += 8
            put(a + 1, a + 1, jnp.where(row > column, tile, jnp.where(row < column, turned, line)))


def factor(matrix):
    size = matrix.shape[0]
    group = 8
    lane = lax.broadcasted_iota(jnp.int32, (size, size), 1)
    row = lax.broadcasted_iota(jnp.int32, (size, size), 0)
    done = []
    live = matrix
    for start in range(0, size, group):
        if start:
            done.append(live[:group])
            live = live[group:]
        count = size - start
        lanes, rows = lane[start:], row[start:]
        columns = [
            jnp.broadcast_to(live[:, start + t : start + t + 1], (count, size)) for t in range(group)
        ]
        for t in range(group):
            pivot = start + t
            inverse = 1.0 / columns[t][t : t + 1, :]
            below = rows > pivot
            scale = jnp.where(below, columns[t] * inverse, 0.0)
            own = jnp.where(lanes[t : t + 1] == pivot, 1.0, live[t : t + 1, :])
            live = jnp.where(below & (lanes == pivot), 0.0, live) - scale * own
            for s in range(t + 1, group):
                columns[s] = columns[s] - scale * columns[s][t : t + 1, :]
    done.append(live)
    result = jnp.concatenate(done, 0)
    diagonal = jnp.sum(jnp.where(lane == row, result, 0.0), axis=1, keepdims=True)
    unit = jnp.where(lane < row, result, jnp.where(lane == row, 1.0, 0.0))
    return unit, diagonal


def first_kernel(plan, replicas, packed_ref, basis_ref, *refs):
    whole_ref, right_ref = refs[len(plan) : len(plan) + 2]
    unpack(packed_ref, whole_ref)
    basis = basis_ref[...]
    plain = contract(whole_ref[...], basis, (1, 0))
    unit, diagonal = factor(contract(basis, plain, (0, 0)))
    right = contract(plain, unit * lax.rsqrt(diagonal), (1, 1))
    right_ref[...] = right
    _, groups, _ = bundles(plan, 0)
    for group, left_ref in zip(groups, refs[len(plan) + 2 :]):
        rows = jnp.concatenate([refs[s][...] for s in group], 0) / replicas
        left_ref[...] = contract(rows, right, (1, 0))


def first_pass(plan, packed, basis, parts, replicas):
    width, rank = basis.shape
    shapes = (near_shape((width, width)), near_shape((width, rank)), *bundle_shapes(plan, 0, rank))
    whole, right, *lefts = kernel_call(
        functools.partial(first_kernel, plan, replicas),
        out_shape=shapes,
        in_specs=specs(*[pltpu.VMEM] * (2 + len(parts))),
        out_specs=tuple(specs(*[pltpu.VMEM] * len(shapes))),
    )(*near(packed, basis, *parts))
    return whole, right, lefts


def product_kernel(whole_ref, right_ref, plain_ref, gram_ref):
    right = right_ref[...]
    plain = contract(whole_ref[...], right, (1, 0))
    plain_ref[...] = plain
    gram_ref[...] = contract(right, plain, (0, 0))


def weight_kernel(plain_ref, gram_ref, high_ref, low_ref):
    unit, diagonal = factor(gram_ref[...])
    inverse = unit * lax.rsqrt(diagonal)
    turned = contract(inverse, plain_ref[...], (1, 1))
    high_ref[...], low_ref[...] = split(contract(inverse, turned, (0, 0)))


def second_pass(whole, right):
    width, rank = right.shape
    pair = functools.partial(
        kernel_call,
        in_specs=specs(pltpu.VMEM, pltpu.VMEM),
        out_specs=tuple(specs(pltpu.VMEM, pltpu.VMEM)),
    )
    plain, gram_matrix = pair(
        product_kernel, out_shape=(near_shape((width, rank)), near_shape((rank, rank)))
    )(*near(whole, right))
    half = near_shape((rank, width), jnp.bfloat16)
    return pair(weight_kernel, out_shape=(half, half))(*near(plain, gram_matrix))


def low_rank(left, high, low):
    left_high, left_low = split(left)
    dot = functools.partial(jnp.dot, preferred_element_type=jnp.float32)
    both = jnp.concatenate([left_high, left_low], 1)
    return dot(both, jnp.concatenate([high, high], 0)) + dot(left_high, low)


def error_pieces(plan, replicas):
    pieces, base = [], 0
    for s, stream in enumerate(plan):
        count = stream.width * replicas // 2
        pieces += [(s, place, base + place, size) for place, size in pieces_of(count, 4 * BLOCK)]
        base += count
    return pieces


def write_errors(plan, replicas, starts_ref, high, low, merged, lefts, out_ref, held_ref, sems, fetched):
    _, _, where = bundles(plan, bit_count(replicas) - 1)
    written = []
    for number, (s, place, spot, size) in enumerate(error_pieces(plan, replicas)):
        index, first = where[s]
        there = pl.ds(pl.multiple_of(starts_ref[s] + place, BLOCK), size)
        here = pl.ds(spot, size)
        change = low_rank(lefts[index][pl.ds(first + place, size), :], high, low)
        if fetched:
            fetched[number].wait()
        held_ref[here, :] = merged[here, :] - change
        written.append(
            pltpu.make_async_copy(held_ref.at[here, :], out_ref.at[there, :], sems.at[number])
        )
        written[-1].start()
    return written


def error_kernel(plan, replicas, starts_ref, high_ref, low_ref, own_ref, *refs):
    n = len(plan)
    out_ref, near_ref, held_ref, fetch_sems, sems, near_sems = refs[-6:]
    fetched = []
    for number, (_, _, spot, size) in enumerate(error_pieces(plan, replicas)):
        here = pl.ds(spot, size)
        fetched.append(
            pltpu.make_async_copy(own_ref.at[here, :], held_ref.at[here, :], fetch_sems.at[number])
        )
        fetched[-1].start()
    others, base = [], 0
    for s, stream in enumerate(plan):
        count = stream.width * replicas // 2
        others.append(
            pltpu.make_async_copy(refs[s], near_ref.at[pl.ds(base, count), :], near_sems.at[s])
        )
        others[-1].start()
        base += count
    written = write_errors(
        plan, replicas, starts_ref, high_ref[...], low_ref[...], held_ref, refs[n:-6], out_ref, held_ref,
        sems, fetched,
    )
    for copy in written + others:
        copy.wait()


def last_error_kernel(plan, replicas, starts_ref, high_ref, low_ref, merged_ref, *refs):
    n = len(plan)
    _, groups, where = bundles(plan, bit_count(replicas) - 1)
    m = len(groups)
    others, lefts = refs[:m], refs[m : 2 * m]
    weights_ref, momentum_ref = refs[2 * m : 2 * m + 2]
    out_ref, weights_out, momentum_out, held_ref, left_ref, sems = refs[-6:]
    high, low = high_ref[...], low_ref[...]
    written = write_errors(
        plan, replicas, starts_ref, high, low, merged_ref, others, out_ref, held_ref, sems, None
    )
    rows = left_ref.shape[0]
    size = min(BLOCK, rows)
    for place in range(0, rows, size):
        want = starts_ref[2 * n] + place
        for k, bundle in ((0, others), (n, lefts)):
            for s, stream in enumerate(plan):
                index, first = where[s]
                skip = want - starts_ref[k + s]

                @pl.when((skip >= 0) & (skip < stream.width * replicas // 2))
                def _(bundle=bundle, index=index, first=first, skip=skip, place=place):
                    row = pl.multiple_of(first + skip, 8)
                    left_ref[place : place + size, :] = bundle[index][pl.ds(row, size), :]

    own_rows = low_rank(left_ref[...], high, low)
    momentum = momentum_rate * momentum_ref[...] + own_rows
    momentum_out[...] = momentum
    weights_out[...] = weights_ref[...] - outer_rate * (own_rows + momentum_rate * momentum)
    for copy in written:
        copy.wait()


def error_options(plan, replicas, width, rank):
    pieces = error_pieces(plan, replicas)
    rows = sum(piece[3] for piece in pieces)
    scratch = pltpu.VMEM((rows, width), jnp.float32), pltpu.SemaphoreType.DMA((len(pieces),))
    cost = pl.CostEstimate(
        flops=6 * rows * width * rank, bytes_accessed=8 * rows * width, transcendentals=0
    )
    return scratch, cost


def error_rows(plan, replicas, starts, own, far, lefts, high, low, shape):
    scratch, cost = error_options(plan, replicas, shape[1], high.shape[0])
    return kernel_call(
        functools.partial(error_kernel, plan, replicas),
        out_shape=(jax.ShapeDtypeStruct(shape, jnp.float32), near_shape(own.shape)),
        in_specs=specs(
            pltpu.SMEM, *[pltpu.VMEM] * 2, *[pltpu.HBM] * (1 + len(far)), *[pltpu.VMEM] * len(lefts)
        ),
        out_specs=tuple(specs(pltpu.HBM, pltpu.VMEM)),
        scratch_shapes=[*scratch, scratch[1], pltpu.SemaphoreType.DMA((len(far),))],
        cost_estimate=cost,
    )(
        jnp.stack(starts).astype(jnp.int32), *near(high, low), distant(own), *map(distant, far), *near(*lefts)
    )


def last_rows(plan, replicas, kept, starts, merged, others, lefts, high, low, weights, momentum):
    rows, width = weights.shape
    (held, sems), cost = error_options(plan, replicas, width, high.shape[0])
    arrays = [
        jnp.stack([*starts, lax.axis_index("rep") * rows]).astype(jnp.int32),
        *near(high, low, merged, *others, *lefts),
        weights,
        momentum,
        kept,
    ]
    result = jax.ShapeDtypeStruct(weights.shape, jnp.float32)
    return kernel_call(
        functools.partial(last_error_kernel, plan, replicas),
        out_shape=(jax.ShapeDtypeStruct(kept.shape, jnp.float32), result, result),
        in_specs=specs(pltpu.SMEM, *[pltpu.VMEM] * (2 * len(lefts) + 5), pltpu.HBM),
        out_specs=tuple(specs(pltpu.HBM, pltpu.VMEM, pltpu.VMEM)),
        scratch_shapes=[held, pltpu.VMEM((rows, high.shape[0]), jnp.float32), sems],
        input_output_aliases={len(arrays) - 1: 0},
        cost_estimate=cost,
    )(*arrays)


@dataclasses.dataclass(frozen=True)
class Stream:
    width: int
    order: tuple
    back: tuple


def stream_plan(replicas, rows_each):
    bits = bit_count(replicas)
    grain = max(8, 2 * BLOCK // replicas)
    units = rows_each // grain
    if bits == 4 and units % 16 == 0:
        shares = SHARES
        plan = [
            Stream(share * units // 16 * grain, order, BACK[order[0]])
            for share, order in shares
        ]
        return plan, TURNS, ARRIVALS
    streams = max(1, min(3, units, bits - 1))
    widths = [units // streams + (1 if s < units % streams else 0) for s in range(streams)]
    lead = list(range(min(3, bits)))
    rest = list(range(len(lead), bits))
    orders = [tuple(lead[s % len(lead) :] + lead[: s % len(lead)] + rest) for s in range(streams)]
    plan = [Stream(w * grain, order, order[::-1]) for w, order in zip(widths, orders)]
    return plan, range(streams), [s for _ in range(bits) for s in range(streams)]


def on_device(tokens_in, norm_gain, key_grad, error_in, basis_init, weights_in, momentum_in):
    replicas = lax.axis_size("rep")
    steps = bit_count(replicas)
    depth = tokens_in.shape[1]
    error = error_in[0]
    square_sums = sum_over(squares(tokens_in), "mp")
    basis = lax.all_gather(basis_init, "mp", axis=0, tiled=True)
    sources = (
        depth * lax.axis_size("mp"), tokens_in, square_sums, norm_gain[None, :], key_grad, error
    )

    plan, turns, arrivals = stream_plan(replicas, depth // replicas)
    halves, here, there, place = [], [], [], 0
    for stream in plan:
        half = stream.width * replicas // 2
        side = bit_of("rep", stream.order[0])
        halves.append(half)
        here.append(place + side * half)
        there.append(place + (1 - side) * half)
        place += 2 * half
    far = merge(True, there, halves, *sources)
    got = [flip(part, "rep", 1 << stream.order[0]) for part, stream in zip(far, plan)]
    *own, own_kept = merge(False, here, halves, *sources, after=[basis])
    parts, after, done = list(own), [], [0] * len(plan)
    for s in arrivals:
        done[s] += 1
        came = got[s]
        if done[s] < steps:
            bit = plan[s].order[done[s]]
            parts[s], send = join(parts[s], came, bit_of("rep", bit), after, [p for k, p in enumerate(parts) if k != s])
            got[s] = flip(send, "rep", 1 << bit)
        else:
            (parts[s],) = join(parts[s], came, None, after, [])
        after = [came]

    packed = sum_everywhere(gram(parts, replicas, 32 * lax.axis_size("mp")))
    whole, right, lefts = first_pass(plan, packed, basis, parts, replicas)
    high, low = second_pass(whole, right)

    bit_sides = jnp.stack([bit_of("rep", bit) for bit in range(steps)]).astype(jnp.int32)
    for step in range(steps):
        bits, _, _ = bundles(plan, step)
        others = [flip(left, "rep", 1 << bit) for left, bit in zip(lefts, bits)]
        if step + 1 < steps:
            lefts = gather_step(plan, step, bit_sides, lefts, others, [high])

    error_out, far_near = error_rows(
        plan, replicas, here, own_kept, far, lefts, high, low, error.shape
    )
    error_out, weights_out, momentum_out = last_rows(
        plan, replicas, error_out, there + here, far_near, others, lefts, high, low, weights_in[0],
        momentum_in[0],
    )
    return (error_out[None], weights_out[None], momentum_out[None])


def solution(mesh):
    in_specs = (
        P("rep", "mp"),
        P("mp"),
        P("rep", None),
        P("rep", "mp", None),
        P("mp", None),
        P("mp", "rep", None),
        P("mp", "rep", None),
    )
    out_specs = (P("rep", "mp", None), P("mp", "rep", None), P("mp", "rep", None))
    return jax.shard_map(
        on_device, mesh=mesh, in_specs=in_specs, out_specs=out_specs, check_vma=False
    )
```

```python
import dataclasses
import functools

import jax
import jax.numpy as jnp
from jax import lax
from jax.experimental import pallas as pl
from jax.experimental.pallas import tpu as pltpu
from jax.sharding import PartitionSpec as P

BLOCK = 128

SHARES = (
    (3, (0, 2, 3, 1)),
    (4, (2, 0, 1, 3)),
    (3, (0, 1, 3, 2)),
    (3, (1, 2, 0, 3)),
    (3, (1, 3, 0, 2)),
)
BACK = {0: (3, 2, 1, 0), 1: (3, 0, 2, 1), 2: (3, 1, 0, 2)}
ARRIVALS = (0, 4, 1, 2, 3, 0, 4, 1, 2, 4, 0, 3, 1, 0, 2, 3, 4, 1, 2, 3)
TURNS = (0, 4, 2, 1, 3)

precise = lax.Precision.HIGHEST
epsilon = 1e-05
momentum_rate = 0.9
outer_rate = 0.7


def contract(first, second, dims, precision=precise):
    return lax.dot_general(
        first,
        second,
        ((dims[:1], dims[1:]), ((), ())),
        precision=precision,
        preferred_element_type=jnp.float32,
    )


def flip(value, axis, mask):
    size = lax.axis_size(axis)
    return lax.ppermute(value, axis, [(i, i ^ mask) for i in range(size)])


def bit_of(axis, bit):
    return (lax.axis_index(axis) >> bit) & 1


def rows_of(value, start, count):
    return lax.dynamic_slice_in_dim(value, start, count, 0)


def halve(value, axis, bit):
    half = value.shape[0] // 2
    side = bit_of(axis, bit)
    sent = rows_of(value, (1 - side) * half, half)
    return rows_of(value, side * half, half) + flip(sent, axis, 1 << bit)


def double(value, axis, bit):
    other = flip(value, axis, 1 << bit)
    side = bit_of(axis, bit)
    both = jnp.concatenate([value, value], 0)
    return lax.dynamic_update_slice_in_dim(both, other, (1 - side) * value.shape[0], 0)


def bit_count(size):
    return size.bit_length() - 1


def sum_over(value, axis):
    for bit in range(bit_count(lax.axis_size(axis))):
        value = value + flip(value, axis, 1 << bit)
    return value


def sum_everywhere(value):
    rep_bits = bit_count(lax.axis_size("rep"))
    mp_bits = bit_count(lax.axis_size("mp"))
    for bit in range(mp_bits):
        value = halve(value, "mp", bit)
    place = lax.axis_index("rep") & 3
    part = value.shape[0] // 4
    pieces = [rows_of(value, (place ^ m) * part, part) for m in range(4)]
    got = [flip(pieces[m], "rep", m) for m in (1, 2, 3)]
    value = (pieces[0] + got[0]) + (got[1] + got[2])
    bit = 2
    while bit < rep_bits:
        if bit + 1 < rep_bits:
            got = [flip(value, "rep", m << bit) for m in (1, 2, 3)]
            value = (value + got[0]) + (got[1] + got[2])
            bit += 2
        else:
            value = value + flip(value, "rep", 1 << bit)
            bit += 1
    got = [value] + [flip(value, "rep", m) for m in (1, 2, 3)]
    whole = jnp.zeros((4 * part,) + value.shape[1:], value.dtype)
    for m in range(4):
        whole = lax.dynamic_update_slice_in_dim(whole, got[m], (place ^ m) * part, 0)
    for bit in reversed(range(mp_bits)):
        whole = double(whole, "mp", bit)
    return whole


LIGHT = pl.CostEstimate(flops=1, bytes_accessed=1, transcendentals=0)


def kernel_call(*args, **options):
    return pl.pallas_call(
        *args, compiler_params=pltpu.CompilerParams(vmem_limit_bytes=10 * 2**20), **options
    )


def near(*arrays):
    return [pltpu.with_memory_space_constraint(array, pltpu.VMEM) for array in arrays]


def distant(array):
    return pltpu.with_memory_space_constraint(array, pltpu.HBM)


def near_shape(shape, dtype=jnp.float32):
    return pltpu.VMEM(shape, dtype)


def specs(*places):
    return [pl.BlockSpec(memory_space=place) for place in places]


def pieces_of(count, most):
    cuts, place = [], 0
    while place < count:
        size = min(most, count - place)
        cuts.append((place, size))
        place += size
    return cuts


def split(value):
    high = value.astype(jnp.bfloat16)
    return high, (value - high.astype(jnp.float32)).astype(jnp.bfloat16)


def squares_kernel(cuts, tokens_ref, out_ref, held_ref, sems):
    copies = []
    for index, (start, size) in enumerate(cuts):
        at = pl.ds(start, size)
        copies.append(
            pltpu.make_async_copy(tokens_ref.at[:, at], held_ref.at[:, at], sems.at[index])
        )
        copies[-1].start()
    total = None
    for copy, (start, size) in zip(copies, cuts):
        copy.wait()
        for place in range(start, start + size, BLOCK):
            wide = held_ref[:, place : place + BLOCK].astype(jnp.float32)
            total = wide * wide if total is None else total + wide * wide
    out_ref[...] = jnp.broadcast_to(jnp.sum(total, axis=1, keepdims=True), out_ref.shape)


def squares(tokens):
    cuts = pieces_of(tokens.shape[1], max(BLOCK, tokens.shape[1] // 4))
    return kernel_call(
        functools.partial(squares_kernel, cuts),
        out_shape=near_shape((tokens.shape[0], BLOCK)),
        in_specs=specs(pltpu.HBM),
        out_specs=specs(pltpu.VMEM)[0],
        scratch_shapes=[
            pltpu.VMEM(tokens.shape, tokens.dtype),
            pltpu.SemaphoreType.DMA((len(cuts),)),
        ],
    )(distant(tokens))


def merge_kernel(
    counts, leaves, depth, starts_ref, tokens_ref, squares_ref, gain_ref, grad_ref, error_ref, *refs
):
    n = len(counts)
    *refs, held_ref, sems, out_sems = refs
    if leaves:
        *outs, sum_ref = refs
    else:
        outs, whole_ref = refs[-n - 1 : -1], refs[-1]
    pieces, base = [], 0
    for s, count in enumerate(counts):
        for place, size in pieces_of(count, 4 * BLOCK):
            there = pl.ds(pl.multiple_of(starts_ref[s] + place, BLOCK), size)
            here, spot = pl.ds(place, size), pl.ds(base + place, size)
            number = len(pieces)
            target = sum_ref.at[spot, :] if leaves else outs[s].at[here, :]
            copies = [
                pltpu.make_async_copy(tokens_ref.at[:, there], held_ref.at[:, spot], sems.at[number, 0]),
                pltpu.make_async_copy(error_ref.at[there, :], target, sems.at[number, 1]),
            ]
            for copy in copies:
                copy.start()
            pieces.append((s, there, here, spot, target, copies))
        base += count
    scale = lax.rsqrt(squares_ref[...] / depth + epsilon)[:, :1]
    written = []
    for s, there, here, spot, target, copies in pieces:
        gain = gain_ref[:, there].astype(jnp.float32)
        copies[0].wait()
        normed = (held_ref[:, spot].astype(jnp.float32) * scale * gain).astype(jnp.bfloat16)
        change = lax.dot_general(
            normed, grad_ref[...], (((0,), (0,)), ((), ())), preferred_element_type=jnp.float32
        )
        copies[1].wait()
        target[...] = change + target[...]
        away = outs[s].at[here, :] if leaves else whole_ref.at[spot, :]
        written.append(pltpu.make_async_copy(target, away, out_sems.at[len(written)]))
        written[-1].start()
    for copy in written:
        copy.wait()


def merge(leaves, starts, counts, depth, tokens, square_sums, gain, grad, error, after=()):
    rows, width = sum(counts), grad.shape[1]
    pieces = sum(len(pieces_of(count, 4 * BLOCK)) for count in counts)
    if leaves:
        shapes = [pltpu.HBM((count, width), jnp.float32) for count in counts]
        places = [pltpu.HBM] * len(counts)
        scratch = [pltpu.VMEM((rows, width), jnp.float32)]
    else:
        shapes = [near_shape((count, width)) for count in counts]
        shapes.append(pltpu.HBM((rows, width), jnp.float32))
        places = [*[pltpu.VMEM] * len(counts), pltpu.HBM]
        scratch = []
    return kernel_call(
        functools.partial(merge_kernel, counts, leaves, depth),
        out_shape=tuple(shapes),
        in_specs=specs(
            pltpu.SMEM, pltpu.HBM, *[pltpu.VMEM] * 3, pltpu.HBM, *[pl.ANY] * len(after)
        ),
        out_specs=tuple(specs(*places)),
        scratch_shapes=[
            *scratch,
            pltpu.VMEM((tokens.shape[0], rows), tokens.dtype),
            pltpu.SemaphoreType.DMA((pieces, 2)),
            pltpu.SemaphoreType.DMA((pieces,)),
        ],
        cost_estimate=pl.CostEstimate(
            flops=2 * rows * width * tokens.shape[0],
            bytes_accessed=8 * rows * width + 2 * tokens.shape[0] * rows,
            transcendentals=0,
        ),
    )(
        jnp.stack(starts).astype(jnp.int32),
        distant(tokens),
        *near(square_sums, gain, grad),
        distant(error),
        *after,
    )


def sides_of(side, half):
    return pl.ds(pl.multiple_of(side * half, 8), half), pl.ds(pl.multiple_of((1 - side) * half, 8), half)


def join_kernel(count, side_ref, own_ref, got_ref, *refs):
    keep_ref, send_ref = refs[-2:]
    stays, goes = sides_of(side_ref[0], count // 2)
    send_ref[...] = own_ref[goes, :] + got_ref[goes, :]
    keep_ref[...] = own_ref[stays, :] + got_ref[stays, :]


def last_kernel(own_ref, got_ref, *refs):
    refs[-1][...] = own_ref[...] + got_ref[...]


def join(own, got, side, after, held):
    count, width = own.shape
    arrays, places = near(own, got), [pltpu.VMEM] * 2
    if side is None:
        kernel, shapes = last_kernel, (near_shape((count, width)),)
    else:
        kernel = functools.partial(join_kernel, count)
        shapes = (near_shape((count // 2, width)),) * 2
        arrays.insert(0, jnp.reshape(side, (1,)).astype(jnp.int32))
        places.insert(0, pltpu.SMEM)
    return kernel_call(
        kernel,
        out_shape=shapes,
        in_specs=specs(*places, *[pl.ANY] * len(after), *[pltpu.VMEM] * len(held)),
        out_specs=tuple(specs(*[pltpu.VMEM] * len(shapes))),
        cost_estimate=LIGHT,
    )(*arrays, *after, *near(*held))


def bundles(plan, step):
    bits = sorted({stream.back[step] for stream in plan})
    groups = [[s for s, stream in enumerate(plan) if stream.back[step] == bit] for bit in bits]
    where = {}
    for index, group in enumerate(groups):
        place = 0
        for s in group:
            where[s] = (index, place)
            place += plan[s].width << step
    return bits, groups, where


def bundle_shapes(plan, step, width):
    _, groups, _ = bundles(plan, step)
    return tuple(near_shape((sum(plan[s].width << step for s in group), width)) for group in groups)


def gather_kernel(plan, step, sides_ref, *refs):
    bits, groups, before = bundles(plan, step)
    _, later_groups, after = bundles(plan, step + 1)
    n = len(groups)
    own, got, out = refs[:n], refs[n : 2 * n], refs[-len(later_groups) :]
    for s, stream in enumerate(plan):
        source, from_row = before[s]
        target, to_row = after[s]
        bit = stream.back[step]
        place = stream.order.index(bit)
        outer = 1 << sum(stream.order.index(b) < place for b in stream.back[:step])
        inner = (stream.width << step) // outer
        for i in range(outer):
            for refs_of, side in ((own, sides_ref[bit]), (got, 1 - sides_ref[bit])):
                row = pl.multiple_of(to_row + 2 * i * inner + side * inner, 8)
                out[target][pl.ds(row, inner), :] = refs_of[source][pl.ds(from_row + i * inner, inner), :]


def gather_step(plan, step, sides, own, got, after):
    shapes = bundle_shapes(plan, step + 1, own[0].shape[1])
    return kernel_call(
        functools.partial(gather_kernel, plan, step),
        out_shape=shapes,
        in_specs=specs(pltpu.SMEM, *[pltpu.VMEM] * (2 * len(own)), *[pl.ANY] * len(after)),
        out_specs=tuple(specs(*[pltpu.VMEM] * len(shapes))),
        cost_estimate=LIGHT,
    )(sides, *near(*own, *got), *after)


def packed_rows(width, share):
    blocks = width // BLOCK
    rows = (blocks * (blocks - 1) // 2 + (blocks + 1) // 2) * BLOCK + 8 * (blocks // 2)
    return -(-rows // share) * share


def block_grid():
    row = lax.broadcasted_iota(jnp.int32, (BLOCK, BLOCK), 0)
    column = lax.broadcasted_iota(jnp.int32, (BLOCK, BLOCK), 1)
    return row, column


def gram_kernel(replicas, *refs):
    out_ref = refs[-1]
    rows = jnp.concatenate([ref[...] for ref in refs[:-1]], 0) / replicas
    blocks = rows.shape[1] // BLOCK
    row, column = block_grid()
    place, diagonals = 0, []
    for a in range(blocks):
        left = rows[:, a * BLOCK : (a + 1) * BLOCK]
        band = contract(left, rows[:, a * BLOCK :], (0, 0))
        diagonals.append(band[:, :BLOCK])
        for b in range(1, blocks - a):
            out_ref[place : place + BLOCK, :] = band[:, b * BLOCK : (b + 1) * BLOCK]
            place += BLOCK
    for a in range(0, blocks, 2):
        both = diagonals[a]
        if a + 1 < blocks:
            both = jnp.where(row <= column, both, diagonals[a + 1])
        out_ref[place : place + BLOCK, :] = both
        place += BLOCK
    for a in range(1, blocks, 2):
        line = jnp.sum(jnp.where(row == column, diagonals[a], 0.0), axis=0, keepdims=True)
        out_ref[place : place + 8, :] = jnp.broadcast_to(line, (8, BLOCK))
        place += 8
    if place < out_ref.shape[0]:
        out_ref[place:, :] = jnp.zeros((out_ref.shape[0] - place, BLOCK), jnp.float32)


def gram(parts, replicas, share):
    rows = packed_rows(parts[0].shape[1], share)
    return kernel_call(
        functools.partial(gram_kernel, replicas),
        out_shape=near_shape((rows, BLOCK)),
        in_specs=specs(*[pltpu.VMEM] * len(parts)),
        out_specs=specs(pltpu.VMEM)[0],
    )(*near(*parts))


def unpack(packed_ref, whole_ref):
    blocks = whole_ref.shape[0] // BLOCK
    row, column = block_grid()
    place = 0

    def put(a, b, tile):
        whole_ref[a * BLOCK : (a + 1) * BLOCK, b * BLOCK : (b + 1) * BLOCK] = tile

    for a in range(blocks):
        for b in range(a + 1, blocks):
            tile = packed_ref[place : place + BLOCK, :]
            put(a, b, tile)
            put(b, a, tile.T)
            place += BLOCK
    line_place = place + (blocks + 1) // 2 * BLOCK
    for a in range(0, blocks, 2):
        tile = packed_ref[place : place + BLOCK, :]
        turned = tile.T
        place += BLOCK
        put(a, a, jnp.where(row <= column, tile, turned))
        if a + 1 < blocks:
            line = packed_ref[line_place : line_place + 1, :]
            line_place += 8
            put(a + 1, a + 1, jnp.where(row > column, tile, jnp.where(row < column, turned, line)))


def factor(matrix):
    size = matrix.shape[0]
    group = 8
    lane = lax.broadcasted_iota(jnp.int32, (size, size), 1)
    row = lax.broadcasted_iota(jnp.int32, (size, size), 0)
    done = []
    live = matrix
    for start in range(0, size, group):
        if start:
            done.append(live[:group])
            live = live[group:]
        count = size - start
        lanes, rows = lane[start:], row[start:]
        columns = [
            jnp.broadcast_to(live[:, start + t : start + t + 1], (count, size)) for t in range(group)
        ]
        for t in range(group):
            pivot = start + t
            inverse = 1.0 / columns[t][t : t + 1, :]
            below = rows > pivot
            scale = jnp.where(below, columns[t] * inverse, 0.0)
            own = jnp.where(lanes[t : t + 1] == pivot, 1.0, live[t : t + 1, :])
            live = jnp.where(below & (lanes == pivot), 0.0, live) - scale * own
            for s in range(t + 1, group):
                columns[s] = columns[s] - scale * columns[s][t : t + 1, :]
    done.append(live)
    result = jnp.concatenate(done, 0)
    diagonal = jnp.sum(jnp.where(lane == row, result, 0.0), axis=1, keepdims=True)
    unit = jnp.where(lane < row, result, jnp.where(lane == row, 1.0, 0.0))
    return unit, diagonal


def first_kernel(plan, replicas, packed_ref, basis_ref, *refs):
    whole_ref, right_ref = refs[len(plan) : len(plan) + 2]
    unpack(packed_ref, whole_ref)
    basis = basis_ref[...]
    plain = contract(whole_ref[...], basis, (1, 0))
    unit, diagonal = factor(contract(basis, plain, (0, 0)))
    right = contract(plain, unit * lax.rsqrt(diagonal), (1, 1))
    right_ref[...] = right
    _, groups, _ = bundles(plan, 0)
    for group, left_ref in zip(groups, refs[len(plan) + 2 :]):
        rows = jnp.concatenate([refs[s][...] for s in group], 0) / replicas
        left_ref[...] = contract(rows, right, (1, 0))


def first_pass(plan, packed, basis, parts, replicas):
    width, rank = basis.shape
    shapes = (near_shape((width, width)), near_shape((width, rank)), *bundle_shapes(plan, 0, rank))
    whole, right, *lefts = kernel_call(
        functools.partial(first_kernel, plan, replicas),
        out_shape=shapes,
        in_specs=specs(*[pltpu.VMEM] * (2 + len(parts))),
        out_specs=tuple(specs(*[pltpu.VMEM] * len(shapes))),
    )(*near(packed, basis, *parts))
    return whole, right, lefts


def product_kernel(whole_ref, right_ref, plain_ref, gram_ref):
    right = right_ref[...]
    plain = contract(whole_ref[...], right, (1, 0))
    plain_ref[...] = plain
    gram_ref[...] = contract(right, plain, (0, 0))


def weight_kernel(plain_ref, gram_ref, high_ref, low_ref):
    unit, diagonal = factor(gram_ref[...])
    inverse = unit * lax.rsqrt(diagonal)
    turned = contract(inverse, plain_ref[...], (1, 1))
    high_ref[...], low_ref[...] = split(contract(inverse, turned, (0, 0)))


def second_pass(whole, right):
    width, rank = right.shape
    pair = functools.partial(
        kernel_call,
        in_specs=specs(pltpu.VMEM, pltpu.VMEM),
        out_specs=tuple(specs(pltpu.VMEM, pltpu.VMEM)),
    )
    plain, gram_matrix = pair(
        product_kernel, out_shape=(near_shape((width, rank)), near_shape((rank, rank)))
    )(*near(whole, right))
    half = near_shape((rank, width), jnp.bfloat16)
    return pair(weight_kernel, out_shape=(half, half))(*near(plain, gram_matrix))


def low_rank(left, high, low):
    left_high, left_low = split(left)
    dot = functools.partial(jnp.dot, preferred_element_type=jnp.float32)
    both = jnp.concatenate([left_high, left_low], 1)
    return dot(both, jnp.concatenate([high, high], 0)) + dot(left_high, low)


def error_pieces(plan, replicas):
    pieces, base = [], 0
    for s, stream in enumerate(plan):
        count = stream.width * replicas // 2
        pieces += [(s, place, base + place, size) for place, size in pieces_of(count, 4 * BLOCK)]
        base += count
    return pieces


def write_errors(plan, replicas, starts_ref, high, low, merged, lefts, out_ref, held_ref, sems, fetched):
    _, _, where = bundles(plan, bit_count(replicas) - 1)
    written = []
    for number, (s, place, spot, size) in enumerate(error_pieces(plan, replicas)):
        index, first = where[s]
        there = pl.ds(pl.multiple_of(starts_ref[s] + place, BLOCK), size)
        here = pl.ds(spot, size)
        change = low_rank(lefts[index][pl.ds(first + place, size), :], high, low)
        if fetched:
            fetched[number].wait()
        held_ref[here, :] = merged[here, :] - change
        written.append(
            pltpu.make_async_copy(held_ref.at[here, :], out_ref.at[there, :], sems.at[number])
        )
        written[-1].start()
    return written


def error_kernel(plan, replicas, starts_ref, high_ref, low_ref, own_ref, *refs):
    n = len(plan)
    out_ref, near_ref, held_ref, fetch_sems, sems, near_sems = refs[-6:]
    fetched = []
    for number, (_, _, spot, size) in enumerate(error_pieces(plan, replicas)):
        here = pl.ds(spot, size)
        fetched.append(
            pltpu.make_async_copy(own_ref.at[here, :], held_ref.at[here, :], fetch_sems.at[number])
        )
        fetched[-1].start()
    others, base = [], 0
    for s, stream in enumerate(plan):
        count = stream.width * replicas // 2
        others.append(
            pltpu.make_async_copy(refs[s], near_ref.at[pl.ds(base, count), :], near_sems.at[s])
        )
        others[-1].start()
        base += count
    written = write_errors(
        plan, replicas, starts_ref, high_ref[...], low_ref[...], held_ref, refs[n:-6], out_ref, held_ref,
        sems, fetched,
    )
    for copy in written + others:
        copy.wait()


def last_error_kernel(plan, replicas, starts_ref, high_ref, low_ref, merged_ref, *refs):
    n = len(plan)
    _, groups, where = bundles(plan, bit_count(replicas) - 1)
    m = len(groups)
    others, lefts = refs[:m], refs[m : 2 * m]
    weights_ref, momentum_ref = refs[2 * m : 2 * m + 2]
    out_ref, weights_out, momentum_out, held_ref, left_ref, sems = refs[-6:]
    high, low = high_ref[...], low_ref[...]
    written = write_errors(
        plan, replicas, starts_ref, high, low, merged_ref, others, out_ref, held_ref, sems, None
    )
    rows = left_ref.shape[0]
    size = min(BLOCK, rows)
    for place in range(0, rows, size):
        want = starts_ref[2 * n] + place
        for k, bundle in ((0, others), (n, lefts)):
            for s, stream in enumerate(plan):
                index, first = where[s]
                skip = want - starts_ref[k + s]

                @pl.when((skip >= 0) & (skip < stream.width * replicas // 2))
                def _(bundle=bundle, index=index, first=first, skip=skip, place=place):
                    row = pl.multiple_of(first + skip, 8)
                    left_ref[place : place + size, :] = bundle[index][pl.ds(row, size), :]

    own_rows = low_rank(left_ref[...], high, low)
    momentum = momentum_rate * momentum_ref[...] + own_rows
    momentum_out[...] = momentum
    weights_out[...] = weights_ref[...] - outer_rate * (own_rows + momentum_rate * momentum)
    for copy in written:
        copy.wait()


def error_options(plan, replicas, width, rank):
    pieces = error_pieces(plan, replicas)
    rows = sum(piece[3] for piece in pieces)
    scratch = pltpu.VMEM((rows, width), jnp.float32), pltpu.SemaphoreType.DMA((len(pieces),))
    cost = pl.CostEstimate(
        flops=6 * rows * width * rank, bytes_accessed=8 * rows * width, transcendentals=0
    )
    return scratch, cost


def error_rows(plan, replicas, starts, own, far, lefts, high, low, shape):
    scratch, cost = error_options(plan, replicas, shape[1], high.shape[0])
    return kernel_call(
        functools.partial(error_kernel, plan, replicas),
        out_shape=(jax.ShapeDtypeStruct(shape, jnp.float32), near_shape(own.shape)),
        in_specs=specs(
            pltpu.SMEM, *[pltpu.VMEM] * 2, *[pltpu.HBM] * (1 + len(far)), *[pltpu.VMEM] * len(lefts)
        ),
        out_specs=tuple(specs(pltpu.HBM, pltpu.VMEM)),
        scratch_shapes=[*scratch, scratch[1], pltpu.SemaphoreType.DMA((len(far),))],
        cost_estimate=cost,
    )(
        jnp.stack(starts).astype(jnp.int32), *near(high, low), distant(own), *map(distant, far), *near(*lefts)
    )


def last_rows(plan, replicas, kept, starts, merged, others, lefts, high, low, weights, momentum):
    rows, width = weights.shape
    (held, sems), cost = error_options(plan, replicas, width, high.shape[0])
    arrays = [
        jnp.stack([*starts, lax.axis_index("rep") * rows]).astype(jnp.int32),
        *near(high, low, merged, *others, *lefts),
        weights,
        momentum,
        kept,
    ]
    result = jax.ShapeDtypeStruct(weights.shape, jnp.float32)
    return kernel_call(
        functools.partial(last_error_kernel, plan, replicas),
        out_shape=(jax.ShapeDtypeStruct(kept.shape, jnp.float32), result, result),
        in_specs=specs(pltpu.SMEM, *[pltpu.VMEM] * (2 * len(lefts) + 5), pltpu.HBM),
        out_specs=tuple(specs(pltpu.HBM, pltpu.VMEM, pltpu.VMEM)),
        scratch_shapes=[held, pltpu.VMEM((rows, high.shape[0]), jnp.float32), sems],
        input_output_aliases={len(arrays) - 1: 0},
        cost_estimate=cost,
    )(*arrays)


@dataclasses.dataclass(frozen=True)
class Stream:
    width: int
    order: tuple
    back: tuple


def stream_plan(replicas, rows_each):
    bits = bit_count(replicas)
    grain = max(8, 2 * BLOCK // replicas)
    units = rows_each // grain
    if bits == 4 and units % 16 == 0:
        shares = SHARES
        plan = [
            Stream(share * units // 16 * grain, order, BACK[order[0]])
            for share, order in shares
        ]
        return plan, TURNS, ARRIVALS
    streams = max(1, min(3, units, bits - 1))
    widths = [units // streams + (1 if s < units % streams else 0) for s in range(streams)]
    lead = list(range(min(3, bits)))
    rest = list(range(len(lead), bits))
    orders = [tuple(lead[s % len(lead) :] + lead[: s % len(lead)] + rest) for s in range(streams)]
    plan = [Stream(w * grain, order, order[::-1]) for w, order in zip(widths, orders)]
    return plan, range(streams), [s for _ in range(bits) for s in range(streams)]


def on_device(tokens_in, norm_gain, key_grad, error_in, basis_init, weights_in, momentum_in):
    replicas = lax.axis_size("rep")
    steps = bit_count(replicas)
    depth = tokens_in.shape[1]
    error = error_in[0]
    square_sums = sum_over(squares(tokens_in), "mp")
    basis = lax.all_gather(basis_init, "mp", axis=0, tiled=True)
    sources = (
        depth * lax.axis_size("mp"), tokens_in, square_sums, norm_gain[None, :], key_grad, error
    )

    plan, turns, arrivals = stream_plan(replicas, depth // replicas)
    halves, here, there, place = [], [], [], 0
    for stream in plan:
        half = stream.width * replicas // 2
        side = bit_of("rep", stream.order[0])
        halves.append(half)
        here.append(place + side * half)
        there.append(place + (1 - side) * half)
        place += 2 * half
    far = merge(True, there, halves, *sources)
    got = [flip(part, "rep", 1 << stream.order[0]) for part, stream in zip(far, plan)]
    *own, own_kept = merge(False, here, halves, *sources, after=[basis])
    parts, after, done = list(own), [], [0] * len(plan)
    for s in arrivals:
        done[s] += 1
        came = got[s]
        if done[s] < steps:
            bit = plan[s].order[done[s]]
            parts[s], send = join(parts[s], came, bit_of("rep", bit), after, [p for k, p in enumerate(parts) if k != s])
            got[s] = flip(send, "rep", 1 << bit)
        else:
            (parts[s],) = join(parts[s], came, None, after, [])
        after = [came]

    packed = sum_everywhere(gram(parts, replicas, 32 * lax.axis_size("mp")))
    whole, right, lefts = first_pass(plan, packed, basis, parts, replicas)
    high, low = second_pass(whole, right)

    bit_sides = jnp.stack([bit_of("rep", bit) for bit in range(steps)]).astype(jnp.int32)
    for step in range(steps):
        bits, _, _ = bundles(plan, step)
        others = [flip(left, "rep", 1 << bit) for left, bit in zip(lefts, bits)]
        if step + 1 < steps:
            lefts = gather_step(plan, step, bit_sides, lefts, others, [high])

    error_out, far_near = error_rows(
        plan, replicas, here, own_kept, far, lefts, high, low, error.shape
    )
    error_out, weights_out, momentum_out = last_rows(
        plan, replicas, error_out, there + here, far_near, others, lefts, high, low, weights_in[0],
        momentum_in[0],
    )
    return (error_out[None], weights_out[None], momentum_out[None])


def solution(mesh):
    in_specs = (
        P("rep", "mp"),
        P("mp"),
        P("rep", None),
        P("rep", "mp", None),
        P("mp", None),
        P("mp", "rep", None),
        P("mp", "rep", None),
    )
    out_specs = (P("rep", "mp", None), P("mp", "rep", None), P("mp", "rep", None))
    return jax.shard_map(
        on_device, mesh=mesh, in_specs=in_specs, out_specs=out_specs, check_vma=False
    )
```

```python
import dataclasses
import functools

import jax
import jax.numpy as jnp
from jax import lax
from jax.experimental import pallas as pl
from jax.experimental.pallas import tpu as pltpu
from jax.sharding import PartitionSpec as P

BLOCK = 128

SHARES = (
    (3, (0, 2, 3, 1)),
    (4, (2, 0, 1, 3)),
    (3, (0, 1, 3, 2)),
    (3, (1, 2, 0, 3)),
    (3, (1, 3, 0, 2)),
)
BACK = {0: (3, 2, 1, 0), 1: (3, 0, 2, 1), 2: (3, 1, 0, 2)}
ARRIVALS = (0, 4, 1, 2, 3, 0, 4, 1, 2, 4, 0, 3, 1, 0, 2, 3, 4, 1, 2, 3)
TURNS = (0, 4, 2, 1, 3)

precise = lax.Precision.HIGHEST
epsilon = 1e-05
momentum_rate = 0.9
outer_rate = 0.7


def contract(first, second, dims, precision=precise):
    return lax.dot_general(
        first,
        second,
        ((dims[:1], dims[1:]), ((), ())),
        precision=precision,
        preferred_element_type=jnp.float32,
    )


def flip(value, axis, mask):
    size = lax.axis_size(axis)
    return lax.ppermute(value, axis, [(i, i ^ mask) for i in range(size)])


def bit_of(axis, bit):
    return (lax.axis_index(axis) >> bit) & 1


def rows_of(value, start, count):
    return lax.dynamic_slice_in_dim(value, start, count, 0)


def halve(value, axis, bit):
    half = value.shape[0] // 2
    side = bit_of(axis, bit)
    sent = rows_of(value, (1 - side) * half, half)
    return rows_of(value, side * half, half) + flip(sent, axis, 1 << bit)


def double(value, axis, bit):
    other = flip(value, axis, 1 << bit)
    side = bit_of(axis, bit)
    both = jnp.concatenate([value, value], 0)
    return lax.dynamic_update_slice_in_dim(both, other, (1 - side) * value.shape[0], 0)


def bit_count(size):
    return size.bit_length() - 1


def sum_over(value, axis):
    for bit in range(bit_count(lax.axis_size(axis))):
        value = value + flip(value, axis, 1 << bit)
    return value


def sum_everywhere(value):
    rep_bits = bit_count(lax.axis_size("rep"))
    mp_bits = bit_count(lax.axis_size("mp"))
    for bit in range(mp_bits):
        value = halve(value, "mp", bit)
    place = lax.axis_index("rep") & 3
    part = value.shape[0] // 4
    pieces = [rows_of(value, (place ^ m) * part, part) for m in range(4)]
    got = [flip(pieces[m], "rep", m) for m in (1, 2, 3)]
    value = (pieces[0] + got[0]) + (got[1] + got[2])
    bit = 2
    while bit < rep_bits:
        if bit + 1 < rep_bits:
            got = [flip(value, "rep", m << bit) for m in (1, 2, 3)]
            value = (value + got[0]) + (got[1] + got[2])
            bit += 2
        else:
            value = value + flip(value, "rep", 1 << bit)
            bit += 1
    got = [value] + [flip(value, "rep", m) for m in (1, 2, 3)]
    whole = jnp.zeros((4 * part,) + value.shape[1:], value.dtype)
    for m in range(4):
        whole = lax.dynamic_update_slice_in_dim(whole, got[m], (place ^ m) * part, 0)
    for bit in reversed(range(mp_bits)):
        whole = double(whole, "mp", bit)
    return whole


LIGHT = pl.CostEstimate(flops=1, bytes_accessed=1, transcendentals=0)


def kernel_call(*args, **options):
    return pl.pallas_call(
        *args, compiler_params=pltpu.CompilerParams(vmem_limit_bytes=10 * 2**20), **options
    )


def near(*arrays):
    return [pltpu.with_memory_space_constraint(array, pltpu.VMEM) for array in arrays]


def distant(array):
    return pltpu.with_memory_space_constraint(array, pltpu.HBM)


def near_shape(shape, dtype=jnp.float32):
    return pltpu.VMEM(shape, dtype)


def specs(*places):
    return [pl.BlockSpec(memory_space=place) for place in places]


def pieces_of(count, most):
    cuts, place = [], 0
    while place < count:
        size = min(most, count - place)
        cuts.append((place, size))
        place += size
    return cuts


def split(value):
    high = value.astype(jnp.bfloat16)
    return high, (value - high.astype(jnp.float32)).astype(jnp.bfloat16)


def squares_kernel(cuts, tokens_ref, grad_ref, out_ref, near_ref, held_ref, sems):
    copies = []
    for index, (start, size) in enumerate(cuts):
        at = pl.ds(start, size)
        copies.append(
            pltpu.make_async_copy(tokens_ref.at[:, at], held_ref.at[:, at], sems.at[index])
        )
        copies[-1].start()
    near_copy = pltpu.make_async_copy(grad_ref, near_ref, sems.at[len(cuts)])
    near_copy.start()
    total = None
    for copy, (start, size) in zip(copies, cuts):
        copy.wait()
        for place in range(start, start + size, BLOCK):
            wide = held_ref[:, place : place + BLOCK].astype(jnp.float32)
            total = wide * wide if total is None else total + wide * wide
    out_ref[...] = jnp.broadcast_to(jnp.sum(total, axis=1, keepdims=True), out_ref.shape)
    near_copy.wait()


def squares(tokens, grad):
    cuts = pieces_of(tokens.shape[1], max(BLOCK, tokens.shape[1] // 4))
    return kernel_call(
        functools.partial(squares_kernel, cuts),
        out_shape=(near_shape((tokens.shape[0], BLOCK)), near_shape(grad.shape, grad.dtype)),
        in_specs=specs(pltpu.HBM, pltpu.HBM),
        out_specs=tuple(specs(pltpu.VMEM, pltpu.VMEM)),
        scratch_shapes=[
            pltpu.VMEM(tokens.shape, tokens.dtype),
            pltpu.SemaphoreType.DMA((len(cuts) + 1,)),
        ],
    )(distant(tokens), distant(grad))


def merge_kernel(
    counts, leaves, depth, starts_ref, tokens_ref, squares_ref, gain_ref, grad_ref, error_ref, *refs
):
    n = len(counts)
    *refs, held_ref, sems, out_sems = refs
    if leaves:
        *outs, sum_ref = refs
    else:
        outs, whole_ref = refs[-n - 1 : -1], refs[-1]
    pieces, base = [], 0
    for s, count in enumerate(counts):
        for place, size in pieces_of(count, 4 * BLOCK):
            there = pl.ds(pl.multiple_of(starts_ref[s] + place, BLOCK), size)
            here, spot = pl.ds(place, size), pl.ds(base + place, size)
            number = len(pieces)
            target = sum_ref.at[spot, :] if leaves else outs[s].at[here, :]
            copies = [
                pltpu.make_async_copy(tokens_ref.at[:, there], held_ref.at[:, spot], sems.at[number, 0]),
                pltpu.make_async_copy(error_ref.at[there, :], target, sems.at[number, 1]),
            ]
            for copy in copies:
                copy.start()
            pieces.append((s, there, here, spot, target, copies))
        base += count
    scale = lax.rsqrt(squares_ref[...] / depth + epsilon)[:, :1]
    written = []
    for s, there, here, spot, target, copies in pieces:
        gain = gain_ref[:, there].astype(jnp.float32)
        copies[0].wait()
        normed = (held_ref[:, spot].astype(jnp.float32) * scale * gain).astype(jnp.bfloat16)
        change = lax.dot_general(
            normed, grad_ref[...], (((0,), (0,)), ((), ())), preferred_element_type=jnp.float32
        )
        copies[1].wait()
        target[...] = change + target[...]
        away = outs[s].at[here, :] if leaves else whole_ref.at[spot, :]
        written.append(pltpu.make_async_copy(target, away, out_sems.at[len(written)]))
        written[-1].start()
    for copy in written:
        copy.wait()


def merge(leaves, starts, counts, depth, tokens, square_sums, gain, grad, error, after=()):
    rows, width = sum(counts), grad.shape[1]
    pieces = sum(len(pieces_of(count, 4 * BLOCK)) for count in counts)
    if leaves:
        shapes = [pltpu.HBM((count, width), jnp.float32) for count in counts]
        places = [pltpu.HBM] * len(counts)
        scratch = [pltpu.VMEM((rows, width), jnp.float32)]
    else:
        shapes = [near_shape((count, width)) for count in counts]
        shapes.append(pltpu.HBM((rows, width), jnp.float32))
        places = [*[pltpu.VMEM] * len(counts), pltpu.HBM]
        scratch = []
    return kernel_call(
        functools.partial(merge_kernel, counts, leaves, depth),
        out_shape=tuple(shapes),
        in_specs=specs(
            pltpu.SMEM, pltpu.HBM, *[pltpu.VMEM] * 3, pltpu.HBM, *[pl.ANY] * len(after)
        ),
        out_specs=tuple(specs(*places)),
        scratch_shapes=[
            *scratch,
            pltpu.VMEM((tokens.shape[0], rows), tokens.dtype),
            pltpu.SemaphoreType.DMA((pieces, 2)),
            pltpu.SemaphoreType.DMA((pieces,)),
        ],
        cost_estimate=pl.CostEstimate(
            flops=2 * rows * width * tokens.shape[0],
            bytes_accessed=8 * rows * width + 2 * tokens.shape[0] * rows,
            transcendentals=0,
        ),
    )(
        jnp.stack(starts).astype(jnp.int32),
        distant(tokens),
        *near(square_sums, gain, grad),
        distant(error),
        *after,
    )


def sides_of(side, half):
    return pl.ds(pl.multiple_of(side * half, 8), half), pl.ds(pl.multiple_of((1 - side) * half, 8), half)


def join_kernel(count, side_ref, own_ref, got_ref, *refs):
    keep_ref, send_ref = refs[-2:]
    stays, goes = sides_of(side_ref[0], count // 2)
    send_ref[...] = own_ref[goes, :] + got_ref[goes, :]
    keep_ref[...] = own_ref[stays, :] + got_ref[stays, :]


def last_kernel(own_ref, got_ref, *refs):
    refs[-1][...] = own_ref[...] + got_ref[...]


def join(own, got, side, after, held):
    count, width = own.shape
    arrays, places = near(own, got), [pltpu.VMEM] * 2
    if side is None:
        kernel, shapes = last_kernel, (near_shape((count, width)),)
    else:
        kernel = functools.partial(join_kernel, count)
        shapes = (near_shape((count // 2, width)),) * 2
        arrays.insert(0, jnp.reshape(side, (1,)).astype(jnp.int32))
        places.insert(0, pltpu.SMEM)
    return kernel_call(
        kernel,
        out_shape=shapes,
        in_specs=specs(*places, *[pl.ANY] * len(after), *[pltpu.VMEM] * len(held)),
        out_specs=tuple(specs(*[pltpu.VMEM] * len(shapes))),
        cost_estimate=LIGHT,
    )(*arrays, *after, *near(*held))


def bundles(plan, step):
    bits = sorted({stream.back[step] for stream in plan})
    groups = [[s for s, stream in enumerate(plan) if stream.back[step] == bit] for bit in bits]
    where = {}
    for index, group in enumerate(groups):
        place = 0
        for s in group:
            where[s] = (index, place)
            place += plan[s].width << step
    return bits, groups, where


def bundle_shapes(plan, step, width):
    _, groups, _ = bundles(plan, step)
    return tuple(near_shape((sum(plan[s].width << step for s in group), width)) for group in groups)


def gather_kernel(plan, step, sides_ref, *refs):
    bits, groups, before = bundles(plan, step)
    _, later_groups, after = bundles(plan, step + 1)
    n = len(groups)
    own, got, out = refs[:n], refs[n : 2 * n], refs[-len(later_groups) :]
    for s, stream in enumerate(plan):
        source, from_row = before[s]
        target, to_row = after[s]
        bit = stream.back[step]
        place = stream.order.index(bit)
        outer = 1 << sum(stream.order.index(b) < place for b in stream.back[:step])
        inner = (stream.width << step) // outer
        for i in range(outer):
            for refs_of, side in ((own, sides_ref[bit]), (got, 1 - sides_ref[bit])):
                row = pl.multiple_of(to_row + 2 * i * inner + side * inner, 8)
                out[target][pl.ds(row, inner), :] = refs_of[source][pl.ds(from_row + i * inner, inner), :]


def gather_step(plan, step, sides, own, got, after):
    shapes = bundle_shapes(plan, step + 1, own[0].shape[1])
    return kernel_call(
        functools.partial(gather_kernel, plan, step),
        out_shape=shapes,
        in_specs=specs(pltpu.SMEM, *[pltpu.VMEM] * (2 * len(own)), *[pl.ANY] * len(after)),
        out_specs=tuple(specs(*[pltpu.VMEM] * len(shapes))),
        cost_estimate=LIGHT,
    )(sides, *near(*own, *got), *after)


def packed_rows(width, share):
    blocks = width // BLOCK
    rows = (blocks * (blocks - 1) // 2 + (blocks + 1) // 2) * BLOCK + 8 * (blocks // 2)
    return -(-rows // share) * share


def block_grid():
    row = lax.broadcasted_iota(jnp.int32, (BLOCK, BLOCK), 0)
    column = lax.broadcasted_iota(jnp.int32, (BLOCK, BLOCK), 1)
    return row, column


def gram_kernel(replicas, *refs):
    out_ref = refs[-1]
    rows = jnp.concatenate([ref[...] for ref in refs[:-1]], 0) / replicas
    blocks = rows.shape[1] // BLOCK
    row, column = block_grid()
    place, diagonals = 0, []
    for a in range(blocks):
        left = rows[:, a * BLOCK : (a + 1) * BLOCK]
        band = contract(left, rows[:, a * BLOCK :], (0, 0))
        diagonals.append(band[:, :BLOCK])
        for b in range(1, blocks - a):
            out_ref[place : place + BLOCK, :] = band[:, b * BLOCK : (b + 1) * BLOCK]
            place += BLOCK
    for a in range(0, blocks, 2):
        both = diagonals[a]
        if a + 1 < blocks:
            both = jnp.where(row <= column, both, diagonals[a + 1])
        out_ref[place : place + BLOCK, :] = both
        place += BLOCK
    for a in range(1, blocks, 2):
        line = jnp.sum(jnp.where(row == column, diagonals[a], 0.0), axis=0, keepdims=True)
        out_ref[place : place + 8, :] = jnp.broadcast_to(line, (8, BLOCK))
        place += 8
    if place < out_ref.shape[0]:
        out_ref[place:, :] = jnp.zeros((out_ref.shape[0] - place, BLOCK), jnp.float32)


def gram(parts, replicas, share):
    rows = packed_rows(parts[0].shape[1], share)
    return kernel_call(
        functools.partial(gram_kernel, replicas),
        out_shape=near_shape((rows, BLOCK)),
        in_specs=specs(*[pltpu.VMEM] * len(parts)),
        out_specs=specs(pltpu.VMEM)[0],
    )(*near(*parts))


def unpack(packed_ref, whole_ref):
    blocks = whole_ref.shape[0] // BLOCK
    row, column = block_grid()
    place = 0

    def put(a, b, tile):
        whole_ref[a * BLOCK : (a + 1) * BLOCK, b * BLOCK : (b + 1) * BLOCK] = tile

    for a in range(blocks):
        for b in range(a + 1, blocks):
            tile = packed_ref[place : place + BLOCK, :]
            put(a, b, tile)
            put(b, a, tile.T)
            place += BLOCK
    line_place = place + (blocks + 1) // 2 * BLOCK
    for a in range(0, blocks, 2):
        tile = packed_ref[place : place + BLOCK, :]
        turned = tile.T
        place += BLOCK
        put(a, a, jnp.where(row <= column, tile, turned))
        if a + 1 < blocks:
            line = packed_ref[line_place : line_place + 1, :]
            line_place += 8
            put(a + 1, a + 1, jnp.where(row > column, tile, jnp.where(row < column, turned, line)))


def factor(matrix):
    size = matrix.shape[0]
    group = 8
    lane = lax.broadcasted_iota(jnp.int32, (size, size), 1)
    row = lax.broadcasted_iota(jnp.int32, (size, size), 0)
    done = []
    live = matrix
    for start in range(0, size, group):
        if start:
            done.append(live[:group])
            live = live[group:]
        count = size - start
        lanes, rows = lane[start:], row[start:]
        columns = [
            jnp.broadcast_to(live[:, start + t : start + t + 1], (count, size)) for t in range(group)
        ]
        for t in range(group):
            pivot = start + t
            inverse = 1.0 / columns[t][t : t + 1, :]
            below = rows > pivot
            scale = jnp.where(below, columns[t] * inverse, 0.0)
            own = jnp.where(lanes[t : t + 1] == pivot, 1.0, live[t : t + 1, :])
            live = jnp.where(below & (lanes == pivot), 0.0, live) - scale * own
            for s in range(t + 1, group):
                columns[s] = columns[s] - scale * columns[s][t : t + 1, :]
    done.append(live)
    result = jnp.concatenate(done, 0)
    diagonal = jnp.sum(jnp.where(lane == row, result, 0.0), axis=1, keepdims=True)
    unit = jnp.where(lane < row, result, jnp.where(lane == row, 1.0, 0.0))
    return unit, diagonal


def first_kernel(plan, replicas, packed_ref, basis_ref, *refs):
    whole_ref, right_ref, gram_ref = refs[len(plan) : len(plan) + 3]
    unpack(packed_ref, whole_ref)
    basis = basis_ref[...]
    plain = contract(whole_ref[...], basis, (1, 0))
    gram_matrix = contract(basis, plain, (0, 0))
    row = lax.broadcasted_iota(jnp.int32, gram_matrix.shape, 0)
    column = lax.broadcasted_iota(jnp.int32, gram_matrix.shape, 1)
    diagonal = jnp.where(row == column, gram_matrix, 0.0)
    across = lax.rsqrt(jnp.sum(diagonal, axis=0, keepdims=True))
    gram_ref[...] = gram_matrix * across * lax.rsqrt(jnp.sum(diagonal, axis=1, keepdims=True))
    right = plain * across
    right_ref[...] = right
    _, groups, _ = bundles(plan, 0)
    for group, left_ref in zip(groups, refs[len(plan) + 3 :]):
        rows = jnp.concatenate([refs[s][...] for s in group], 0) / replicas
        left_ref[...] = contract(rows, right, (1, 0))


def first_pass(plan, packed, basis, parts, replicas):
    width, rank = basis.shape
    shapes = (
        near_shape((width, width)),
        near_shape((width, rank)),
        near_shape((rank, rank)),
        *bundle_shapes(plan, 0, rank),
    )
    whole, right, gram_matrix, *lefts = kernel_call(
        functools.partial(first_kernel, plan, replicas),
        out_shape=shapes,
        in_specs=specs(*[pltpu.VMEM] * (2 + len(parts))),
        out_specs=tuple(specs(*[pltpu.VMEM] * len(shapes))),
    )(*near(packed, basis, *parts))
    return whole, right, gram_matrix, lefts


def inverse_factor(matrix):
    unit, diagonal = factor(matrix)
    return unit * lax.rsqrt(diagonal)


def product_kernel(whole_ref, right_ref, gram_ref, inverse_ref, plain_ref, second_ref):
    inverse = inverse_factor(gram_ref[...])
    inverse_ref[...] = inverse
    right = contract(right_ref[...], inverse, (1, 1))
    plain = contract(whole_ref[...], right, (1, 0))
    plain_ref[...] = plain
    second_ref[...] = contract(right, plain, (0, 0))


def weight_kernel(first_ref, plain_ref, gram_ref, high_ref, low_ref):
    inverse = inverse_factor(gram_ref[...])
    turned = contract(inverse, plain_ref[...], (1, 1))
    weights = contract(first_ref[...], contract(inverse, turned, (0, 0)), (0, 0))
    high_ref[...], low_ref[...] = split(weights)


def second_pass(whole, right, gram_matrix):
    width, rank = right.shape
    square = near_shape((rank, rank))
    inverse, plain, second = kernel_call(
        product_kernel,
        out_shape=(square, near_shape((width, rank)), square),
        in_specs=specs(*[pltpu.VMEM] * 3),
        out_specs=tuple(specs(*[pltpu.VMEM] * 3)),
    )(*near(whole, right, gram_matrix))
    half = near_shape((rank, width), jnp.bfloat16)
    weights = kernel_call(
        weight_kernel,
        out_shape=(half, half),
        in_specs=specs(*[pltpu.VMEM] * 3),
        out_specs=tuple(specs(*[pltpu.VMEM] * 2)),
    )(*near(inverse, plain, second))
    return second, weights


def low_rank(left, high, low):
    left_high, left_low = split(left)
    dot = functools.partial(jnp.dot, preferred_element_type=jnp.float32)
    both = jnp.concatenate([left_high, left_low], 1)
    return dot(both, jnp.concatenate([high, high], 0)) + dot(left_high, low)


def error_pieces(plan, replicas):
    pieces, base = [], 0
    for s, stream in enumerate(plan):
        count = stream.width * replicas // 2
        pieces += [(s, place, base + place, size) for place, size in pieces_of(count, 4 * BLOCK)]
        base += count
    return pieces


def write_errors(plan, replicas, starts_ref, high, low, merged, lefts, out_ref, held_ref, sems, fetched):
    _, _, where = bundles(plan, bit_count(replicas) - 1)
    written = []
    for number, (s, place, spot, size) in enumerate(error_pieces(plan, replicas)):
        index, first = where[s]
        there = pl.ds(pl.multiple_of(starts_ref[s] + place, BLOCK), size)
        here = pl.ds(spot, size)
        change = low_rank(lefts[index][pl.ds(first + place, size), :], high, low)
        if fetched:
            fetched[number].wait()
        held_ref[here, :] = merged[here, :] - change
        written.append(
            pltpu.make_async_copy(held_ref.at[here, :], out_ref.at[there, :], sems.at[number])
        )
        written[-1].start()
    return written


def error_kernel(plan, replicas, starts_ref, high_ref, low_ref, own_ref, *refs):
    n = len(plan)
    out_ref, near_ref, held_ref, fetch_sems, sems, near_sems = refs[-6:]
    fetched = []
    for number, (_, _, spot, size) in enumerate(error_pieces(plan, replicas)):
        here = pl.ds(spot, size)
        fetched.append(
            pltpu.make_async_copy(own_ref.at[here, :], held_ref.at[here, :], fetch_sems.at[number])
        )
        fetched[-1].start()
    others, base = [], 0
    for s, stream in enumerate(plan):
        count = stream.width * replicas // 2
        others.append(
            pltpu.make_async_copy(refs[s], near_ref.at[pl.ds(base, count), :], near_sems.at[s])
        )
        others[-1].start()
        base += count
    written = write_errors(
        plan, replicas, starts_ref, high_ref[...], low_ref[...], held_ref, refs[n:-6], out_ref, held_ref,
        sems, fetched,
    )
    for copy in written + others:
        copy.wait()


def last_error_kernel(plan, replicas, starts_ref, high_ref, low_ref, merged_ref, *refs):
    n = len(plan)
    _, groups, where = bundles(plan, bit_count(replicas) - 1)
    m = len(groups)
    others, lefts = refs[:m], refs[m : 2 * m]
    weights_ref, momentum_ref = refs[2 * m : 2 * m + 2]
    out_ref, weights_out, momentum_out, held_ref, left_ref, sems = refs[-6:]
    high, low = high_ref[...], low_ref[...]
    written = write_errors(
        plan, replicas, starts_ref, high, low, merged_ref, others, out_ref, held_ref, sems, None
    )
    rows = left_ref.shape[0]
    size = min(BLOCK, rows)
    for place in range(0, rows, size):
        want = starts_ref[2 * n] + place
        for k, bundle in ((0, others), (n, lefts)):
            for s, stream in enumerate(plan):
                index, first = where[s]
                skip = want - starts_ref[k + s]

                @pl.when((skip >= 0) & (skip < stream.width * replicas // 2))
                def _(bundle=bundle, index=index, first=first, skip=skip, place=place):
                    row = pl.multiple_of(first + skip, 8)
                    left_ref[place : place + size, :] = bundle[index][pl.ds(row, size), :]

    own_rows = low_rank(left_ref[...], high, low)
    momentum = momentum_rate * momentum_ref[...] + own_rows
    momentum_out[...] = momentum
    weights_out[...] = weights_ref[...] - outer_rate * (own_rows + momentum_rate * momentum)
    for copy in written:
        copy.wait()


def error_options(plan, replicas, width, rank):
    pieces = error_pieces(plan, replicas)
    rows = sum(piece[3] for piece in pieces)
    scratch = pltpu.VMEM((rows, width), jnp.float32), pltpu.SemaphoreType.DMA((len(pieces),))
    cost = pl.CostEstimate(
        flops=6 * rows * width * rank, bytes_accessed=8 * rows * width, transcendentals=0
    )
    return scratch, cost


def error_rows(plan, replicas, starts, own, far, lefts, high, low, shape):
    scratch, cost = error_options(plan, replicas, shape[1], high.shape[0])
    return kernel_call(
        functools.partial(error_kernel, plan, replicas),
        out_shape=(jax.ShapeDtypeStruct(shape, jnp.float32), near_shape(own.shape)),
        in_specs=specs(
            pltpu.SMEM, *[pltpu.VMEM] * 2, *[pltpu.HBM] * (1 + len(far)), *[pltpu.VMEM] * len(lefts)
        ),
        out_specs=tuple(specs(pltpu.HBM, pltpu.VMEM)),
        scratch_shapes=[*scratch, scratch[1], pltpu.SemaphoreType.DMA((len(far),))],
        cost_estimate=cost,
    )(
        jnp.stack(starts).astype(jnp.int32), *near(high, low), distant(own), *map(distant, far), *near(*lefts)
    )


def last_rows(plan, replicas, kept, starts, merged, others, lefts, high, low, weights, momentum):
    rows, width = weights.shape
    (held, sems), cost = error_options(plan, replicas, width, high.shape[0])
    arrays = [
        jnp.stack([*starts, lax.axis_index("rep") * rows]).astype(jnp.int32),
        *near(high, low, merged, *others, *lefts),
        weights,
        momentum,
        kept,
    ]
    result = jax.ShapeDtypeStruct(weights.shape, jnp.float32)
    return kernel_call(
        functools.partial(last_error_kernel, plan, replicas),
        out_shape=(jax.ShapeDtypeStruct(kept.shape, jnp.float32), result, result),
        in_specs=specs(pltpu.SMEM, *[pltpu.VMEM] * (2 * len(lefts) + 5), pltpu.HBM),
        out_specs=tuple(specs(pltpu.HBM, pltpu.VMEM, pltpu.VMEM)),
        scratch_shapes=[held, pltpu.VMEM((rows, high.shape[0]), jnp.float32), sems],
        input_output_aliases={len(arrays) - 1: 0},
        cost_estimate=cost,
    )(*arrays)


@dataclasses.dataclass(frozen=True)
class Stream:
    width: int
    order: tuple
    back: tuple


def stream_plan(replicas, rows_each):
    bits = bit_count(replicas)
    grain = max(8, 2 * BLOCK // replicas)
    units = rows_each // grain
    if bits == 4 and units % 16 == 0:
        shares = SHARES
        plan = [
            Stream(share * units // 16 * grain, order, BACK[order[0]])
            for share, order in shares
        ]
        return plan, TURNS, ARRIVALS
    streams = max(1, min(3, units, bits - 1))
    widths = [units // streams + (1 if s < units % streams else 0) for s in range(streams)]
    lead = list(range(min(3, bits)))
    rest = list(range(len(lead), bits))
    orders = [tuple(lead[s % len(lead) :] + lead[: s % len(lead)] + rest) for s in range(streams)]
    plan = [Stream(w * grain, order, order[::-1]) for w, order in zip(widths, orders)]
    return plan, range(streams), [s for _ in range(bits) for s in range(streams)]


def on_device(tokens_in, norm_gain, key_grad, error_in, basis_init, weights_in, momentum_in):
    replicas = lax.axis_size("rep")
    steps = bit_count(replicas)
    depth = tokens_in.shape[1]
    error = error_in[0]
    square_sums, grad = squares(tokens_in, key_grad)
    square_sums = sum_over(square_sums, "mp")
    basis = lax.all_gather(basis_init, "mp", axis=0, tiled=True)
    sources = (
        depth * lax.axis_size("mp"), tokens_in, square_sums, norm_gain[None, :], grad, error
    )

    plan, turns, arrivals = stream_plan(replicas, depth // replicas)
    halves, here, there, place = [], [], [], 0
    for stream in plan:
        half = stream.width * replicas // 2
        side = bit_of("rep", stream.order[0])
        halves.append(half)
        here.append(place + side * half)
        there.append(place + (1 - side) * half)
        place += 2 * half
    far = merge(True, there, halves, *sources)
    got = [flip(part, "rep", 1 << stream.order[0]) for part, stream in zip(far, plan)]
    *own, own_kept = merge(False, here, halves, *sources, after=[basis])
    parts, after, done = list(own), [], [0] * len(plan)
    for s in arrivals:
        done[s] += 1
        came = got[s]
        if done[s] < steps:
            bit = plan[s].order[done[s]]
            parts[s], send = join(parts[s], came, bit_of("rep", bit), after, [p for k, p in enumerate(parts) if k != s])
            got[s] = flip(send, "rep", 1 << bit)
        else:
            (parts[s],) = join(parts[s], came, None, after, [])
        after = [came]

    packed = sum_everywhere(gram(parts, replicas, 32 * lax.axis_size("mp")))
    whole, right, gram_matrix, lefts = first_pass(plan, packed, basis, parts, replicas)
    second, (high, low) = second_pass(whole, right, gram_matrix)

    bit_sides = jnp.stack([bit_of("rep", bit) for bit in range(steps)]).astype(jnp.int32)
    for step in range(steps):
        bits, _, _ = bundles(plan, step)
        others = [flip(left, "rep", 1 << bit) for left, bit in zip(lefts, bits)]
        if step + 1 < steps:
            lefts = gather_step(plan, step, bit_sides, lefts, others, [high if step + 2 >= steps else second])

    error_out, far_near = error_rows(
        plan, replicas, here, own_kept, far, lefts, high, low, error.shape
    )
    error_out, weights_out, momentum_out = last_rows(
        plan, replicas, error_out, there + here, far_near, others, lefts, high, low, weights_in[0],
        momentum_in[0],
    )
    return (error_out[None], weights_out[None], momentum_out[None])


def solution(mesh):
    in_specs = (
        P("rep", "mp"),
        P("mp"),
        P("rep", None),
        P("rep", "mp", None),
        P("mp", None),
        P("mp", "rep", None),
        P("mp", "rep", None),
    )
    out_specs = (P("rep", "mp", None), P("mp", "rep", None), P("mp", "rep", None))
    return jax.shard_map(
        on_device, mesh=mesh, in_specs=in_specs, out_specs=out_specs, check_vma=False
    )
```

```python
import dataclasses
import functools

import jax
import jax.numpy as jnp
from jax import lax
from jax.experimental import pallas as pl
from jax.experimental.pallas import tpu as pltpu
from jax.sharding import PartitionSpec as P

BLOCK = 128

SHARES = (
    (3, (0, 2, 1, 3)),
    (4, (2, 0, 1, 3)),
    (3, (0, 1, 3, 2)),
    (3, (1, 2, 0, 3)),
    (3, (1, 3, 0, 2)),
)
BACK = {0: (3, 2, 1, 0), 1: (3, 0, 2, 1), 2: (3, 1, 0, 2)}
ARRIVALS = (0, 4, 1, 2, 3, 0, 4, 1, 2, 4, 0, 3, 1, 2, 4, 3, 0, 2, 1, 3)
TURNS = (0, 4, 2, 1, 3)

precise = lax.Precision.HIGHEST
epsilon = 1e-05
momentum_rate = 0.9
outer_rate = 0.7


def contract(first, second, dims, precision=precise):
    return lax.dot_general(
        first,
        second,
        ((dims[:1], dims[1:]), ((), ())),
        precision=precision,
        preferred_element_type=jnp.float32,
    )


def flip(value, axis, mask):
    size = lax.axis_size(axis)
    return lax.ppermute(value, axis, [(i, i ^ mask) for i in range(size)])


def bit_of(axis, bit):
    return (lax.axis_index(axis) >> bit) & 1


def rows_of(value, start, count):
    return lax.dynamic_slice_in_dim(value, start, count, 0)


def halve(value, axis, bit):
    half = value.shape[0] // 2
    side = bit_of(axis, bit)
    sent = rows_of(value, (1 - side) * half, half)
    return rows_of(value, side * half, half) + flip(sent, axis, 1 << bit)


def double(value, axis, bit):
    other = flip(value, axis, 1 << bit)
    side = bit_of(axis, bit)
    both = jnp.concatenate([value, value], 0)
    return lax.dynamic_update_slice_in_dim(both, other, (1 - side) * value.shape[0], 0)


def bit_count(size):
    return size.bit_length() - 1


def sum_over(value, axis):
    for bit in range(bit_count(lax.axis_size(axis))):
        value = value + flip(value, axis, 1 << bit)
    return value


def sum_everywhere(value):
    rep_bits = bit_count(lax.axis_size("rep"))
    mp_bits = bit_count(lax.axis_size("mp"))
    for bit in range(mp_bits):
        value = halve(value, "mp", bit)
    place = lax.axis_index("rep") & 3
    part = value.shape[0] // 4
    pieces = [rows_of(value, (place ^ m) * part, part) for m in range(4)]
    got = [flip(pieces[m], "rep", m) for m in (1, 2, 3)]
    value = (pieces[0] + got[0]) + (got[1] + got[2])
    bit = 2
    while bit < rep_bits:
        if bit + 1 < rep_bits:
            got = [flip(value, "rep", m << bit) for m in (1, 2, 3)]
            value = (value + got[0]) + (got[1] + got[2])
            bit += 2
        else:
            value = value + flip(value, "rep", 1 << bit)
            bit += 1
    got = [value] + [flip(value, "rep", m) for m in (1, 2, 3)]
    whole = jnp.zeros((4 * part,) + value.shape[1:], value.dtype)
    for m in range(4):
        whole = lax.dynamic_update_slice_in_dim(whole, got[m], (place ^ m) * part, 0)
    for bit in reversed(range(mp_bits)):
        whole = double(whole, "mp", bit)
    return whole


LIGHT = pl.CostEstimate(flops=1, bytes_accessed=1, transcendentals=0)


def kernel_call(*args, **options):
    return pl.pallas_call(
        *args, compiler_params=pltpu.CompilerParams(vmem_limit_bytes=10 * 2**20), **options
    )


def near(*arrays):
    return [pltpu.with_memory_space_constraint(array, pltpu.VMEM) for array in arrays]


def distant(array):
    return pltpu.with_memory_space_constraint(array, pltpu.HBM)


def near_shape(shape, dtype=jnp.float32):
    return pltpu.VMEM(shape, dtype)


def specs(*places):
    return [pl.BlockSpec(memory_space=place) for place in places]


def pieces_of(count, most):
    cuts, place = [], 0
    while place < count:
        size = min(most, count - place)
        cuts.append((place, size))
        place += size
    return cuts


def split(value):
    high = value.astype(jnp.bfloat16)
    return high, (value - high.astype(jnp.float32)).astype(jnp.bfloat16)


def squares_kernel(cuts, tokens_ref, grad_ref, out_ref, near_ref, held_ref, sems):
    copies = []
    for index, (start, size) in enumerate(cuts):
        at = pl.ds(start, size)
        copies.append(
            pltpu.make_async_copy(tokens_ref.at[:, at], held_ref.at[:, at], sems.at[index])
        )
        copies[-1].start()
    near_copy = pltpu.make_async_copy(grad_ref, near_ref, sems.at[len(cuts)])
    near_copy.start()
    total = None
    for copy, (start, size) in zip(copies, cuts):
        copy.wait()
        for place in range(start, start + size, BLOCK):
            wide = held_ref[:, place : place + BLOCK].astype(jnp.float32)
            total = wide * wide if total is None else total + wide * wide
    out_ref[...] = jnp.broadcast_to(jnp.sum(total, axis=1, keepdims=True), out_ref.shape)
    near_copy.wait()


def squares(tokens, grad):
    cuts = pieces_of(tokens.shape[1], max(BLOCK, tokens.shape[1] // 4))
    return kernel_call(
        functools.partial(squares_kernel, cuts),
        out_shape=(near_shape((tokens.shape[0], BLOCK)), near_shape(grad.shape, grad.dtype)),
        in_specs=specs(pltpu.HBM, pltpu.HBM),
        out_specs=tuple(specs(pltpu.VMEM, pltpu.VMEM)),
        scratch_shapes=[
            pltpu.VMEM(tokens.shape, tokens.dtype),
            pltpu.SemaphoreType.DMA((len(cuts) + 1,)),
        ],
    )(distant(tokens), distant(grad))


def merge_kernel(
    counts, leaves, depth, starts_ref, tokens_ref, squares_ref, gain_ref, grad_ref, error_ref, *refs
):
    n = len(counts)
    *refs, held_ref, sems, out_sems = refs
    if leaves:
        *outs, sum_ref = refs
    else:
        outs, whole_ref = refs[-n - 1 : -1], refs[-1]
    pieces, base = [], 0
    for s, count in enumerate(counts):
        for place, size in pieces_of(count, 4 * BLOCK):
            there = pl.ds(pl.multiple_of(starts_ref[s] + place, BLOCK), size)
            here, spot = pl.ds(place, size), pl.ds(base + place, size)
            number = len(pieces)
            target = sum_ref.at[spot, :] if leaves else outs[s].at[here, :]
            copies = [
                pltpu.make_async_copy(tokens_ref.at[:, there], held_ref.at[:, spot], sems.at[number, 0]),
                pltpu.make_async_copy(error_ref.at[there, :], target, sems.at[number, 1]),
            ]
            for copy in copies:
                copy.start()
            pieces.append((s, there, here, spot, target, copies))
        base += count
    scale = lax.rsqrt(squares_ref[...] / depth + epsilon)[:, :1]
    written = []
    for s, there, here, spot, target, copies in pieces:
        gain = gain_ref[:, there].astype(jnp.float32)
        copies[0].wait()
        normed = (held_ref[:, spot].astype(jnp.float32) * scale * gain).astype(jnp.bfloat16)
        change = lax.dot_general(
            normed, grad_ref[...], (((0,), (0,)), ((), ())), preferred_element_type=jnp.float32
        )
        copies[1].wait()
        target[...] = change + target[...]
        away = outs[s].at[here, :] if leaves else whole_ref.at[spot, :]
        written.append(pltpu.make_async_copy(target, away, out_sems.at[len(written)]))
        written[-1].start()
    for copy in written:
        copy.wait()


def merge(leaves, starts, counts, depth, tokens, square_sums, gain, grad, error, after=()):
    rows, width = sum(counts), grad.shape[1]
    pieces = sum(len(pieces_of(count, 4 * BLOCK)) for count in counts)
    if leaves:
        shapes = [pltpu.HBM((count, width), jnp.float32) for count in counts]
        places = [pltpu.HBM] * len(counts)
        scratch = [pltpu.VMEM((rows, width), jnp.float32)]
    else:
        shapes = [near_shape((count, width)) for count in counts]
        shapes.append(pltpu.HBM((rows, width), jnp.float32))
        places = [*[pltpu.VMEM] * len(counts), pltpu.HBM]
        scratch = []
    return kernel_call(
        functools.partial(merge_kernel, counts, leaves, depth),
        out_shape=tuple(shapes),
        in_specs=specs(
            pltpu.SMEM, pltpu.HBM, *[pltpu.VMEM] * 3, pltpu.HBM, *[pl.ANY] * len(after)
        ),
        out_specs=tuple(specs(*places)),
        scratch_shapes=[
            *scratch,
            pltpu.VMEM((tokens.shape[0], rows), tokens.dtype),
            pltpu.SemaphoreType.DMA((pieces, 2)),
            pltpu.SemaphoreType.DMA((pieces,)),
        ],
        cost_estimate=pl.CostEstimate(
            flops=2 * rows * width * tokens.shape[0],
            bytes_accessed=8 * rows * width + 2 * tokens.shape[0] * rows,
            transcendentals=0,
        ),
    )(
        jnp.stack(starts).astype(jnp.int32),
        distant(tokens),
        *near(square_sums, gain, grad),
        distant(error),
        *after,
    )


def sides_of(side, half):
    return pl.ds(pl.multiple_of(side * half, 8), half), pl.ds(pl.multiple_of((1 - side) * half, 8), half)


def join_kernel(count, side_ref, own_ref, got_ref, *refs):
    keep_ref, send_ref = refs[-2:]
    stays, goes = sides_of(side_ref[0], count // 2)
    send_ref[...] = own_ref[goes, :] + got_ref[goes, :]
    keep_ref[...] = own_ref[stays, :] + got_ref[stays, :]


def last_kernel(own_ref, got_ref, *refs):
    refs[-1][...] = own_ref[...] + got_ref[...]


def join(own, got, side, after, held):
    count, width = own.shape
    arrays, places = near(own, got), [pltpu.VMEM] * 2
    if side is None:
        kernel, shapes = last_kernel, (near_shape((count, width)),)
    else:
        kernel = functools.partial(join_kernel, count)
        shapes = (near_shape((count // 2, width)),) * 2
        arrays.insert(0, jnp.reshape(side, (1,)).astype(jnp.int32))
        places.insert(0, pltpu.SMEM)
    return kernel_call(
        kernel,
        out_shape=shapes,
        in_specs=specs(*places, *[pl.ANY] * len(after), *[pltpu.VMEM] * len(held)),
        out_specs=tuple(specs(*[pltpu.VMEM] * len(shapes))),
        cost_estimate=LIGHT,
    )(*arrays, *after, *near(*held))


def bundles(plan, step):
    bits = sorted({stream.back[step] for stream in plan})
    groups = [[s for s, stream in enumerate(plan) if stream.back[step] == bit] for bit in bits]
    where = {}
    for index, group in enumerate(groups):
        place = 0
        for s in group:
            where[s] = (index, place)
            place += plan[s].width << step
    return bits, groups, where


def bundle_shapes(plan, step, width):
    _, groups, _ = bundles(plan, step)
    return tuple(near_shape((sum(plan[s].width << step for s in group), width)) for group in groups)


def gather_kernel(plan, step, sides_ref, *refs):
    bits, groups, before = bundles(plan, step)
    _, later_groups, after = bundles(plan, step + 1)
    n = len(groups)
    own, got, out = refs[:n], refs[n : 2 * n], refs[-len(later_groups) :]
    for s, stream in enumerate(plan):
        source, from_row = before[s]
        target, to_row = after[s]
        bit = stream.back[step]
        place = stream.order.index(bit)
        outer = 1 << sum(stream.order.index(b) < place for b in stream.back[:step])
        inner = (stream.width << step) // outer
        for i in range(outer):
            for refs_of, side in ((own, sides_ref[bit]), (got, 1 - sides_ref[bit])):
                row = pl.multiple_of(to_row + 2 * i * inner + side * inner, 8)
                out[target][pl.ds(row, inner), :] = refs_of[source][pl.ds(from_row + i * inner, inner), :]


def gather_step(plan, step, sides, own, got, after):
    shapes = bundle_shapes(plan, step + 1, own[0].shape[1])
    return kernel_call(
        functools.partial(gather_kernel, plan, step),
        out_shape=shapes,
        in_specs=specs(pltpu.SMEM, *[pltpu.VMEM] * (2 * len(own)), *[pl.ANY] * len(after)),
        out_specs=tuple(specs(*[pltpu.VMEM] * len(shapes))),
        cost_estimate=LIGHT,
    )(sides, *near(*own, *got), *after)


def packed_rows(width, share):
    blocks = width // BLOCK
    rows = (blocks * (blocks - 1) // 2 + (blocks + 1) // 2) * BLOCK + 8 * (blocks // 2)
    return -(-rows // share) * share


def block_grid():
    row = lax.broadcasted_iota(jnp.int32, (BLOCK, BLOCK), 0)
    column = lax.broadcasted_iota(jnp.int32, (BLOCK, BLOCK), 1)
    return row, column


def gram_kernel(replicas, *refs):
    out_ref = refs[-1]
    rows = jnp.concatenate([ref[...] for ref in refs[:-1]], 0) / replicas
    blocks = rows.shape[1] // BLOCK
    row, column = block_grid()
    place, diagonals = 0, []
    for a in range(blocks):
        left = rows[:, a * BLOCK : (a + 1) * BLOCK]
        band = contract(left, rows[:, a * BLOCK :], (0, 0))
        diagonals.append(band[:, :BLOCK])
        for b in range(1, blocks - a):
            out_ref[place : place + BLOCK, :] = band[:, b * BLOCK : (b + 1) * BLOCK]
            place += BLOCK
    for a in range(0, blocks, 2):
        both = diagonals[a]
        if a + 1 < blocks:
            both = jnp.where(row <= column, both, diagonals[a + 1])
        out_ref[place : place + BLOCK, :] = both
        place += BLOCK
    for a in range(1, blocks, 2):
        line = jnp.sum(jnp.where(row == column, diagonals[a], 0.0), axis=0, keepdims=True)
        out_ref[place : place + 8, :] = jnp.broadcast_to(line, (8, BLOCK))
        place += 8
    if place < out_ref.shape[0]:
        out_ref[place:, :] = jnp.zeros((out_ref.shape[0] - place, BLOCK), jnp.float32)


def gram(parts, replicas, share):
    rows = packed_rows(parts[0].shape[1], share)
    return kernel_call(
        functools.partial(gram_kernel, replicas),
        out_shape=near_shape((rows, BLOCK)),
        in_specs=specs(*[pltpu.VMEM] * len(parts)),
        out_specs=specs(pltpu.VMEM)[0],
    )(*near(*parts))


def unpack(packed_ref, whole_ref):
    blocks = whole_ref.shape[0] // BLOCK
    row, column = block_grid()
    place = 0

    def put(a, b, tile):
        whole_ref[a * BLOCK : (a + 1) * BLOCK, b * BLOCK : (b + 1) * BLOCK] = tile

    for a in range(blocks):
        for b in range(a + 1, blocks):
            tile = packed_ref[place : place + BLOCK, :]
            put(a, b, tile)
            put(b, a, tile.T)
            place += BLOCK
    line_place = place + (blocks + 1) // 2 * BLOCK
    for a in range(0, blocks, 2):
        tile = packed_ref[place : place + BLOCK, :]
        turned = tile.T
        place += BLOCK
        put(a, a, jnp.where(row <= column, tile, turned))
        if a + 1 < blocks:
            line = packed_ref[line_place : line_place + 1, :]
            line_place += 8
            put(a + 1, a + 1, jnp.where(row > column, tile, jnp.where(row < column, turned, line)))


def factor(matrix):
    size = matrix.shape[0]
    group = 8
    lane = lax.broadcasted_iota(jnp.int32, (size, size), 1)
    row = lax.broadcasted_iota(jnp.int32, (size, size), 0)
    done = []
    live = matrix
    for start in range(0, size, group):
        if start:
            done.append(live[:group])
            live = live[group:]
        count = size - start
        lanes, rows = lane[start:], row[start:]
        columns = [
            jnp.broadcast_to(live[:, start + t : start + t + 1], (count, size)) for t in range(group)
        ]
        for t in range(group):
            pivot = start + t
            inverse = 1.0 / columns[t][t : t + 1, :]
            below = rows > pivot
            scale = jnp.where(below, columns[t] * inverse, 0.0)
            own = jnp.where(lanes[t : t + 1] == pivot, 1.0, live[t : t + 1, :])
            live = jnp.where(below & (lanes == pivot), 0.0, live) - scale * own
            for s in range(t + 1, group):
                columns[s] = columns[s] - scale * columns[s][t : t + 1, :]
    done.append(live)
    result = jnp.concatenate(done, 0)
    diagonal = jnp.sum(jnp.where(lane == row, result, 0.0), axis=1, keepdims=True)
    unit = jnp.where(lane < row, result, jnp.where(lane == row, 1.0, 0.0))
    return unit, diagonal


def first_kernel(plan, replicas, packed_ref, basis_ref, *refs):
    whole_ref, right_ref, gram_ref = refs[len(plan) : len(plan) + 3]
    unpack(packed_ref, whole_ref)
    basis = basis_ref[...]
    plain = contract(whole_ref[...], basis, (1, 0))
    gram_matrix = contract(basis, plain, (0, 0))
    row = lax.broadcasted_iota(jnp.int32, gram_matrix.shape, 0)
    column = lax.broadcasted_iota(jnp.int32, gram_matrix.shape, 1)
    diagonal = jnp.where(row == column, gram_matrix, 0.0)
    across = lax.rsqrt(jnp.sum(diagonal, axis=0, keepdims=True))
    gram_ref[...] = gram_matrix * across * lax.rsqrt(jnp.sum(diagonal, axis=1, keepdims=True))
    right = plain * across
    right_ref[...] = right
    _, groups, _ = bundles(plan, 0)
    for group, left_ref in zip(groups, refs[len(plan) + 3 :]):
        rows = jnp.concatenate([refs[s][...] for s in group], 0) / replicas
        left_ref[...] = contract(rows, right, (1, 0))


def first_pass(plan, packed, basis, parts, replicas):
    width, rank = basis.shape
    shapes = (
        near_shape((width, width)),
        near_shape((width, rank)),
        near_shape((rank, rank)),
        *bundle_shapes(plan, 0, rank),
    )
    whole, right, gram_matrix, *lefts = kernel_call(
        functools.partial(first_kernel, plan, replicas),
        out_shape=shapes,
        in_specs=specs(*[pltpu.VMEM] * (2 + len(parts))),
        out_specs=tuple(specs(*[pltpu.VMEM] * len(shapes))),
    )(*near(packed, basis, *parts))
    return whole, right, gram_matrix, lefts


def inverse_factor(matrix):
    unit, diagonal = factor(matrix)
    return unit * lax.rsqrt(diagonal)


def product_kernel(whole_ref, right_ref, gram_ref, inverse_ref, plain_ref, second_ref):
    inverse = inverse_factor(gram_ref[...])
    inverse_ref[...] = inverse
    right = contract(right_ref[...], inverse, (1, 1))
    plain = contract(whole_ref[...], right, (1, 0))
    plain_ref[...] = plain
    second_ref[...] = contract(right, plain, (0, 0))


def weight_kernel(first_ref, plain_ref, gram_ref, high_ref, low_ref):
    inverse = inverse_factor(gram_ref[...])
    turned = contract(inverse, plain_ref[...], (1, 1))
    weights = contract(first_ref[...], contract(inverse, turned, (0, 0)), (0, 0))
    high_ref[...], low_ref[...] = split(weights)


def second_pass(whole, right, gram_matrix):
    width, rank = right.shape
    square = near_shape((rank, rank))
    inverse, plain, second = kernel_call(
        product_kernel,
        out_shape=(square, near_shape((width, rank)), square),
        in_specs=specs(*[pltpu.VMEM] * 3),
        out_specs=tuple(specs(*[pltpu.VMEM] * 3)),
    )(*near(whole, right, gram_matrix))
    half = near_shape((rank, width), jnp.bfloat16)
    weights = kernel_call(
        weight_kernel,
        out_shape=(half, half),
        in_specs=specs(*[pltpu.VMEM] * 3),
        out_specs=tuple(specs(*[pltpu.VMEM] * 2)),
    )(*near(inverse, plain, second))
    return second, weights


def low_rank(left, high, low):
    left_high, left_low = split(left)
    dot = functools.partial(jnp.dot, preferred_element_type=jnp.float32)
    both = jnp.concatenate([left_high, left_low], 1)
    return dot(both, jnp.concatenate([high, high], 0)) + dot(left_high, low)


def error_pieces(plan, replicas):
    pieces, base = [], 0
    for s, stream in enumerate(plan):
        count = stream.width * replicas // 2
        pieces += [(s, place, base + place, size) for place, size in pieces_of(count, 4 * BLOCK)]
        base += count
    return pieces


def write_errors(plan, replicas, starts_ref, high, low, merged, lefts, out_ref, held_ref, sems, fetched):
    _, _, where = bundles(plan, bit_count(replicas) - 1)
    written = []
    for number, (s, place, spot, size) in enumerate(error_pieces(plan, replicas)):
        index, first = where[s]
        there = pl.ds(pl.multiple_of(starts_ref[s] + place, BLOCK), size)
        here = pl.ds(spot, size)
        change = low_rank(lefts[index][pl.ds(first + place, size), :], high, low)
        if fetched:
            fetched[number].wait()
        held_ref[here, :] = merged[here, :] - change
        written.append(
            pltpu.make_async_copy(held_ref.at[here, :], out_ref.at[there, :], sems.at[number])
        )
        written[-1].start()
    return written


def error_kernel(plan, replicas, starts_ref, high_ref, low_ref, own_ref, *refs):
    n = len(plan)
    out_ref, near_ref, held_ref, fetch_sems, sems, near_sems = refs[-6:]
    fetched = []
    for number, (_, _, spot, size) in enumerate(error_pieces(plan, replicas)):
        here = pl.ds(spot, size)
        fetched.append(
            pltpu.make_async_copy(own_ref.at[here, :], held_ref.at[here, :], fetch_sems.at[number])
        )
        fetched[-1].start()
    others, base = [], 0
    for s, stream in enumerate(plan):
        count = stream.width * replicas // 2
        others.append(
            pltpu.make_async_copy(refs[s], near_ref.at[pl.ds(base, count), :], near_sems.at[s])
        )
        others[-1].start()
        base += count
    written = write_errors(
        plan, replicas, starts_ref, high_ref[...], low_ref[...], held_ref, refs[n:-6], out_ref, held_ref,
        sems, fetched,
    )
    for copy in written + others:
        copy.wait()


def last_error_kernel(plan, replicas, starts_ref, high_ref, low_ref, merged_ref, *refs):
    n = len(plan)
    _, groups, where = bundles(plan, bit_count(replicas) - 1)
    m = len(groups)
    others, lefts = refs[:m], refs[m : 2 * m]
    weights_ref, momentum_ref = refs[2 * m : 2 * m + 2]
    out_ref, weights_out, momentum_out, held_ref, left_ref, sems = refs[-6:]
    high, low = high_ref[...], low_ref[...]
    written = write_errors(
        plan, replicas, starts_ref, high, low, merged_ref, others, out_ref, held_ref, sems, None
    )
    rows = left_ref.shape[0]
    size = min(BLOCK, rows)
    for place in range(0, rows, size):
        want = starts_ref[2 * n] + place
        for k, bundle in ((0, others), (n, lefts)):
            for s, stream in enumerate(plan):
                index, first = where[s]
                skip = want - starts_ref[k + s]

                @pl.when((skip >= 0) & (skip < stream.width * replicas // 2))
                def _(bundle=bundle, index=index, first=first, skip=skip, place=place):
                    row = pl.multiple_of(first + skip, 8)
                    left_ref[place : place + size, :] = bundle[index][pl.ds(row, size), :]

    own_rows = low_rank(left_ref[...], high, low)
    momentum = momentum_rate * momentum_ref[...] + own_rows
    momentum_out[...] = momentum
    weights_out[...] = weights_ref[...] - outer_rate * (own_rows + momentum_rate * momentum)
    for copy in written:
        copy.wait()


def error_options(plan, replicas, width, rank):
    pieces = error_pieces(plan, replicas)
    rows = sum(piece[3] for piece in pieces)
    scratch = pltpu.VMEM((rows, width), jnp.float32), pltpu.SemaphoreType.DMA((len(pieces),))
    cost = pl.CostEstimate(
        flops=6 * rows * width * rank, bytes_accessed=8 * rows * width, transcendentals=0
    )
    return scratch, cost


def error_rows(plan, replicas, starts, own, far, lefts, high, low, shape):
    scratch, cost = error_options(plan, replicas, shape[1], high.shape[0])
    return kernel_call(
        functools.partial(error_kernel, plan, replicas),
        out_shape=(jax.ShapeDtypeStruct(shape, jnp.float32), near_shape(own.shape)),
        in_specs=specs(
            pltpu.SMEM, *[pltpu.VMEM] * 2, *[pltpu.HBM] * (1 + len(far)), *[pltpu.VMEM] * len(lefts)
        ),
        out_specs=tuple(specs(pltpu.HBM, pltpu.VMEM)),
        scratch_shapes=[*scratch, scratch[1], pltpu.SemaphoreType.DMA((len(far),))],
        cost_estimate=cost,
    )(
        jnp.stack(starts).astype(jnp.int32), *near(high, low), distant(own), *map(distant, far), *near(*lefts)
    )


def last_rows(plan, replicas, kept, starts, merged, others, lefts, high, low, weights, momentum):
    rows, width = weights.shape
    (held, sems), cost = error_options(plan, replicas, width, high.shape[0])
    arrays = [
        jnp.stack([*starts, lax.axis_index("rep") * rows]).astype(jnp.int32),
        *near(high, low, merged, *others, *lefts),
        weights,
        momentum,
        kept,
    ]
    result = jax.ShapeDtypeStruct(weights.shape, jnp.float32)
    return kernel_call(
        functools.partial(last_error_kernel, plan, replicas),
        out_shape=(jax.ShapeDtypeStruct(kept.shape, jnp.float32), result, result),
        in_specs=specs(pltpu.SMEM, *[pltpu.VMEM] * (2 * len(lefts) + 5), pltpu.HBM),
        out_specs=tuple(specs(pltpu.HBM, pltpu.VMEM, pltpu.VMEM)),
        scratch_shapes=[held, pltpu.VMEM((rows, high.shape[0]), jnp.float32), sems],
        input_output_aliases={len(arrays) - 1: 0},
        cost_estimate=cost,
    )(*arrays)


@dataclasses.dataclass(frozen=True)
class Stream:
    width: int
    order: tuple
    back: tuple


def stream_plan(replicas, rows_each):
    bits = bit_count(replicas)
    grain = max(8, 2 * BLOCK // replicas)
    units = rows_each // grain
    if bits == 4 and units % 16 == 0:
        shares = SHARES
        plan = [
            Stream(share * units // 16 * grain, order, BACK[order[0]])
            for share, order in shares
        ]
        return plan, TURNS, ARRIVALS
    streams = max(1, min(3, units, bits - 1))
    widths = [units // streams + (1 if s < units % streams else 0) for s in range(streams)]
    lead = list(range(min(3, bits)))
    rest = list(range(len(lead), bits))
    orders = [tuple(lead[s % len(lead) :] + lead[: s % len(lead)] + rest) for s in range(streams)]
    plan = [Stream(w * grain, order, order[::-1]) for w, order in zip(widths, orders)]
    return plan, range(streams), [s for _ in range(bits) for s in range(streams)]


def on_device(tokens_in, norm_gain, key_grad, error_in, basis_init, weights_in, momentum_in):
    replicas = lax.axis_size("rep")
    steps = bit_count(replicas)
    depth = tokens_in.shape[1]
    error = error_in[0]
    square_sums, grad = squares(tokens_in, key_grad)
    square_sums = sum_over(square_sums, "mp")
    basis = lax.all_gather(basis_init, "mp", axis=0, tiled=True)
    sources = (
        depth * lax.axis_size("mp"), tokens_in, square_sums, norm_gain[None, :], grad, error
    )

    plan, turns, arrivals = stream_plan(replicas, depth // replicas)
    halves, here, there, place = [], [], [], 0
    for stream in plan:
        half = stream.width * replicas // 2
        side = bit_of("rep", stream.order[0])
        halves.append(half)
        here.append(place + side * half)
        there.append(place + (1 - side) * half)
        place += 2 * half
    far = merge(True, there, halves, *sources)
    got = [flip(part, "rep", 1 << stream.order[0]) for part, stream in zip(far, plan)]
    *own, own_kept = merge(False, here, halves, *sources, after=[basis])
    parts, after, done = list(own), [], [0] * len(plan)
    for s in arrivals:
        done[s] += 1
        came = got[s]
        if done[s] < steps:
            bit = plan[s].order[done[s]]
            parts[s], send = join(parts[s], came, bit_of("rep", bit), after, [p for k, p in enumerate(parts) if k != s])
            got[s] = flip(send, "rep", 1 << bit)
        else:
            (parts[s],) = join(parts[s], came, None, after, [])
        after = [came]

    packed = sum_everywhere(gram(parts, replicas, 32 * lax.axis_size("mp")))
    whole, right, gram_matrix, lefts = first_pass(plan, packed, basis, parts, replicas)
    second, (high, low) = second_pass(whole, right, gram_matrix)

    bit_sides = jnp.stack([bit_of("rep", bit) for bit in range(steps)]).astype(jnp.int32)
    for step in range(steps):
        bits, _, _ = bundles(plan, step)
        others = [flip(left, "rep", 1 << bit) for left, bit in zip(lefts, bits)]
        if step + 1 < steps:
            lefts = gather_step(plan, step, bit_sides, lefts, others, [high if step + 2 >= steps else second])

    error_out, far_near = error_rows(
        plan, replicas, here, own_kept, far, lefts, high, low, error.shape
    )
    error_out, weights_out, momentum_out = last_rows(
        plan, replicas, error_out, there + here, far_near, others, lefts, high, low, weights_in[0],
        momentum_in[0],
    )
    return (error_out[None], weights_out[None], momentum_out[None])


def solution(mesh):
    in_specs = (
        P("rep", "mp"),
        P("mp"),
        P("rep", None),
        P("rep", "mp", None),
        P("mp", None),
        P("mp", "rep", None),
        P("mp", "rep", None),
    )
    out_specs = (P("rep", "mp", None), P("mp", "rep", None), P("mp", "rep", None))
    return jax.shard_map(
        on_device, mesh=mesh, in_specs=in_specs, out_specs=out_specs, check_vma=False
    )
```

```python
import dataclasses
import functools

import jax
import jax.numpy as jnp
from jax import lax
from jax.experimental import pallas as pl
from jax.experimental.pallas import tpu as pltpu
from jax.sharding import PartitionSpec as P

BLOCK = 128

SHARES = (
    (3, (0, 2, 1, 3)),
    (4, (2, 0, 1, 3)),
    (3, (0, 1, 3, 2)),
    (3, (1, 2, 0, 3)),
    (3, (1, 3, 0, 2)),
)
BACK = {0: (3, 2, 1, 0), 1: (3, 0, 2, 1), 2: (3, 1, 0, 2)}
ARRIVALS = (0, 4, 1, 2, 3, 0, 4, 1, 2, 4, 0, 3, 1, 2, 4, 3, 0, 2, 1, 3)
TURNS = (0, 4, 2, 1, 3)

precise = lax.Precision.HIGHEST
epsilon = 1e-05
momentum_rate = 0.9
outer_rate = 0.7


def contract(first, second, dims, precision=precise):
    return lax.dot_general(
        first,
        second,
        ((dims[:1], dims[1:]), ((), ())),
        precision=precision,
        preferred_element_type=jnp.float32,
    )


def flip(value, axis, mask):
    size = lax.axis_size(axis)
    return lax.ppermute(value, axis, [(i, i ^ mask) for i in range(size)])


def bit_of(axis, bit):
    return (lax.axis_index(axis) >> bit) & 1


def rows_of(value, start, count):
    return lax.dynamic_slice_in_dim(value, start, count, 0)


def halve(value, axis, bit):
    half = value.shape[0] // 2
    side = bit_of(axis, bit)
    sent = rows_of(value, (1 - side) * half, half)
    return rows_of(value, side * half, half) + flip(sent, axis, 1 << bit)


def double(value, axis, bit):
    other = flip(value, axis, 1 << bit)
    side = bit_of(axis, bit)
    both = jnp.concatenate([value, value], 0)
    return lax.dynamic_update_slice_in_dim(both, other, (1 - side) * value.shape[0], 0)


def bit_count(size):
    return size.bit_length() - 1


def sum_over(value, axis):
    for bit in range(bit_count(lax.axis_size(axis))):
        value = value + flip(value, axis, 1 << bit)
    return value


def sum_everywhere(value):
    rep_bits = bit_count(lax.axis_size("rep"))
    mp_bits = bit_count(lax.axis_size("mp"))
    for bit in range(mp_bits):
        value = halve(value, "mp", bit)
    place = lax.axis_index("rep") & 3
    part = value.shape[0] // 4
    pieces = [rows_of(value, (place ^ m) * part, part) for m in range(4)]
    got = [flip(pieces[m], "rep", m) for m in (1, 2, 3)]
    value = (pieces[0] + got[0]) + (got[1] + got[2])
    bit = 2
    while bit < rep_bits:
        if bit + 1 < rep_bits:
            got = [flip(value, "rep", m << bit) for m in (1, 2, 3)]
            value = (value + got[0]) + (got[1] + got[2])
            bit += 2
        else:
            value = value + flip(value, "rep", 1 << bit)
            bit += 1
    got = [value] + [flip(value, "rep", m) for m in (1, 2, 3)]
    whole = jnp.zeros((4 * part,) + value.shape[1:], value.dtype)
    for m in range(4):
        whole = lax.dynamic_update_slice_in_dim(whole, got[m], (place ^ m) * part, 0)
    for bit in reversed(range(mp_bits)):
        whole = double(whole, "mp", bit)
    return whole


LIGHT = pl.CostEstimate(flops=1, bytes_accessed=1, transcendentals=0)


def kernel_call(*args, **options):
    return pl.pallas_call(
        *args, compiler_params=pltpu.CompilerParams(vmem_limit_bytes=10 * 2**20), **options
    )


def near(*arrays):
    return [pltpu.with_memory_space_constraint(array, pltpu.VMEM) for array in arrays]


def distant(array):
    return pltpu.with_memory_space_constraint(array, pltpu.HBM)


def near_shape(shape, dtype=jnp.float32):
    return pltpu.VMEM(shape, dtype)


def specs(*places):
    return [pl.BlockSpec(memory_space=place) for place in places]


def pieces_of(count, most):
    cuts, place = [], 0
    while place < count:
        size = min(most, count - place)
        cuts.append((place, size))
        place += size
    return cuts


def split(value):
    high = value.astype(jnp.bfloat16)
    return high, (value - high.astype(jnp.float32)).astype(jnp.bfloat16)


def squares_kernel(cuts, tokens_ref, grad_ref, out_ref, near_ref, held_ref, sems):
    copies = []
    for index, (start, size) in enumerate(cuts):
        at = pl.ds(start, size)
        copies.append(
            pltpu.make_async_copy(tokens_ref.at[:, at], held_ref.at[:, at], sems.at[index])
        )
        copies[-1].start()
    near_copy = pltpu.make_async_copy(grad_ref, near_ref, sems.at[len(cuts)])
    near_copy.start()
    total = None
    for copy, (start, size) in zip(copies, cuts):
        copy.wait()
        for place in range(start, start + size, BLOCK):
            wide = held_ref[:, place : place + BLOCK].astype(jnp.float32)
            total = wide * wide if total is None else total + wide * wide
    out_ref[...] = jnp.broadcast_to(jnp.sum(total, axis=1, keepdims=True), out_ref.shape)
    near_copy.wait()


def squares(tokens, grad):
    cuts = pieces_of(tokens.shape[1], max(BLOCK, tokens.shape[1] // 4))
    return kernel_call(
        functools.partial(squares_kernel, cuts),
        out_shape=(near_shape((tokens.shape[0], BLOCK)), near_shape(grad.shape, grad.dtype)),
        in_specs=specs(pltpu.HBM, pltpu.HBM),
        out_specs=tuple(specs(pltpu.VMEM, pltpu.VMEM)),
        scratch_shapes=[
            pltpu.VMEM(tokens.shape, tokens.dtype),
            pltpu.SemaphoreType.DMA((len(cuts) + 1,)),
        ],
    )(distant(tokens), distant(grad))


def merge_kernel(
    counts, leaves, depth, starts_ref, tokens_ref, squares_ref, gain_ref, grad_ref, error_ref, *refs
):
    n = len(counts)
    *refs, held_ref, sems, out_sems = refs
    if leaves:
        *outs, sum_ref = refs
    else:
        outs, whole_ref = refs[-n - 1 : -1], refs[-1]
    pieces, base = [], 0
    for s, count in enumerate(counts):
        for place, size in pieces_of(count, 2 * BLOCK):
            there = pl.ds(pl.multiple_of(starts_ref[s] + place, BLOCK), size)
            here, spot = pl.ds(place, size), pl.ds(base + place, size)
            number = len(pieces)
            target = sum_ref.at[spot, :] if leaves else outs[s].at[here, :]
            copies = [
                pltpu.make_async_copy(tokens_ref.at[:, there], held_ref.at[:, spot], sems.at[number, 0]),
                pltpu.make_async_copy(error_ref.at[there, :], target, sems.at[number, 1]),
            ]
            for copy in copies:
                copy.start()
            pieces.append((s, there, here, spot, target, copies))
        base += count
    scale = lax.rsqrt(squares_ref[...] / depth + epsilon)[:, :1]
    written = []
    for s, there, here, spot, target, copies in pieces:
        gain = gain_ref[:, there].astype(jnp.float32)
        copies[0].wait()
        normed = (held_ref[:, spot].astype(jnp.float32) * scale * gain).astype(jnp.bfloat16)
        change = lax.dot_general(
            normed, grad_ref[...], (((0,), (0,)), ((), ())), preferred_element_type=jnp.float32
        )
        copies[1].wait()
        target[...] = change + target[...]
        away = outs[s].at[here, :] if leaves else whole_ref.at[spot, :]
        written.append(pltpu.make_async_copy(target, away, out_sems.at[len(written)]))
        written[-1].start()
    for copy in written:
        copy.wait()


def merge(leaves, starts, counts, depth, tokens, square_sums, gain, grad, error, after=()):
    rows, width = sum(counts), grad.shape[1]
    pieces = sum(len(pieces_of(count, 2 * BLOCK)) for count in counts)
    if leaves:
        shapes = [pltpu.HBM((count, width), jnp.float32) for count in counts]
        places = [pltpu.HBM] * len(counts)
        scratch = [pltpu.VMEM((rows, width), jnp.float32)]
    else:
        shapes = [near_shape((count, width)) for count in counts]
        shapes.append(pltpu.HBM((rows, width), jnp.float32))
        places = [*[pltpu.VMEM] * len(counts), pltpu.HBM]
        scratch = []
    return kernel_call(
        functools.partial(merge_kernel, counts, leaves, depth),
        out_shape=tuple(shapes),
        in_specs=specs(
            pltpu.SMEM, pltpu.HBM, *[pltpu.VMEM] * 3, pltpu.HBM, *[pl.ANY] * len(after)
        ),
        out_specs=tuple(specs(*places)),
        scratch_shapes=[
            *scratch,
            pltpu.VMEM((tokens.shape[0], rows), tokens.dtype),
            pltpu.SemaphoreType.DMA((pieces, 2)),
            pltpu.SemaphoreType.DMA((pieces,)),
        ],
        cost_estimate=pl.CostEstimate(
            flops=2 * rows * width * tokens.shape[0],
            bytes_accessed=8 * rows * width + 2 * tokens.shape[0] * rows,
            transcendentals=0,
        ),
    )(
        jnp.stack(starts).astype(jnp.int32),
        distant(tokens),
        *near(square_sums, gain, grad),
        distant(error),
        *after,
    )


def sides_of(side, half):
    return pl.ds(pl.multiple_of(side * half, 8), half), pl.ds(pl.multiple_of((1 - side) * half, 8), half)


def join_kernel(count, side_ref, own_ref, got_ref, *refs):
    keep_ref, send_ref = refs[-2:]
    stays, goes = sides_of(side_ref[0], count // 2)
    send_ref[...] = own_ref[goes, :] + got_ref[goes, :]
    keep_ref[...] = own_ref[stays, :] + got_ref[stays, :]


def last_kernel(own_ref, got_ref, *refs):
    refs[-1][...] = own_ref[...] + got_ref[...]


def join(own, got, side, after, held):
    count, width = own.shape
    arrays, places = near(own, got), [pltpu.VMEM] * 2
    if side is None:
        kernel, shapes = last_kernel, (near_shape((count, width)),)
    else:
        kernel = functools.partial(join_kernel, count)
        shapes = (near_shape((count // 2, width)),) * 2
        arrays.insert(0, jnp.reshape(side, (1,)).astype(jnp.int32))
        places.insert(0, pltpu.SMEM)
    return kernel_call(
        kernel,
        out_shape=shapes,
        in_specs=specs(*places, *[pl.ANY] * len(after), *[pltpu.VMEM] * len(held)),
        out_specs=tuple(specs(*[pltpu.VMEM] * len(shapes))),
        cost_estimate=LIGHT,
    )(*arrays, *after, *near(*held))


def bundles(plan, step):
    bits = sorted({stream.back[step] for stream in plan})
    groups = [[s for s, stream in enumerate(plan) if stream.back[step] == bit] for bit in bits]
    where = {}
    for index, group in enumerate(groups):
        place = 0
        for s in group:
            where[s] = (index, place)
            place += plan[s].width << step
    return bits, groups, where


def bundle_shapes(plan, step, width):
    _, groups, _ = bundles(plan, step)
    return tuple(near_shape((sum(plan[s].width << step for s in group), width)) for group in groups)


def gather_kernel(plan, step, sides_ref, *refs):
    bits, groups, before = bundles(plan, step)
    _, later_groups, after = bundles(plan, step + 1)
    n = len(groups)
    own, got, out = refs[:n], refs[n : 2 * n], refs[-len(later_groups) :]
    for s, stream in enumerate(plan):
        source, from_row = before[s]
        target, to_row = after[s]
        bit = stream.back[step]
        place = stream.order.index(bit)
        outer = 1 << sum(stream.order.index(b) < place for b in stream.back[:step])
        inner = (stream.width << step) // outer
        for i in range(outer):
            for refs_of, side in ((own, sides_ref[bit]), (got, 1 - sides_ref[bit])):
                row = pl.multiple_of(to_row + 2 * i * inner + side * inner, 8)
                out[target][pl.ds(row, inner), :] = refs_of[source][pl.ds(from_row + i * inner, inner), :]


def gather_step(plan, step, sides, own, got, after):
    shapes = bundle_shapes(plan, step + 1, own[0].shape[1])
    return kernel_call(
        functools.partial(gather_kernel, plan, step),
        out_shape=shapes,
        in_specs=specs(pltpu.SMEM, *[pltpu.VMEM] * (2 * len(own)), *[pl.ANY] * len(after)),
        out_specs=tuple(specs(*[pltpu.VMEM] * len(shapes))),
        cost_estimate=LIGHT,
    )(sides, *near(*own, *got), *after)


def packed_rows(width, share):
    blocks = width // BLOCK
    rows = (blocks * (blocks - 1) // 2 + (blocks + 1) // 2) * BLOCK + 8 * (blocks // 2)
    return -(-rows // share) * share


def block_grid():
    row = lax.broadcasted_iota(jnp.int32, (BLOCK, BLOCK), 0)
    column = lax.broadcasted_iota(jnp.int32, (BLOCK, BLOCK), 1)
    return row, column


def gram_kernel(replicas, *refs):
    out_ref = refs[-1]
    rows = jnp.concatenate([ref[...] for ref in refs[:-1]], 0) / replicas
    blocks = rows.shape[1] // BLOCK
    row, column = block_grid()
    place, diagonals = 0, []
    for a in range(blocks):
        left = rows[:, a * BLOCK : (a + 1) * BLOCK]
        band = contract(left, rows[:, a * BLOCK :], (0, 0))
        diagonals.append(band[:, :BLOCK])
        for b in range(1, blocks - a):
            out_ref[place : place + BLOCK, :] = band[:, b * BLOCK : (b + 1) * BLOCK]
            place += BLOCK
    for a in range(0, blocks, 2):
        both = diagonals[a]
        if a + 1 < blocks:
            both = jnp.where(row <= column, both, diagonals[a + 1])
        out_ref[place : place + BLOCK, :] = both
        place += BLOCK
    for a in range(1, blocks, 2):
        line = jnp.sum(jnp.where(row == column, diagonals[a], 0.0), axis=0, keepdims=True)
        out_ref[place : place + 8, :] = jnp.broadcast_to(line, (8, BLOCK))
        place += 8
    if place < out_ref.shape[0]:
        out_ref[place:, :] = jnp.zeros((out_ref.shape[0] - place, BLOCK), jnp.float32)


def gram(parts, replicas, share):
    rows = packed_rows(parts[0].shape[1], share)
    return kernel_call(
        functools.partial(gram_kernel, replicas),
        out_shape=near_shape((rows, BLOCK)),
        in_specs=specs(*[pltpu.VMEM] * len(parts)),
        out_specs=specs(pltpu.VMEM)[0],
    )(*near(*parts))


def unpack(packed_ref, whole_ref):
    blocks = whole_ref.shape[0] // BLOCK
    row, column = block_grid()
    place = 0

    def put(a, b, tile):
        whole_ref[a * BLOCK : (a + 1) * BLOCK, b * BLOCK : (b + 1) * BLOCK] = tile

    for a in range(blocks):
        for b in range(a + 1, blocks):
            tile = packed_ref[place : place + BLOCK, :]
            put(a, b, tile)
            put(b, a, tile.T)
            place += BLOCK
    line_place = place + (blocks + 1) // 2 * BLOCK
    for a in range(0, blocks, 2):
        tile = packed_ref[place : place + BLOCK, :]
        turned = tile.T
        place += BLOCK
        put(a, a, jnp.where(row <= column, tile, turned))
        if a + 1 < blocks:
            line = packed_ref[line_place : line_place + 1, :]
            line_place += 8
            put(a + 1, a + 1, jnp.where(row > column, tile, jnp.where(row < column, turned, line)))


def factor(matrix):
    size = matrix.shape[0]
    group = 8
    lane = lax.broadcasted_iota(jnp.int32, (size, size), 1)
    row = lax.broadcasted_iota(jnp.int32, (size, size), 0)
    done = []
    live = matrix
    for start in range(0, size, group):
        if start:
            done.append(live[:group])
            live = live[group:]
        count = size - start
        lanes, rows = lane[start:], row[start:]
        columns = [
            jnp.broadcast_to(live[:, start + t : start + t + 1], (count, size)) for t in range(group)
        ]
        for t in range(group):
            pivot = start + t
            inverse = 1.0 / columns[t][t : t + 1, :]
            below = rows > pivot
            scale = jnp.where(below, columns[t] * inverse, 0.0)
            own = jnp.where(lanes[t : t + 1] == pivot, 1.0, live[t : t + 1, :])
            live = jnp.where(below & (lanes == pivot), 0.0, live) - scale * own
            for s in range(t + 1, group):
                columns[s] = columns[s] - scale * columns[s][t : t + 1, :]
    done.append(live)
    result = jnp.concatenate(done, 0)
    diagonal = jnp.sum(jnp.where(lane == row, result, 0.0), axis=1, keepdims=True)
    unit = jnp.where(lane < row, result, jnp.where(lane == row, 1.0, 0.0))
    return unit, diagonal


def first_kernel(plan, replicas, packed_ref, basis_ref, *refs):
    whole_ref, right_ref, gram_ref = refs[len(plan) : len(plan) + 3]
    unpack(packed_ref, whole_ref)
    basis = basis_ref[...]
    plain = contract(whole_ref[...], basis, (1, 0))
    gram_matrix = contract(basis, plain, (0, 0))
    row = lax.broadcasted_iota(jnp.int32, gram_matrix.shape, 0)
    column = lax.broadcasted_iota(jnp.int32, gram_matrix.shape, 1)
    diagonal = jnp.where(row == column, gram_matrix, 0.0)
    across = lax.rsqrt(jnp.sum(diagonal, axis=0, keepdims=True))
    gram_ref[...] = gram_matrix * across * lax.rsqrt(jnp.sum(diagonal, axis=1, keepdims=True))
    right = plain * across
    right_ref[...] = right
    _, groups, _ = bundles(plan, 0)
    for group, left_ref in zip(groups, refs[len(plan) + 3 :]):
        rows = jnp.concatenate([refs[s][...] for s in group], 0) / replicas
        left_ref[...] = contract(rows, right, (1, 0))


def first_pass(plan, packed, basis, parts, replicas):
    width, rank = basis.shape
    shapes = (
        near_shape((width, width)),
        near_shape((width, rank)),
        near_shape((rank, rank)),
        *bundle_shapes(plan, 0, rank),
    )
    whole, right, gram_matrix, *lefts = kernel_call(
        functools.partial(first_kernel, plan, replicas),
        out_shape=shapes,
        in_specs=specs(*[pltpu.VMEM] * (2 + len(parts))),
        out_specs=tuple(specs(*[pltpu.VMEM] * len(shapes))),
    )(*near(packed, basis, *parts))
    return whole, right, gram_matrix, lefts


def inverse_factor(matrix):
    unit, diagonal = factor(matrix)
    return unit * lax.rsqrt(diagonal)


def product_kernel(whole_ref, right_ref, gram_ref, inverse_ref, plain_ref, second_ref):
    inverse = inverse_factor(gram_ref[...])
    inverse_ref[...] = inverse
    right = contract(right_ref[...], inverse, (1, 1))
    plain = contract(whole_ref[...], right, (1, 0))
    plain_ref[...] = plain
    second_ref[...] = contract(right, plain, (0, 0))


def weight_kernel(first_ref, plain_ref, gram_ref, high_ref, low_ref):
    inverse = inverse_factor(gram_ref[...])
    turned = contract(inverse, plain_ref[...], (1, 1))
    weights = contract(first_ref[...], contract(inverse, turned, (0, 0)), (0, 0))
    high_ref[...], low_ref[...] = split(weights)


def second_pass(whole, right, gram_matrix):
    width, rank = right.shape
    square = near_shape((rank, rank))
    inverse, plain, second = kernel_call(
        product_kernel,
        out_shape=(square, near_shape((width, rank)), square),
        in_specs=specs(*[pltpu.VMEM] * 3),
        out_specs=tuple(specs(*[pltpu.VMEM] * 3)),
    )(*near(whole, right, gram_matrix))
    half = near_shape((rank, width), jnp.bfloat16)
    weights = kernel_call(
        weight_kernel,
        out_shape=(half, half),
        in_specs=specs(*[pltpu.VMEM] * 3),
        out_specs=tuple(specs(*[pltpu.VMEM] * 2)),
    )(*near(inverse, plain, second))
    return second, weights


def low_rank(left, high, low):
    left_high, left_low = split(left)
    dot = functools.partial(jnp.dot, preferred_element_type=jnp.float32)
    both = jnp.concatenate([left_high, left_low], 1)
    return dot(both, jnp.concatenate([high, high], 0)) + dot(left_high, low)


def error_pieces(plan, replicas):
    pieces, base = [], 0
    for s, stream in enumerate(plan):
        count = stream.width * replicas // 2
        pieces += [(s, place, base + place, size) for place, size in pieces_of(count, 4 * BLOCK)]
        base += count
    return pieces


def write_errors(plan, replicas, starts_ref, high, low, merged, lefts, out_ref, held_ref, sems, fetched):
    _, _, where = bundles(plan, bit_count(replicas) - 1)
    written = []
    for number, (s, place, spot, size) in enumerate(error_pieces(plan, replicas)):
        index, first = where[s]
        there = pl.ds(pl.multiple_of(starts_ref[s] + place, BLOCK), size)
        here = pl.ds(spot, size)
        change = low_rank(lefts[index][pl.ds(first + place, size), :], high, low)
        if fetched:
            fetched[number].wait()
        held_ref[here, :] = merged[here, :] - change
        written.append(
            pltpu.make_async_copy(held_ref.at[here, :], out_ref.at[there, :], sems.at[number])
        )
        written[-1].start()
    return written


def error_kernel(plan, replicas, starts_ref, high_ref, low_ref, own_ref, *refs):
    n = len(plan)
    out_ref, near_ref, held_ref, fetch_sems, sems, near_sems = refs[-6:]
    fetched = []
    for number, (_, _, spot, size) in enumerate(error_pieces(plan, replicas)):
        here = pl.ds(spot, size)
        fetched.append(
            pltpu.make_async_copy(own_ref.at[here, :], held_ref.at[here, :], fetch_sems.at[number])
        )
        fetched[-1].start()
    others, base = [], 0
    for s, stream in enumerate(plan):
        count = stream.width * replicas // 2
        others.append(
            pltpu.make_async_copy(refs[s], near_ref.at[pl.ds(base, count), :], near_sems.at[s])
        )
        others[-1].start()
        base += count
    written = write_errors(
        plan, replicas, starts_ref, high_ref[...], low_ref[...], held_ref, refs[n:-6], out_ref, held_ref,
        sems, fetched,
    )
    for copy in written + others:
        copy.wait()


def last_error_kernel(plan, replicas, starts_ref, high_ref, low_ref, merged_ref, *refs):
    n = len(plan)
    _, groups, where = bundles(plan, bit_count(replicas) - 1)
    m = len(groups)
    others, lefts = refs[:m], refs[m : 2 * m]
    weights_ref, momentum_ref = refs[2 * m : 2 * m + 2]
    out_ref, weights_out, momentum_out, held_ref, left_ref, sems = refs[-6:]
    high, low = high_ref[...], low_ref[...]
    written = write_errors(
        plan, replicas, starts_ref, high, low, merged_ref, others, out_ref, held_ref, sems, None
    )
    rows = left_ref.shape[0]
    size = min(BLOCK, rows)
    for place in range(0, rows, size):
        want = starts_ref[2 * n] + place
        for k, bundle in ((0, others), (n, lefts)):
            for s, stream in enumerate(plan):
                index, first = where[s]
                skip = want - starts_ref[k + s]

                @pl.when((skip >= 0) & (skip < stream.width * replicas // 2))
                def _(bundle=bundle, index=index, first=first, skip=skip, place=place):
                    row = pl.multiple_of(first + skip, 8)
                    left_ref[place : place + size, :] = bundle[index][pl.ds(row, size), :]

    own_rows = low_rank(left_ref[...], high, low)
    momentum = momentum_rate * momentum_ref[...] + own_rows
    momentum_out[...] = momentum
    weights_out[...] = weights_ref[...] - outer_rate * (own_rows + momentum_rate * momentum)
    for copy in written:
        copy.wait()


def error_options(plan, replicas, width, rank):
    pieces = error_pieces(plan, replicas)
    rows = sum(piece[3] for piece in pieces)
    scratch = pltpu.VMEM((rows, width), jnp.float32), pltpu.SemaphoreType.DMA((len(pieces),))
    cost = pl.CostEstimate(
        flops=6 * rows * width * rank, bytes_accessed=8 * rows * width, transcendentals=0
    )
    return scratch, cost


def error_rows(plan, replicas, starts, own, far, lefts, high, low, shape):
    scratch, cost = error_options(plan, replicas, shape[1], high.shape[0])
    return kernel_call(
        functools.partial(error_kernel, plan, replicas),
        out_shape=(jax.ShapeDtypeStruct(shape, jnp.float32), near_shape(own.shape)),
        in_specs=specs(
            pltpu.SMEM, *[pltpu.VMEM] * 2, *[pltpu.HBM] * (1 + len(far)), *[pltpu.VMEM] * len(lefts)
        ),
        out_specs=tuple(specs(pltpu.HBM, pltpu.VMEM)),
        scratch_shapes=[*scratch, scratch[1], pltpu.SemaphoreType.DMA((len(far),))],
        cost_estimate=cost,
    )(
        jnp.stack(starts).astype(jnp.int32), *near(high, low), distant(own), *map(distant, far), *near(*lefts)
    )


def last_rows(plan, replicas, kept, starts, merged, others, lefts, high, low, weights, momentum):
    rows, width = weights.shape
    (held, sems), cost = error_options(plan, replicas, width, high.shape[0])
    arrays = [
        jnp.stack([*starts, lax.axis_index("rep") * rows]).astype(jnp.int32),
        *near(high, low, merged, *others, *lefts),
        weights,
        momentum,
        kept,
    ]
    result = jax.ShapeDtypeStruct(weights.shape, jnp.float32)
    return kernel_call(
        functools.partial(last_error_kernel, plan, replicas),
        out_shape=(jax.ShapeDtypeStruct(kept.shape, jnp.float32), result, result),
        in_specs=specs(pltpu.SMEM, *[pltpu.VMEM] * (2 * len(lefts) + 5), pltpu.HBM),
        out_specs=tuple(specs(pltpu.HBM, pltpu.VMEM, pltpu.VMEM)),
        scratch_shapes=[held, pltpu.VMEM((rows, high.shape[0]), jnp.float32), sems],
        input_output_aliases={len(arrays) - 1: 0},
        cost_estimate=cost,
    )(*arrays)


@dataclasses.dataclass(frozen=True)
class Stream:
    width: int
    order: tuple
    back: tuple


def stream_plan(replicas, rows_each):
    bits = bit_count(replicas)
    grain = max(8, 2 * BLOCK // replicas)
    units = rows_each // grain
    if bits == 4 and units % 16 == 0:
        shares = SHARES
        plan = [
            Stream(share * units // 16 * grain, order, BACK[order[0]])
            for share, order in shares
        ]
        return plan, TURNS, ARRIVALS
    streams = max(1, min(3, units, bits - 1))
    widths = [units // streams + (1 if s < units % streams else 0) for s in range(streams)]
    lead = list(range(min(3, bits)))
    rest = list(range(len(lead), bits))
    orders = [tuple(lead[s % len(lead) :] + lead[: s % len(lead)] + rest) for s in range(streams)]
    plan = [Stream(w * grain, order, order[::-1]) for w, order in zip(widths, orders)]
    return plan, range(streams), [s for _ in range(bits) for s in range(streams)]


def on_device(tokens_in, norm_gain, key_grad, error_in, basis_init, weights_in, momentum_in):
    replicas = lax.axis_size("rep")
    steps = bit_count(replicas)
    depth = tokens_in.shape[1]
    error = error_in[0]
    square_sums, grad = squares(tokens_in, key_grad)
    square_sums = sum_over(square_sums, "mp")
    basis = lax.all_gather(basis_init, "mp", axis=0, tiled=True)
    sources = (
        depth * lax.axis_size("mp"), tokens_in, square_sums, norm_gain[None, :], grad, error
    )

    plan, turns, arrivals = stream_plan(replicas, depth // replicas)
    halves, here, there, place = [], [], [], 0
    for stream in plan:
        half = stream.width * replicas // 2
        side = bit_of("rep", stream.order[0])
        halves.append(half)
        here.append(place + side * half)
        there.append(place + (1 - side) * half)
        place += 2 * half
    far = merge(True, there, halves, *sources)
    got = [flip(part, "rep", 1 << stream.order[0]) for part, stream in zip(far, plan)]
    *own, own_kept = merge(False, here, halves, *sources, after=[basis])
    parts, after, done = list(own), [], [0] * len(plan)
    for s in arrivals:
        done[s] += 1
        came = got[s]
        if done[s] < steps:
            bit = plan[s].order[done[s]]
            parts[s], send = join(parts[s], came, bit_of("rep", bit), after, [p for k, p in enumerate(parts) if k != s])
            got[s] = flip(send, "rep", 1 << bit)
        else:
            (parts[s],) = join(parts[s], came, None, after, [])
        after = [came]

    packed = sum_everywhere(gram(parts, replicas, 32 * lax.axis_size("mp")))
    whole, right, gram_matrix, lefts = first_pass(plan, packed, basis, parts, replicas)
    second, (high, low) = second_pass(whole, right, gram_matrix)

    bit_sides = jnp.stack([bit_of("rep", bit) for bit in range(steps)]).astype(jnp.int32)
    for step in range(steps):
        bits, _, _ = bundles(plan, step)
        others = [flip(left, "rep", 1 << bit) for left, bit in zip(lefts, bits)]
        if step + 1 < steps:
            lefts = gather_step(plan, step, bit_sides, lefts, others, [high if step + 2 >= steps else second])

    error_out, far_near = error_rows(
        plan, replicas, here, own_kept, far, lefts, high, low, error.shape
    )
    error_out, weights_out, momentum_out = last_rows(
        plan, replicas, error_out, there + here, far_near, others, lefts, high, low, weights_in[0],
        momentum_in[0],
    )
    return (error_out[None], weights_out[None], momentum_out[None])


def solution(mesh):
    in_specs = (
        P("rep", "mp"),
        P("mp"),
        P("rep", None),
        P("rep", "mp", None),
        P("mp", None),
        P("mp", "rep", None),
        P("mp", "rep", None),
    )
    out_specs = (P("rep", "mp", None), P("mp", "rep", None), P("mp", "rep", None))
    return jax.shard_map(
        on_device, mesh=mesh, in_specs=in_specs, out_specs=out_specs, check_vma=False
    )
```
